128 devices in a mesh: arc: 64 (over y, z, x_lo, core), circ: 2 (over x_hi).
Axes of the slice: x: 4 (x_hi: 2, x_lo: 2; x = x_hi * 2 + x_lo), y: 4, z: 4, core: 2. Of those that a mesh axis runs over, the one named last changes fastest.
Arguments:
- displacement: float32 [3, 32768, 256], P(None, 'arc', 'circ'), may hold values from -1.2 to 1.2
- velocity: float32 [3, 32768, 256], P(None, 'arc', 'circ'), may hold values from -1.8 to 1.8
- node_mass: float32 [32768, 256], P('arc', 'circ'), may hold values from 0.5 to 2
- wall_stiff: float32 [32768, 256], P('arc', 'circ'), may hold values from 0.5 to 2
- pad_state: float32 [64, 16, 256], P('arc', None, 'circ'), may hold values from 0 to 0.3
- roller_lift: float32 [40], replicated, may hold values from 0.2 to 0.6
- contact_rows: int32 [4, 40, 16], replicated, may hold values from 0 to 32767, as said below
- roller_slot: int32 [40], replicated, may hold values from 0 to 63, as said below
Outputs:
- displacement_out: float32 [3, 32768, 256], P(None, 'arc', 'circ')
- velocity_out: float32 [3, 32768, 256], P(None, 'arc', 'circ')
- pad_out: float32 [64, 16, 256], P('arc', None, 'circ')
The draws below stay inside these ranges and needn't reach their ends.
Inputs may be any that keep to these rules, and one draw needn't show every extreme that they name: contact_rows[s, r] lie within 20 cycles of cycle r * 32767 // 39, clipped to the pipe; cycles may repeat. `roller_slot`: distinct pad slots; slot t lies on index t // 1 of arc.
All inputs are finite; a program needn't handle non-finite values.
Results may differ from the reference program's by a relative error of at most 0.000084.
Values sent between devices are 32-bit elements; how exact they have to be, the bound alone decides.
No kernel may reach another device: no remote copies, remote signals or barrier semaphores. Data moves between devices by JAX's collectives and lax.ppermute only.
A program may use at most 64 MiB of HBM per device.

```python
import math
import jax
import jax.numpy as jnp

CIRC = 256
NROLL = 40
CAP = 16
STEPS = 4
CYCLES = 32768
SLOTS = 64


def draw_contact_rows(key, part):
    roller_ids = jnp.arange(NROLL, dtype=jnp.int32)
    centres = roller_ids * (CYCLES - 1) // (NROLL - 1)
    slot_ids = jnp.arange(CAP, dtype=jnp.int32)
    step_ids = jnp.arange(STEPS, dtype=jnp.int32)
    jitter = jax.random.randint(key, (STEPS, NROLL, CAP), 0, 3, dtype=jnp.int32)
    cycle_list = centres[None, :, None] + 2 * slot_ids[None, None, :] - CAP + step_ids[:, None, None] + jitter
    return jnp.clip(cycle_list, 0, CYCLES - 1).astype(jnp.int32)


def draw_roller_slot(key, part):
    first_key = jax.random.fold_in(key, 11)
    second_key = jax.random.fold_in(key, 12)
    middle = jax.random.permutation(first_key, SLOTS - 2)[:NROLL - 2].astype(jnp.int32) + 1
    chosen = jnp.concatenate([jnp.array([0, SLOTS - 1], dtype=jnp.int32), middle])
    return chosen[jax.random.permutation(second_key, NROLL)].astype(jnp.int32)


def shard_levels(key, extent, pieces, low, top_value):
    factor_of, own = 1.0, jax.random.fold_in(key, 6)
    for position, parts in pieces:
        draws = jnp.exp(jax.random.uniform(jax.random.fold_in(own, position), (parts,), jnp.float32, low / len(pieces), top_value / len(pieces)))
        factor_of = factor_of * jnp.repeat(draws, extent[position] // parts).reshape([-1 if axis == position else 1 for axis in range(len(extent))])
    return factor_of


def centred(rng, dims, deviation, limit, shards=(), held_as=jnp.bfloat16):
    values = jax.random.normal(rng, dims, jnp.float32) * deviation
    if len(shards) > 0:
        values = shard_levels(rng, dims, shards, -0.22, 0.18) * values
    return jnp.clip(values, min=-limit, max=limit).astype(held_as)


def setup_inputs(seed: int = 0) -> dict:
    seeds = jax.random.split(jax.random.key(seed), 9)
    displacement = centred(seeds[0], (3, CYCLES, CIRC), 0.2, 1.2, ((1, 64), (2, 2)), jnp.float32)
    velocity = centred(seeds[1], (3, CYCLES, CIRC), 0.3, 1.8, ((1, 64), (2, 2)), jnp.float32)
    node_mass = jnp.clip(jnp.exp(math.log(2.0) - 1.3862944 * jax.random.uniform(seeds[2], (CYCLES, CIRC), jnp.float32) ** shard_levels(seeds[2], (CYCLES, CIRC), ((0, 64), (1, 2)), -0.2, 0.2)), 0.5, 2.0)
    wall_stiff = jnp.clip(jnp.exp(math.log(2.0) - 1.3862944 * jax.random.uniform(seeds[3], (CYCLES, CIRC), jnp.float32) ** shard_levels(seeds[3], (CYCLES, CIRC), ((0, 64), (1, 2)), -0.2, 0.2)), 0.5, 2.0)
    pad_state = jnp.clip(0.3 * jax.random.uniform(seeds[4], (SLOTS, CAP, CIRC), jnp.float32) ** shard_levels(seeds[4], (SLOTS, CAP, CIRC), ((0, 64), (2, 2)), -0.2, 0.2), 0.0, 0.3)
    roller_lift = jnp.clip(jax.random.uniform(seeds[5], (NROLL,), jnp.float32, 0.2, 0.6), 0.2, 0.6)
    contact_rows = draw_contact_rows(jax.random.fold_in(seeds[8], 71), 0)
    roller_slot = draw_roller_slot(jax.random.fold_in(seeds[8], 71), 0)
    return {"displacement": displacement, "velocity": velocity, "node_mass": node_mass, "wall_stiff": wall_stiff, "pad_state": pad_state, "roller_lift": roller_lift, "contact_rows": contact_rows, "roller_slot": roller_slot}


time_step = 0.1
gravity = 0.2
contact_stiff = 2.0
cradle_curve = 0.5
pad_rate = 0.2
pad_stiff = 1.0

def directions(first_col, count, circ_total):
    columns = (first_col + jnp.arange(count, dtype=jnp.int32)).astype(jnp.float32)
    phases = 2.0 * math.pi * (columns + 0.5) / circ_total
    step_angle = 2.0 * math.pi / circ_total
    chord_len = 2.0 * math.sin(step_angle / 2.0)
    length = math.sqrt(step_angle * step_angle + chord_len * chord_len)
    cos_phase = jnp.cos(phases)
    sin_phase = jnp.sin(phases)
    hoop_dir = (jnp.zeros_like(phases), cos_phase, sin_phase)
    diag_dir = (jnp.full_like(phases, step_angle / length), chord_len * cos_phase / length, chord_len * sin_phase / length)
    anti_dir = (jnp.full_like(phases, -step_angle / length), chord_len * cos_phase / length, chord_len * sin_phase / length)
    return (hoop_dir, diag_dir, anti_dir)

def spring_pull(centre, partner, spring_k, unit_dir):
    stretch = spring_k * (unit_dir[0] * (partner[0] - centre[0]) + unit_dir[1] * (partner[1] - centre[1]) + unit_dir[2] * (partner[2] - centre[2]))
    return jnp.stack([stretch * unit_dir[0], stretch * unit_dir[1], stretch * unit_dir[2]])

def internal_force(ext_shift, ext_k, first_col, circ_total):
    cycle_count = ext_shift.shape[1] - 2
    col_count = ext_shift.shape[2] - 2
    hoop_dir, diag_dir, anti_dir = directions(first_col, col_count + 2, circ_total)
    axial_dir = (1.0, 0.0, 0.0)
    centre = ext_shift[:, 1:cycle_count + 1, 1:col_count + 1]

    def neighbour(cycle_step, col_step):
        return ext_shift[:, 1 + cycle_step:cycle_count + 1 + cycle_step, 1 + col_step:col_count + 1 + col_step]

    def element_at(cycle_off, col_off):
        return ext_k[cycle_off:cycle_off + cycle_count, col_off:col_off + col_count]

    def pick(vector, col_off):
        return tuple((part_v[col_off:col_off + col_count] for part_v in vector))
    internal = spring_pull(centre, neighbour(1, 0), 0.5 * (element_at(1, 0) + element_at(1, 1)), axial_dir)
    internal = internal + spring_pull(centre, neighbour(-1, 0), 0.5 * (element_at(0, 0) + element_at(0, 1)), axial_dir)
    internal = internal + spring_pull(centre, neighbour(0, 1), 0.5 * (element_at(1, 1) + element_at(0, 1)), pick(hoop_dir, 1))
    internal = internal + spring_pull(centre, neighbour(0, -1), 0.5 * (element_at(1, 0) + element_at(0, 0)), pick(hoop_dir, 0))
    internal = internal + spring_pull(centre, neighbour(1, 1), element_at(1, 1), pick(diag_dir, 1))
    internal = internal + spring_pull(centre, neighbour(-1, -1), element_at(0, 0), pick(diag_dir, 0))
    internal = internal + spring_pull(centre, neighbour(1, -1), element_at(1, 0), pick(anti_dir, 0))
    internal = internal + spring_pull(centre, neighbour(-1, 1), element_at(0, 1), pick(anti_dir, 1))
    return internal

def roller_press(lift_up, shift_y, shift_z, pad_now, sin_angle, cos_angle):
    lateral = sin_angle + shift_y
    intrusion = lift_up + cradle_curve * lateral * lateral - (1.0 - cos_angle) - shift_z - pad_now
    contact_load = contact_stiff * jnp.maximum(intrusion, 0.0)
    normal_load = contact_load / jnp.sqrt(1.0 + 4.0 * cradle_curve * cradle_curve * lateral * lateral)
    return (-2.0 * cradle_curve * lateral * normal_load, normal_load, pad_now + pad_rate * (contact_load - pad_stiff * pad_now))

def wrap_pad(field_in):
    cycle_padded = jnp.pad(field_in, [(0, 0)] * (field_in.ndim - 2) + [(1, 1), (0, 0)])
    return jnp.concatenate([cycle_padded[..., -1:], cycle_padded, cycle_padded[..., :1]], axis=-1)

def reference(displacement, velocity, node_mass, wall_stiff, pad_state, roller_lift, contact_rows, roller_slot):
    cycle_ids = jnp.arange(CYCLES, dtype=jnp.int32)
    element_k = jnp.where((cycle_ids < CYCLES - 1)[:, None], wall_stiff, jnp.float32(0.0))
    ext_k = wrap_pad(element_k)
    angles = 2.0 * math.pi * jnp.arange(CIRC, dtype=jnp.int32).astype(jnp.float32) / CIRC
    sin_angle = jnp.sin(angles)
    cos_angle = jnp.cos(angles)
    pad_now = pad_state
    for step_index in range(STEPS):
        internal = internal_force(wrap_pad(displacement), ext_k, -1, CIRC)
        cycle_list = contact_rows[step_index]
        shift_y = displacement[1][cycle_list]
        shift_z = displacement[2][cycle_list]
        pad_roll = pad_now[roller_slot]
        force_y, force_z, pad_new = roller_press(roller_lift[:, None, None], shift_y, shift_z, pad_roll, sin_angle, cos_angle)
        pad_now = pad_now.at[roller_slot].set(pad_new)
        force_pairs = jnp.stack([force_y, force_z], axis=2).reshape(-1, 2, CIRC)
        contact_force = jnp.zeros((CYCLES, 2, CIRC), jnp.float32).at[cycle_list.reshape(-1)].add(force_pairs)
        contact_force = jnp.transpose(contact_force, (1, 0, 2))
        total_force = internal + jnp.stack([jnp.zeros_like(node_mass), contact_force[0], contact_force[1] - gravity * node_mass])
        velocity = velocity + time_step * total_force / node_mass
        displacement = displacement + time_step * velocity
    return (displacement, velocity, pad_now)
```

```python
import functools
import math

import jax
import jax.numpy as jnp
import numpy as np
from jax import lax
from jax.experimental import pallas as pl
from jax.experimental.pallas import tpu as pltpu
from jax.sharding import PartitionSpec as P

STEPS = 4
REACH = 20
TIME_STEP = 0.1
GRAVITY = 0.2
CONTACT_STIFF = 2.0
CRADLE_CURVE = 0.5
PAD_RATE = 0.2
PAD_STIFF = 1.0

LANES = 128
EDGE = 4
HALO = 48
WIN = 64
CHUNKS = 4
SIZES = (4, 4, 2, 2)


def arc_digits(index):
    return (index // 16, (index // 4) % 4, (index // 2) % 2, index % 2)


def arc_index(y, z, x, c):
    return (((y % 4) * 4 + z % 4) * 2 + x % 2) * 2 + c % 2


def pairs(shift):
    out = []
    for i in range(64):
        y, z, x, c = arc_digits(i)
        out.append((i, arc_index(y + shift[0], z + shift[1], x + shift[2], c + shift[3])))
    return out


def column_table(circ_total):
    step = 2.0 * math.pi / circ_total
    chord = 2.0 * math.sin(step / 2.0)
    length = math.sqrt(step * step + chord * chord)
    rows = []
    for half in range(2):
        cols = (half * LANES + np.arange(2 * LANES)) % circ_total
        phase = step * (cols + 0.5)
        before = step * (cols - 0.5)
        theta = step * cols
        parts = [
            chord / length * np.cos(phase),
            chord / length * np.sin(phase),
            chord / length * np.cos(before),
            chord / length * np.sin(before),
            np.sin(theta),
            np.cos(theta),
            np.zeros_like(theta),
            np.zeros_like(theta),
        ]
        rows.append(np.concatenate([p.reshape(2, LANES) for p in parts], axis=0))
    axial = step / length
    hoop_gain = 1.0 / (chord / length) ** 2
    return np.stack(rows).astype(np.float32), axial, hoop_gain


def prep_kernel(cycle_total, base_ref, disp, vel, mass, stiff, low, high, ext, pack):
    own = disp.shape[1]
    halo = low.shape[1]
    total = own + 2 * halo
    half = total // 2
    base = base_ref[0] - halo

    def put(row, count, raw):
        ids = base + row + lax.broadcasted_iota(jnp.int32, (count, LANES), 0)
        for a in range(3):
            ext[a, row : row + count, :] = raw(a)
        for a in range(3, 6):
            ext[a, row : row + count, :] = raw(a) * TIME_STEP
        m = raw(6)
        ext[6, row : row + count, :] = (TIME_STEP * TIME_STEP) / jnp.where(m > 0.0, m, 1.0)
        inside = (ids >= 0) & (ids < cycle_total - 1)
        ext[7, row : row + count, :] = jnp.where(inside, raw(7), 0.0)

    put(0, halo, lambda a: low[a])
    put(halo + own, halo, lambda a: high[a])
    for row in range(0, own, 64):
        span = slice(row, row + 64)

        def raw(a, span=span):
            if a < 3:
                return disp[a, span, :]
            if a < 6:
                return vel[a - 3, span, :]
            return mass[span, :] if a == 6 else stiff[span, :]

        put(halo + row, 64, raw)
    lane = lax.broadcasted_iota(jnp.int32, (8, LANES), 1) // (2 * EDGE)

    def body(b, carry):
        r = pl.multiple_of(b * 8, 8)
        packed = jnp.zeros((8, LANES), jnp.float32)
        for part in range(2):
            for a in range(8):
                value = ext[a, pl.ds(pl.multiple_of(r + part * half, 8), 8), :]
                moved = pltpu.roll(value, (8 * a + EDGE + 64 * part) % LANES, 1)
                packed = jnp.where(lane == a + 8 * part, moved, packed)
        pack[pl.ds(r, 8), :] = packed
        return carry

    lax.fori_loop(0, half // 8, body, 0)


def ring_left(tiles, last):
    a, b = (pltpu.roll(t, LANES - 1, 1) for t in tiles)
    return jnp.where(last, b, a), jnp.where(last, a, b)


def ring_right(tiles, first):
    a, b = (pltpu.roll(t, 1, 1) for t in tiles)
    return jnp.where(first, b, a), jnp.where(first, a, b)


def unpack_block(pack, row, half, a, keep):
    upper = row >= half
    at = pl.multiple_of(jnp.where(upper, row - half, row), 8)
    shift = jnp.where(upper, (2 * LANES - 8 * a - EDGE - 64) % LANES, (2 * LANES - 8 * a - EDGE) % LANES)
    return jnp.where(keep, pltpu.roll(pack[pl.ds(at, 8), :], shift, 1), 0.0)


def load_state(source, pack, first_row, rows, half, state, vels, coef):
    lane = lax.broadcasted_iota(jnp.int32, (8, LANES), 1)
    sub = lax.broadcasted_iota(jnp.int32, (8, LANES), 0)
    keep = (lane < EDGE) | (lane >= LANES - EDGE)
    first = lane == 0
    top = sub == 0

    def body(b, carry):
        r = pl.multiple_of(b * 8, 8)
        e = first_row + r
        span = pl.ds(r, 8)
        for a in range(3):
            state[0, a, 0, span, :] = source(a, r)
            state[0, a, 1, span, :] = unpack_block(pack, e, half, a, keep)
            vels[a, 0, span, :] = source(3 + a, r)
            vels[a, 1, span, :] = unpack_block(pack, e, half, 3 + a, keep)
        coef[0, 0, span, :] = source(6, r)
        coef[0, 1, span, :] = unpack_block(pack, e, half, 6, keep)
        k = (source(7, r), unpack_block(pack, e, half, 7, keep))
        kr = ring_right(k, first)
        new = []
        for t in range(2):
            down = pltpu.roll(k[t], 1, 0)
            coef[1, t, span, :] = k[t]
            coef[2, t, span, :] = 0.5 * (k[t] + kr[t])
            coef[3, t, span, :] = (0.5 * HOOP_GAIN) * (k[t] + jnp.where(top, carry[t], down))
            new.append(down)
        return tuple(new)

    zero = jnp.zeros((8, LANES), jnp.float32)
    lax.fori_loop(0, rows // 8, body, (zero, zero))
    for buf in range(2):
        for a in range(3):
            for t in range(2):
                state[buf, a, t, rows : rows + 8, :] = zero


TABLE, AXIAL, HOOP_GAIN = column_table(2 * LANES)


def advance(table, rows, step, state, vels, coef, push=None):
    now, later = step % 2, (step + 1) % 2
    lane = lax.broadcasted_iota(jnp.int32, (8, LANES), 1)
    top = lax.broadcasted_iota(jnp.int32, (8, LANES), 0) == 0
    first, last = lane == 0, lane == LANES - 1

    def const(i):
        return [jnp.broadcast_to(table[2 * i + t : 2 * i + t + 1, :], (8, LANES)) for t in range(2)]

    cj, sj, cb, sb = (const(i) for i in range(4))
    two = range(2)

    def body(b, carry):
        r = pl.multiple_of(b * 8, 8)
        span, below = pl.ds(r, 8), pl.ds(r + 1, 8)
        x, y, z = ([state[now, a, t, span, :] for t in two] for a in range(3))
        xn, yn, zn = ([state[now, a, t, below, :] for t in two] for a in range(3))
        p = [cj[t] * y[t] + sj[t] * z[t] for t in two]
        q = [cb[t] * y[t] + sb[t] * z[t] for t in two]
        ax = [AXIAL * x[t] for t in two]
        pn = [cj[t] * yn[t] + sj[t] * zn[t] for t in two]
        qn = [cb[t] * yn[t] + sb[t] * zn[t] for t in two]
        axn = [AXIAL * xn[t] for t in two]
        q_next = ring_left(q, last)
        anti_next = ring_left([q[t] - ax[t] for t in two], last)
        diag_next = ring_left([qn[t] + axn[t] for t in two], last)
        k = [coef[1, t, span, :] for t in two]
        t_d = [k[t] * (diag_next[t] - (p[t] + ax[t])) for t in two]
        t_a = [k[t] * (anti_next[t] - (pn[t] - axn[t])) for t in two]
        t_h = [coef[3, t, span, :] * (q_next[t] - p[t]) for t in two]
        fx = [coef[2, t, span, :] * (xn[t] - x[t]) for t in two]
        d_left = ring_right(t_d, first)
        a_left = ring_right(t_a, first)
        g_left = ring_right([t_a[t] + t_h[t] for t in two], first)
        new = []
        for t in two:
            up = t_d[t] + t_h[t]
            force = [
                fx[t] + AXIAL * (t_d[t] + a_left[t]),
                cj[t] * up - cb[t] * g_left[t],
                sj[t] * up - sb[t] * g_left[t],
            ]
            low = [
                fx[t] + AXIAL * (d_left[t] + t_a[t]),
                cb[t] * d_left[t] - cj[t] * t_a[t],
                sb[t] * d_left[t] - sj[t] * t_a[t],
            ]
            at = (x[t], y[t], z[t])
            inverse = coef[0, t, span, :]
            for a in range(3):
                moved = pltpu.roll(low[a], 1, 0)
                total = force[a] - jnp.where(top, carry[3 * t + a], moved)
                new.append(moved)
                if push is not None and a > 0:
                    total = total + push[a - 1, t, span, :]
                w = vels[a, t, span, :] + inverse * total
                if a == 2:
                    w = w - (GRAVITY * TIME_STEP * TIME_STEP)
                vels[a, t, span, :] = w
                state[later, a, t, span, :] = at[a] + w
        return tuple(new)

    zero = jnp.zeros((8, LANES), jnp.float32)
    lax.fori_loop(0, rows // 8, body, (zero,) * 6)


def window_kernel(
    half, where_ref, list_ref, lift_ref, table, ext, pack, pads, result, pad_out,
    raw, state, vels, coef, push, taken, given, held, sem,
):
    start = pl.multiple_of(where_ref[0], 8)
    copy = pltpu.make_async_copy(ext.at[:, pl.ds(start, WIN), :], raw, sem)
    copy.start()
    copy.wait()
    load_state(lambda a, r: raw[a, pl.ds(r, 8), :], pack, start, WIN, half, state, vels, coef)
    held[...] = pads[...]
    slots = pads.shape[1]
    lift = lift_ref[0]
    for step in range(STEPS):
        now = step % 2
        push[...] = jnp.zeros_like(push)
        for m in range(slots):
            g = list_ref[step, m]
            for a in range(2):
                for t in range(2):
                    taken[a, t, m : m + 1, :] = state[now, a + 1, t, pl.ds(g, 1), :]
        for t in range(2):
            sin_angle, cos_angle = table[8 + t : 9 + t, :], table[10 + t : 11 + t, :]
            lateral = sin_angle + taken[0, t]
            q = held[t]
            intrusion = lift + CRADLE_CURVE * lateral * lateral - (1.0 - cos_angle) - taken[1, t] - q
            load = CONTACT_STIFF * jnp.maximum(intrusion, 0.0)
            normal = load / jnp.sqrt(1.0 + 4.0 * CRADLE_CURVE * CRADLE_CURVE * lateral * lateral)
            given[0, t] = -2.0 * CRADLE_CURVE * lateral * normal
            given[1, t] = normal
            held[t] = q + PAD_RATE * (load - PAD_STIFF * q)
        for m in range(slots):
            g = list_ref[step, m]
            for a in range(2):
                for t in range(2):
                    push[a, t, pl.ds(g, 1), :] += given[a, t, m : m + 1, :]
        advance(table, WIN, step, state, vels, coef, push)
    for a in range(3):
        result[a] = state[STEPS % 2, a, 0, :WIN, :]
        result[3 + a] = vels[a, 0] * (1.0 / TIME_STEP)
    pad_out[0] = held[0]


def bulk_kernel(half, rows, where_ref, table, ext, pack, window, disp_out, vel_out, state, vels, coef):
    chunk = pl.program_id(0)
    count = rows - 16
    first_row = HALO - 8 + chunk * count

    def source(a, r):
        return ext[a, pl.ds(pl.multiple_of(first_row + r, 8), 8), :]

    load_state(source, pack, first_row, rows, half, state, vels, coef)
    for step in range(STEPS):
        advance(table, rows, step, state, vels, coef)
    start = where_ref[1]
    sub = lax.broadcasted_iota(jnp.int32, (8, LANES), 0)

    def body(b, carry):
        r = pl.multiple_of(b * 8, 8)
        inner = pl.ds(pl.multiple_of(r + 8, 8), 8)
        rel = first_row + 8 + r - start
        at = pl.ds(pl.multiple_of(jnp.clip(rel, 0, WIN - 8), 8), 8)
        ids = rel + sub
        use = (ids >= STEPS) & (ids < WIN - STEPS)
        for a in range(3):
            disp_out[a, pl.ds(r, 8), :] = jnp.where(use, window[a, at, :], state[STEPS % 2, a, 0, inner, :])
            vel_out[a, pl.ds(r, 8), :] = jnp.where(
                use, window[3 + a, at, :], vels[a, 0, inner, :] * (1.0 / TIME_STEP)
            )
        return carry

    lax.fori_loop(0, count // 8, body, 0)


def pick(held, index):
    count = held.shape[0]
    out = []
    for i in range(index.shape[0]):
        value = held[0]
        for n in range(1, count):
            value = jnp.where(index[i] == n, held[n], value)
        out.append(value)
    return jnp.stack(out)


def route(value, needs, me, both):
    my_y, my_x, my_c = me // 16, (me // 2) % 2, me % 2
    got = [value]
    for k in range(1, 4):
        got.append(lax.ppermute(value, "arc", pairs((k, 0, 0, 0))))
    held = jnp.stack(got)
    other = lax.ppermute(held, "arc", pairs((0, 0, 0, 1)))
    held = jnp.concatenate([held, other])
    need_y, need_z, need_x, need_c = arc_digits(needs)
    index = (need_c ^ my_c) * 4 + (my_y - need_y) % 4
    chosen = pick(held, index)
    parts = [chosen[0:2]]
    for k in range(1, 4):
        parts.append(lax.ppermute(chosen[2 * k : 2 * k + 2], "arc", pairs((0, k, 0, 0))))
    back = ((me // 4) % 4 - need_z[0:2]) % 4
    mine = []
    for xr in range(2):
        best = parts[0][xr]
        for k in range(1, 4):
            best = jnp.where(back[xr] == k, parts[k][xr], best)
        mine.append(best)
    same = need_x[0] == my_x
    across = pairs((0, 0, 1, 0))
    near = lax.ppermute(mine[1], "arc", across)
    result = jnp.where(same, mine[0], near)
    if not both:
        return result
    swap = [(0, 1), (1, 0)]
    double = [(2 * s + h, 2 * d + 1 - h) for s, d in across for h in range(2)]
    far = lax.ppermute(mine[0], "circ", swap)
    cross = lax.ppermute(mine[1], ("arc", "circ"), double)
    return jnp.stack([result, jnp.where(same, far, cross)])


def static_tables(arc_count, cycle_dev, roller_total):
    cycle_total = arc_count * cycle_dev
    centres = [r * (cycle_total - 1) // (roller_total - 1) for r in range(roller_total)]
    span = REACH + STEPS - 1
    near = np.full(arc_count, -1, np.int32)
    start = np.zeros(arc_count, np.int32)
    for d in range(arc_count):
        base = d * cycle_dev
        touching = [r for r, c in enumerate(centres) if base - span <= c < base + cycle_dev + span]
        assert len(touching) <= 1
        if touching:
            near[d] = touching[0]
            offset = centres[touching[0]] - base - REACH - STEPS - STEPS + 1 + HALO
            start[d] = offset // 8 * 8
            assert 0 <= start[d] <= cycle_dev + 2 * HALO - WIN
    home = np.array([c // cycle_dev for c in centres], np.int32)
    dests = np.zeros((arc_count, 8), np.int32)
    for d in range(arc_count):
        y, z, x, c = arc_digits(d)
        for k in range(4):
            for xr in range(2):
                dests[d, 2 * k + xr] = arc_index(y, z + k, x + xr, c)
    return near, start, home, dests


def local(displacement, velocity, node_mass, wall_stiff, pad_state, roller_lift, contact_rows, roller_slot):
    cycle_dev = displacement.shape[1]
    slots = pad_state.shape[1]
    roller_total = roller_lift.shape[0]
    arc_count = lax.axis_size("arc")
    cycle_total = cycle_dev * arc_count
    total = cycle_dev + 2 * HALO
    half = total // 2
    near, start, home, dests = static_tables(arc_count, cycle_dev, roller_total)
    me = lax.axis_index("arc")
    vmem = pl.BlockSpec(memory_space=pltpu.VMEM)
    smem = pl.BlockSpec(memory_space=pltpu.SMEM)
    params = pltpu.CompilerParams(vmem_limit_bytes=40 * 1024 * 1024)

    roller_ids = jnp.arange(roller_total, dtype=jnp.int32)
    dest_row = jnp.asarray(np.concatenate([dests, near[dests], near[:, None], start[:, None]], axis=1))[me]
    dest_ids, dest_rolls, roll, begin = dest_row[:8], dest_row[8:16], dest_row[16], dest_row[17]
    needs_in = jnp.sum(
        jnp.where(dest_rolls[:, None] == roller_ids[None, :], roller_slot[None, :], 0), axis=1
    )
    matches = roller_slot[None, :] == dest_ids[:, None]
    needs_out = jnp.sum(jnp.where(matches, jnp.asarray(home)[None, :], 0), axis=1)
    used = jnp.any(matches[0])

    def edge(at):
        return jnp.concatenate(
            [displacement[:, at], velocity[:, at], node_mass[None, at], wall_stiff[None, at]], axis=0
        )

    up = [(i, i + 1) for i in range(arc_count - 1)]
    low = lax.ppermute(edge(slice(cycle_dev - HALO, cycle_dev)), "arc", up)
    high = lax.ppermute(edge(slice(0, HALO)), "arc", [(b, a) for a, b in up])

    pads = route(pad_state[0], needs_in, me, True)

    base = jnp.reshape(me * cycle_dev, (1,)).astype(jnp.int32)

    ext, pack = pl.pallas_call(
        functools.partial(prep_kernel, cycle_total),
        out_shape=(
            jax.ShapeDtypeStruct((8, total, LANES), jnp.float32),
            jax.ShapeDtypeStruct((half, LANES), jnp.float32),
        ),
        in_specs=[smem] + [vmem] * 6,
        out_specs=(vmem, vmem),
        compiler_params=params,
        name="prep",
    )(base, displacement, velocity, node_mass, wall_stiff, low, high)
    pack = lax.ppermute(pack, "circ", [(0, 1), (1, 0)])

    safe_roll = jnp.maximum(roll, 0)
    cycles = lax.dynamic_slice(contact_rows, (0, safe_roll, 0), (STEPS, 1, slots))[:, 0]
    rows_in = jnp.clip(cycles - (me * cycle_dev - HALO + begin), 0, WIN - 1)
    lift = jnp.where(roll >= 0, lax.dynamic_slice(roller_lift, (safe_roll,), (1,)), -1e9)
    where = jnp.stack([begin, jnp.where(roll >= 0, begin, -4 * WIN)])
    table = jnp.asarray(TABLE)[lax.axis_index("circ")]

    def scratch(rows):
        return [
            pltpu.VMEM((2, 3, 2, rows + 8, LANES), jnp.float32),
            pltpu.VMEM((3, 2, rows, LANES), jnp.float32),
            pltpu.VMEM((4, 2, rows, LANES), jnp.float32),
        ]

    window, pad_new = pl.pallas_call(
        functools.partial(window_kernel, half),
        out_shape=(
            jax.ShapeDtypeStruct((6, WIN, LANES), jnp.float32),
            jax.ShapeDtypeStruct((1, slots, LANES), jnp.float32),
        ),
        in_specs=[smem, smem, smem, vmem, pl.BlockSpec(memory_space=pl.ANY), vmem, vmem],
        out_specs=(vmem, vmem),
        scratch_shapes=[pltpu.VMEM((8, WIN, LANES), jnp.float32)]
        + scratch(WIN)
        + [
            pltpu.VMEM((2, 2, WIN, LANES), jnp.float32),
            pltpu.VMEM((2, 2, slots, LANES), jnp.float32),
            pltpu.VMEM((2, 2, slots, LANES), jnp.float32),
            pltpu.VMEM((2, slots, LANES), jnp.float32),
            pltpu.SemaphoreType.DMA,
        ],
        compiler_params=params,
        name="window",
    )(where, rows_in, lift, table, ext, pack, pads)

    rows = cycle_dev // CHUNKS + 16
    disp_out, vel_out = pl.pallas_call(
        functools.partial(bulk_kernel, half, rows),
        grid=(CHUNKS,),
        out_shape=(
            jax.ShapeDtypeStruct(displacement.shape, jnp.float32),
            jax.ShapeDtypeStruct(displacement.shape, jnp.float32),
        ),
        in_specs=[smem, vmem, vmem, vmem, vmem],
        out_specs=(
            pl.BlockSpec((3, rows - 16, LANES), lambda i: (0, i, 0)),
            pl.BlockSpec((3, rows - 16, LANES), lambda i: (0, i, 0)),
        ),
        scratch_shapes=scratch(rows),
        compiler_params=params,
        cost_estimate=pl.CostEstimate(flops=30_000_000, bytes_accessed=8_000_000, transcendentals=0),
        name="bulk",
    )(where, table, ext, pack, window)

    returned = route(pad_new[0], needs_out, me, False)
    pad_result = jnp.where(used, returned, pad_state[0])[None]
    return disp_out, vel_out, pad_result


def solution(mesh):
    placed = (
        P(None, "arc", "circ"),
        P(None, "arc", "circ"),
        P("arc", "circ"),
        P("arc", "circ"),
        P("arc", None, "circ"),
        P(),
        P(),
        P(),
    )
    return jax.shard_map(
        local,
        mesh=mesh,
        in_specs=placed,
        out_specs=(P(None, "arc", "circ"), P(None, "arc", "circ"), P("arc", None, "circ")),
        check_vma=False,
    )
```

```python
import functools
import math

import jax
import jax.numpy as jnp
import numpy as np
from jax import lax
from jax.experimental import pallas as pl
from jax.experimental.pallas import tpu as pltpu
from jax.sharding import PartitionSpec as P

STEPS = 4
REACH = 20
TIME_STEP = 0.1
GRAVITY = 0.2
CONTACT_STIFF = 2.0
CRADLE_CURVE = 0.5
PAD_RATE = 0.2
PAD_STIFF = 1.0

LANES = 128
EDGE = 4
HALO = 48
WIN = 64
CHUNKS = 4
GROUP = 6
LOAD_GROUP = 2
LIMIT = 40 * 1024 * 1024
SIZES = (4, 4, 2, 2)


def arc_digits(index):
    return (index // 16, (index // 4) % 4, (index // 2) % 2, index % 2)


def arc_index(y, z, x, c):
    return (((y % 4) * 4 + z % 4) * 2 + x % 2) * 2 + c % 2


def pairs(shift):
    out = []
    for i in range(64):
        y, z, x, c = arc_digits(i)
        out.append((i, arc_index(y + shift[0], z + shift[1], x + shift[2], c + shift[3])))
    return out


def column_table(circ_total):
    step = 2.0 * math.pi / circ_total
    chord = 2.0 * math.sin(step / 2.0)
    length = math.sqrt(step * step + chord * chord)
    rows = []
    for half in range(2):
        cols = (half * LANES + np.arange(2 * LANES)) % circ_total
        phase = step * (cols + 0.5)
        before = step * (cols - 0.5)
        theta = step * cols
        parts = [
            chord / length * np.cos(phase),
            chord / length * np.sin(phase),
            chord / length * np.cos(before),
            chord / length * np.sin(before),
            np.sin(theta),
            np.cos(theta),
            np.zeros_like(theta),
            np.zeros_like(theta),
        ]
        rows.append(np.concatenate([p.reshape(2, LANES) for p in parts], axis=0))
    axial = step / length
    hoop_gain = 1.0 / (chord / length) ** 2
    return np.stack(rows).astype(np.float32), axial, hoop_gain


def start_kernel(
    halo, slot_ref, lift_ref, rows_ref, near_ref, begin_ref, home_ref, disp, vel, mass, stiff,
    low_edge, high_edge, plan, where_ref, list_ref, lift_out, source, sems,
):
    own = disp.shape[1]
    copies = []
    for n, (edge, at) in enumerate(((low_edge, 0), (high_edge, own - halo))):
        span = pl.ds(at, halo)
        copies += [
            pltpu.make_async_copy(disp.at[:, span, :], edge.at[0:3], sems.at[4 * n]),
            pltpu.make_async_copy(vel.at[:, span, :], edge.at[3:6], sems.at[4 * n + 1]),
            pltpu.make_async_copy(mass.at[span, :], edge.at[6], sems.at[4 * n + 2]),
            pltpu.make_async_copy(stiff.at[span, :], edge.at[7], sems.at[4 * n + 3]),
        ]
    for copy in copies:
        copy.start()
    me = lax.axis_index("arc")
    y, z, x, c = arc_digits(me)
    rollers = slot_ref.shape[0]
    roll = near_ref[me]
    begin = begin_ref[me]
    valid = roll >= 0
    safe = jnp.maximum(roll, 0)
    where_ref[0] = begin
    where_ref[1] = jnp.where(valid, begin, -4 * WIN)
    lift_out[0] = jnp.where(valid, lift_ref[safe], -1e9)
    for step in range(STEPS):
        for m in range(list_ref.shape[1]):
            g = rows_ref[step, safe, m] - (me * own - halo + begin)
            list_ref[step, m] = jnp.clip(g, 0, WIN - 1)

    def clear(i, carry):
        source[i] = -1
        return carry

    def note(r, carry):
        source[slot_ref[r]] = home_ref[r]
        return carry

    lax.fori_loop(0, source.shape[0], clear, 0)
    lax.fori_loop(0, rollers, note, 0)

    def line(value):
        return jnp.full((1, LANES), value, jnp.int32)

    for way in range(2):
        at = 16 * way
        for k in range(4):
            for xr in range(2):
                dest = arc_index(y, z + k, x + xr, c)
                if way == 0:
                    need = slot_ref[jnp.maximum(near_ref[dest], 0)]
                else:
                    need = jnp.maximum(source[dest], 0)
                ny, nz, nx, nc = arc_digits(need)
                plan[at + 2 * k + xr : at + 2 * k + xr + 1, :] = line((nc ^ c) * 4 + (y - ny + 4) % 4)
                if k == 0:
                    plan[at + 8 + xr : at + 9 + xr, :] = line((z - nz + 4) % 4)
                if k == 0 and xr == 0:
                    plan[at + 10 : at + 11, :] = line((nx == x).astype(jnp.int32))
        plan[at + 11 : at + 12, :] = line((source[me] >= 0).astype(jnp.int32))
        plan[at + 12 : at + 16, :] = jnp.zeros((4, LANES), jnp.int32)
    for copy in copies:
        copy.wait()


def prep_kernel(disp, vel, mass, stiff, low, high, ext, pack, sems):
    own = disp.shape[1]
    halo = low.shape[1]
    half = (own + 2 * halo) // 2
    span = pl.ds(halo, own)
    copies = [
        pltpu.make_async_copy(disp, ext.at[0:3, span, :], sems.at[0]),
        pltpu.make_async_copy(vel, ext.at[3:6, span, :], sems.at[1]),
        pltpu.make_async_copy(mass, ext.at[6, span, :], sems.at[2]),
        pltpu.make_async_copy(stiff, ext.at[7, span, :], sems.at[3]),
        pltpu.make_async_copy(low, ext.at[:, 0:halo, :], sems.at[4]),
        pltpu.make_async_copy(high, ext.at[:, halo + own : 2 * halo + own, :], sems.at[5]),
    ]
    for copy in copies:
        copy.start()
    for copy in copies:
        copy.wait()
    lane = lax.broadcasted_iota(jnp.int32, (8, LANES), 1) // (2 * EDGE)

    def body(b, carry):
        for u in range(2):
            r = pl.multiple_of(b * 16, 8) + 8 * u
            packed = jnp.zeros((8, LANES), jnp.float32)
            for part in range(2):
                for a in range(8):
                    value = ext[a, pl.ds(r + part * half, 8), :]
                    moved = pltpu.roll(value, (8 * a + EDGE + 64 * part) % LANES, 1)
                    packed = jnp.where(lane == a + 8 * part, moved, packed)
            pack[pl.ds(r, 8), :] = packed
        return carry

    lax.fori_loop(0, half // 16, body, 0)


def ring_left(tiles, last):
    a, b = (pltpu.roll(t, LANES - 1, 1) for t in tiles)
    return jnp.where(last, b, a), jnp.where(last, a, b)


def ring_right(tiles, first):
    a, b = (pltpu.roll(t, 1, 1) for t in tiles)
    return jnp.where(first, b, a), jnp.where(first, a, b)


def unpack_block(pack, row, half, a, keep):
    upper = row >= half
    at = pl.multiple_of(jnp.where(upper, row - half, row), 8)
    shift = jnp.where(upper, (2 * LANES - 8 * a - EDGE - 64) % LANES, (2 * LANES - 8 * a - EDGE) % LANES)
    return jnp.where(keep, pltpu.roll(pack[pl.ds(at, 8), :], shift, 1), 0.0)


def load_state(source, pack, first_row, base, cycle_total, rows, half, state, vels, coef):
    lane = lax.broadcasted_iota(jnp.int32, (8, LANES), 1)
    sub = lax.broadcasted_iota(jnp.int32, (8, LANES), 0)
    keep = (lane < EDGE) | (lane >= LANES - EDGE)
    first = lane == 0
    top = sub == 0

    def body(b, carry):
        r = pl.multiple_of(b * 8, 8)
        e = first_row + r
        span = pl.ds(r, 8)
        for a in range(3):
            state[0, a, 0, span, :] = source(a, r)
            state[0, a, 1, span, :] = unpack_block(pack, e, half, a, keep)
            vels[a, 0, span, :] = TIME_STEP * source(3 + a, r)
            vels[a, 1, span, :] = TIME_STEP * unpack_block(pack, e, half, 3 + a, keep)
        for t, m in enumerate((source(6, r), unpack_block(pack, e, half, 6, keep))):
            coef[0, t, span, :] = (TIME_STEP * TIME_STEP) / jnp.where(m > 0.0, m, 1.0)
        ids = base + e + sub
        inside = (ids >= 0) & (ids < cycle_total - 1)
        k = [
            jnp.where(inside, v, 0.0)
            for v in (source(7, r), unpack_block(pack, e, half, 7, keep))
        ]
        kr = ring_right(k, first)
        new = []
        for t in range(2):
            down = pltpu.roll(k[t], 1, 0)
            coef[1, t, span, :] = k[t]
            coef[2, t, span, :] = 0.5 * (k[t] + kr[t])
            coef[3, t, span, :] = (0.5 * HOOP_GAIN) * (k[t] + jnp.where(top, carry[t], down))
            new.append(down)
        return tuple(new)

    zero = jnp.zeros((8, LANES), jnp.float32)
    group = LOAD_GROUP

    def several(b, carry):
        for u in range(group):
            carry = body(b * group + u, carry)
        return carry

    lax.fori_loop(0, rows // (8 * group), several, (zero, zero))
    for buf in range(2):
        for a in range(3):
            for t in range(2):
                state[buf, a, t, rows : rows + 8, :] = zero


TABLE, AXIAL, HOOP_GAIN = column_table(2 * LANES)


def advance(table, rows, step, state, vels, coef, group, push=None):
    now, later = step % 2, (step + 1) % 2
    lane = lax.broadcasted_iota(jnp.int32, (8, LANES), 1)
    top = lax.broadcasted_iota(jnp.int32, (8, LANES), 0) == 0
    first, last = lane == 0, lane == LANES - 1

    def const(i):
        return [jnp.broadcast_to(table[2 * i + t : 2 * i + t + 1, :], (8, LANES)) for t in range(2)]

    cj, sj, cb, sb = (const(i) for i in range(4))
    two = range(2)

    def block(r, carry):
        span, below = pl.ds(r, 8), pl.ds(r + 1, 8)
        x, y, z = ([state[now, a, t, span, :] for t in two] for a in range(3))
        xn, yn, zn = ([state[now, a, t, below, :] for t in two] for a in range(3))
        p = [cj[t] * y[t] + sj[t] * z[t] for t in two]
        q = [cb[t] * y[t] + sb[t] * z[t] for t in two]
        ax = [AXIAL * x[t] for t in two]
        pn = [cj[t] * yn[t] + sj[t] * zn[t] for t in two]
        qn = [cb[t] * yn[t] + sb[t] * zn[t] for t in two]
        axn = [AXIAL * xn[t] for t in two]
        q_next = ring_left(q, last)
        anti_next = ring_left([q[t] - ax[t] for t in two], last)
        diag_next = ring_left([qn[t] + axn[t] for t in two], last)
        k = [coef[1, t, span, :] for t in two]
        t_d = [k[t] * (diag_next[t] - (p[t] + ax[t])) for t in two]
        t_a = [k[t] * (anti_next[t] - (pn[t] - axn[t])) for t in two]
        t_h = [coef[3, t, span, :] * (q_next[t] - p[t]) for t in two]
        fx = [coef[2, t, span, :] * (xn[t] - x[t]) for t in two]
        d_left = ring_right(t_d, first)
        a_left = ring_right(t_a, first)
        g_left = ring_right([t_a[t] + t_h[t] for t in two], first)
        new = []
        for t in two:
            up = t_d[t] + t_h[t]
            force = [
                fx[t] + AXIAL * (t_d[t] + a_left[t]),
                cj[t] * up - cb[t] * g_left[t],
                sj[t] * up - sb[t] * g_left[t],
            ]
            low = [
                fx[t] + AXIAL * (d_left[t] + t_a[t]),
                cb[t] * d_left[t] - cj[t] * t_a[t],
                sb[t] * d_left[t] - sj[t] * t_a[t],
            ]
            at = (x[t], y[t], z[t])
            inverse = coef[0, t, span, :]
            for a in range(3):
                moved = pltpu.roll(low[a], 1, 0)
                total = force[a] - jnp.where(top, carry[3 * t + a], moved)
                new.append(moved)
                if push is not None and a > 0:
                    total = total + push[a - 1, t, span, :]
                w = vels[a, t, span, :] + inverse * total
                if a == 2:
                    w = w - (GRAVITY * TIME_STEP * TIME_STEP)
                vels[a, t, span, :] = w
                state[later, a, t, span, :] = at[a] + w
        return tuple(new)

    def body(b, carry):
        for u in range(group):
            carry = block(pl.multiple_of(b * (8 * group), 8) + 8 * u, carry)
        return carry

    zero = jnp.zeros((8, LANES), jnp.float32)
    carry = (zero,) * 6
    if group * 8 == rows:
        for u in range(group):
            carry = block(8 * u, carry)
    else:
        lax.fori_loop(0, rows // (8 * group), body, carry)


def window_kernel(
    half, base, cycle_total, where_ref, list_ref, lift_ref, table, plan, ext, pack, mine, near, far, cross,
    result, pad_out, raw, state, vels, coef, push, taken, given, held, sem,
):
    start = pl.multiple_of(where_ref[0], 8)
    copy = pltpu.make_async_copy(ext.at[:, pl.ds(start, WIN), :], raw, sem)
    copy.start()
    copy.wait()
    first_id = base(lax.axis_index("arc"))
    load_state(
        lambda a, r: raw[a, pl.ds(r, 8), :], pack, start, first_id, cycle_total, WIN, half, state, vels, coef
    )
    same = plan[10:11, :] > 0
    held[0] = jnp.where(same, mine[0], near[...])
    held[1] = jnp.where(same, far[...], cross[...])
    slots = near.shape[0]
    lift = lift_ref[0]
    for step in range(STEPS):
        now = step % 2
        push[...] = jnp.zeros_like(push)
        for m in range(slots):
            g = list_ref[step, m]
            for a in range(2):
                for t in range(2):
                    taken[a, t, m : m + 1, :] = state[now, a + 1, t, pl.ds(g, 1), :]
        for t in range(2):
            sin_angle, cos_angle = table[8 + t : 9 + t, :], table[10 + t : 11 + t, :]
            lateral = sin_angle + taken[0, t]
            q = held[t]
            intrusion = lift + CRADLE_CURVE * lateral * lateral - (1.0 - cos_angle) - taken[1, t] - q
            load = CONTACT_STIFF * jnp.maximum(intrusion, 0.0)
            normal = load / jnp.sqrt(1.0 + 4.0 * CRADLE_CURVE * CRADLE_CURVE * lateral * lateral)
            given[0, t] = -2.0 * CRADLE_CURVE * lateral * normal
            given[1, t] = normal
            held[t] = q + PAD_RATE * (load - PAD_STIFF * q)
        for m in range(slots):
            g = list_ref[step, m]
            for a in range(2):
                for t in range(2):
                    push[a, t, pl.ds(g, 1), :] += given[a, t, m : m + 1, :]
        advance(table, WIN, step, state, vels, coef, WIN // 8, push)
    for a in range(3):
        result[a] = state[STEPS % 2, a, 0, :WIN, :]
        result[3 + a] = vels[a, 0] * (1.0 / TIME_STEP)
    pad_out[...] = held[0]


def bulk_kernel(half, base, cycle_total, rows, chunk, where_ref, table, ext, pack, window, *rest):
    disp_out, vel_out, state, vels, coef, result, sems = rest[-7:]
    count = rows - 16
    first_row = HALO - 8 + chunk * count

    def source(a, r):
        return ext[a, pl.ds(pl.multiple_of(first_row + r, 8), 8), :]

    first_id = base(lax.axis_index("arc"))
    load_state(source, pack, first_row, first_id, cycle_total, rows, half, state, vels, coef)
    for step in range(STEPS):
        advance(table, rows, step, state, vels, coef, GROUP)
    start = where_ref[1]
    sub = lax.broadcasted_iota(jnp.int32, (8, LANES), 0)

    def body(b, carry):
        r = pl.multiple_of(b * 8, 8)
        inner = pl.ds(pl.multiple_of(r + 8, 8), 8)
        rel = first_row + 8 + r - start
        at = pl.ds(pl.multiple_of(jnp.clip(rel, 0, WIN - 8), 8), 8)
        ids = rel + sub
        use = (ids >= STEPS) & (ids < WIN - STEPS)
        for a in range(3):
            result[a, pl.ds(r, 8), :] = jnp.where(use, window[a, at, :], state[STEPS % 2, a, 0, inner, :])
            result[3 + a, pl.ds(r, 8), :] = jnp.where(
                use, window[3 + a, at, :], vels[a, 0, inner, :] * (1.0 / TIME_STEP)
            )
        return carry

    lax.fori_loop(0, count // 8, body, 0)
    span = pl.ds(chunk * count, count)
    copies = [
        pltpu.make_async_copy(result.at[0:3], disp_out.at[:, span, :], sems.at[0]),
        pltpu.make_async_copy(result.at[3:6], vel_out.at[:, span, :], sems.at[1]),
    ]
    for copy in copies:
        copy.start()
    for copy in copies:
        copy.wait()


def pick_kernel(way, plan, held, other, *outs):
    parts = [ref[n] for ref in (held, other) for n in range(4)]
    for k in range(4):
        for xr in range(2):
            at = 16 * way + 2 * k + xr
            index = plan[at : at + 1, :]
            value = parts[0]
            for n in range(1, 8):
                value = jnp.where(index == n, parts[n], value)
            outs[k][xr] = value


def join_kernel(way, plan, *refs):
    parts, out = refs[:4], refs[4]
    for xr in range(2):
        at = 16 * way + 8 + xr
        back = plan[at : at + 1, :]
        value = parts[0][xr]
        for k in range(1, 4):
            value = jnp.where(back == k, parts[k][xr], value)
        out[xr] = value


def last_kernel(plan, mine, near, before, out):
    used = plan[27:28, :] > 0
    same = plan[26:27, :] > 0
    out[0] = jnp.where(used, jnp.where(same, mine[0], near[...]), before[0])


def route(value, plan, way):
    shape = value.shape
    vmem = pl.BlockSpec(memory_space=pltpu.VMEM)
    params = pltpu.CompilerParams(vmem_limit_bytes=LIMIT)
    got = [value]
    for k in range(1, 4):
        got.append(lax.ppermute(value, "arc", pairs((k, 0, 0, 0))))
    held = jnp.stack(got)
    other = lax.ppermute(held, "arc", pairs((0, 0, 0, 1)))
    two = jax.ShapeDtypeStruct((2,) + shape, jnp.float32)
    parts = pl.pallas_call(
        functools.partial(pick_kernel, way),
        out_shape=(two,) * 4,
        in_specs=[vmem] * 3,
        out_specs=(vmem,) * 4,
        compiler_params=params,
        name="pick",
    )(plan, held, other)
    parts = [parts[0]] + [lax.ppermute(parts[k], "arc", pairs((0, k, 0, 0))) for k in range(1, 4)]
    return pl.pallas_call(
        functools.partial(join_kernel, way),
        out_shape=two,
        in_specs=[vmem] * 5,
        out_specs=vmem,
        compiler_params=params,
        name="join",
    )(plan, *parts)


def static_tables(arc_count, cycle_dev, roller_total):
    cycle_total = arc_count * cycle_dev
    centres = [r * (cycle_total - 1) // (roller_total - 1) for r in range(roller_total)]
    span = REACH + STEPS - 1
    near = np.full(arc_count, -1, np.int32)
    start = np.zeros(arc_count, np.int32)
    for d in range(arc_count):
        base = d * cycle_dev
        touching = [r for r, c in enumerate(centres) if base - span <= c < base + cycle_dev + span]
        assert len(touching) <= 1
        if touching:
            near[d] = touching[0]
            offset = centres[touching[0]] - base - REACH - STEPS - STEPS + 1 + HALO
            start[d] = offset // 8 * 8
            assert 0 <= start[d] <= cycle_dev + 2 * HALO - WIN
    home = np.array([c // cycle_dev for c in centres], np.int32)
    return near, start, home


def local(displacement, velocity, node_mass, wall_stiff, pad_state, roller_lift, contact_rows, roller_slot):
    cycle_dev = displacement.shape[1]
    slots = pad_state.shape[1]
    roller_total = roller_lift.shape[0]
    arc_count = lax.axis_size("arc")
    cycle_total = cycle_dev * arc_count
    total = cycle_dev + 2 * HALO
    half = total // 2
    near, begin, home = static_tables(arc_count, cycle_dev, roller_total)
    vmem = pl.BlockSpec(memory_space=pltpu.VMEM)
    smem = pl.BlockSpec(memory_space=pltpu.SMEM)
    anywhere = pl.BlockSpec(memory_space=pl.ANY)
    params = pltpu.CompilerParams(vmem_limit_bytes=LIMIT)

    def real(*shape):
        return jax.ShapeDtypeStruct(shape, jnp.float32)

    def whole(*shape):
        return jax.ShapeDtypeStruct(shape, jnp.int32)

    fields = (displacement, velocity, node_mass, wall_stiff)
    low_edge, high_edge, plan, where, rows_in, lift = pl.pallas_call(
        functools.partial(start_kernel, HALO),
        out_shape=(
            real(8, HALO, LANES), real(8, HALO, LANES), whole(32, LANES), whole(2), whole(STEPS, slots), real(1),
        ),
        in_specs=[smem] * 6 + [anywhere] * 4,
        out_specs=(vmem, vmem, vmem, smem, smem, smem),
        scratch_shapes=[pltpu.SMEM((arc_count,), jnp.int32), pltpu.SemaphoreType.DMA((8,))],
        compiler_params=params,
        name="start",
    )(roller_slot, roller_lift, contact_rows, jnp.asarray(near), jnp.asarray(begin), jnp.asarray(home), *fields)

    up = [(i, i + 1) for i in range(arc_count - 1)]
    low = lax.ppermute(high_edge, "arc", up)
    high = lax.ppermute(low_edge, "arc", [(b, a) for a, b in up])

    mine = route(pad_state[0], plan, 0)
    across = pairs((0, 0, 1, 0))
    swap = [(0, 1), (1, 0)]
    double = [(2 * s + h, 2 * d + 1 - h) for s, d in across for h in range(2)]
    near_pad = lax.ppermute(mine[1], "arc", across)
    far_pad = lax.ppermute(mine[0], "circ", swap)
    cross_pad = lax.ppermute(mine[1], ("arc", "circ"), double)

    ext, pack = pl.pallas_call(
        prep_kernel,
        out_shape=(real(8, total, LANES), real(half, LANES)),
        in_specs=[anywhere] * 6,
        out_specs=(vmem, vmem),
        scratch_shapes=[pltpu.SemaphoreType.DMA((6,))],
        compiler_params=params,
        name="prep",
    )(*fields, low, high)
    pack = lax.ppermute(pack, "circ", swap)
    table = jnp.asarray(TABLE)[lax.axis_index("circ")]

    def scratch(rows):
        return [
            pltpu.VMEM((2, 3, 2, rows + 8, LANES), jnp.float32),
            pltpu.VMEM((3, 2, rows, LANES), jnp.float32),
            pltpu.VMEM((4, 2, rows, LANES), jnp.float32),
        ]

    def base(me):
        return me * cycle_dev - HALO

    window, pad_new = pl.pallas_call(
        functools.partial(window_kernel, half, base, cycle_total),
        out_shape=(real(6, WIN, LANES), real(slots, LANES)),
        in_specs=[smem] * 3 + [vmem, vmem, anywhere] + [vmem] * 5,
        out_specs=(vmem, vmem),
        scratch_shapes=[pltpu.VMEM((8, WIN, LANES), jnp.float32)]
        + scratch(WIN)
        + [
            pltpu.VMEM((2, 2, WIN, LANES), jnp.float32),
            pltpu.VMEM((2, 2, slots, LANES), jnp.float32),
            pltpu.VMEM((2, 2, slots, LANES), jnp.float32),
            pltpu.VMEM((2, slots, LANES), jnp.float32),
            pltpu.SemaphoreType.DMA,
        ],
        compiler_params=params,
        name="window",
    )(where, rows_in, lift, table, plan, ext, pack, mine, near_pad, far_pad, cross_pad)

    rows = cycle_dev // CHUNKS + 16
    outs = ()
    for chunk in range(CHUNKS):
        outs = pl.pallas_call(
            functools.partial(bulk_kernel, half, base, cycle_total, rows, chunk),
            out_shape=(real(3, cycle_dev, LANES),) * 2,
            in_specs=[smem] + [vmem] * 4 + [anywhere] * len(outs),
            out_specs=(anywhere, anywhere),
            input_output_aliases={5: 0, 6: 1} if outs else {},
            scratch_shapes=scratch(rows)
            + [pltpu.VMEM((6, rows - 16, LANES), jnp.float32), pltpu.SemaphoreType.DMA((2,))],
            compiler_params=params,
            cost_estimate=pl.CostEstimate(flops=0, bytes_accessed=48_000_000 // CHUNKS, transcendentals=0),
            name="bulk",
        )(where, table, ext, pack, window, *outs)

    back = route(pad_new, plan, 1)
    pad_result = pl.pallas_call(
        last_kernel,
        out_shape=real(1, slots, LANES),
        in_specs=[vmem] * 4,
        out_specs=vmem,
        compiler_params=params,
        name="last",
    )(plan, back, lax.ppermute(back[1], "arc", across), pad_state)
    return outs[0], outs[1], pad_result


def solution(mesh):
    placed = (
        P(None, "arc", "circ"),
        P(None, "arc", "circ"),
        P("arc", "circ"),
        P("arc", "circ"),
        P("arc", None, "circ"),
        P(),
        P(),
        P(),
    )
    return jax.shard_map(
        local,
        mesh=mesh,
        in_specs=placed,
        out_specs=(P(None, "arc", "circ"), P(None, "arc", "circ"), P("arc", None, "circ")),
        check_vma=False,
    )
```

```python
import functools
import math

import jax
import jax.numpy as jnp
import numpy as np
from jax import lax
from jax.experimental import pallas as pl
from jax.experimental.pallas import tpu as pltpu
from jax.sharding import PartitionSpec as P

STEPS = 4
REACH = 20
TIME_STEP = 0.1
GRAVITY = 0.2
CONTACT_STIFF = 2.0
CRADLE_CURVE = 0.5
PAD_RATE = 0.2
PAD_STIFF = 1.0

LANES = 128
EDGE = 4
HALO = 48
WIN = 64
CHUNKS = 4
GROUP = 11
PARTS = 3
LOAD_GROUP = 4
LIMIT = 40 * 1024 * 1024
MOST = 60 * 1024 * 1024


def arc_digits(index):
    return (index >> 4, (index >> 2) & 3, (index >> 1) & 1, index & 1)


def arc_index(y, z, x, c):
    return (y << 4) + (z << 2) + (x << 1) + c


def flips(y=0, z=0, x=0, c=0):
    out = []
    for i in range(64):
        iy, iz, ix, ic = arc_digits(i)
        out.append((i, arc_index(iy ^ y, iz ^ z, ix ^ x, ic ^ c)))
    return out


def column_table(circ_total):
    step = 2.0 * math.pi / circ_total
    chord = 2.0 * math.sin(step / 2.0)
    length = math.sqrt(step * step + chord * chord)
    rows = []
    for half in range(2):
        cols = (half * LANES + np.arange(2 * LANES)) % circ_total
        phase = step * (cols + 0.5)
        before = step * (cols - 0.5)
        theta = step * cols
        parts = [
            chord / length * np.cos(phase),
            chord / length * np.sin(phase),
            chord / length * np.cos(before),
            chord / length * np.sin(before),
            np.sin(theta),
            np.cos(theta),
            np.zeros_like(theta),
            np.zeros_like(theta),
        ]
        rows.append(np.concatenate([p.reshape(2, LANES) for p in parts], axis=0))
    axial = step / length
    hoop_gain = 1.0 / (chord / length) ** 2
    return np.stack(rows).astype(np.float32), axial, hoop_gain


def edge_kernel(halo, disp, vel, mass, stiff, field, inner, outer, sems):
    own = disp.shape[1]
    odd = lax.axis_index("arc") & 1
    copies = [
        pltpu.make_async_copy(disp, field.at[0:3], sems.at[8]),
        pltpu.make_async_copy(vel, field.at[3:6], sems.at[9]),
        pltpu.make_async_copy(mass, field.at[6], sems.at[10]),
        pltpu.make_async_copy(stiff, field.at[7], sems.at[11]),
    ]
    for n, (edge, at) in enumerate(((inner, (1 - odd) * (own - halo)), (outer, odd * (own - halo)))):
        span = pl.ds(pl.multiple_of(at, 8), halo)
        copies += [
            pltpu.make_async_copy(disp.at[:, span, :], edge.at[0:3], sems.at[4 * n]),
            pltpu.make_async_copy(vel.at[:, span, :], edge.at[3:6], sems.at[4 * n + 1]),
            pltpu.make_async_copy(mass.at[span, :], edge.at[6], sems.at[4 * n + 2]),
            pltpu.make_async_copy(stiff.at[span, :], edge.at[7], sems.at[4 * n + 3]),
        ]
    for copy in copies:
        copy.start()
    for copy in copies:
        copy.wait()


KEEP, SEND, FROM_Z, FAR_Z, SAME_X, USED, PLAN = 0, 4, 8, 12, 14, 15, 16


def plan_kernel(
    arc_count, own, slot_ref, lift_ref, rows_ref, static_ref, plan, where_ref, list_ref, lift_out, source
):
    me = lax.axis_index("arc")
    y, z, x, c = arc_digits(me)
    rollers = slot_ref.shape[0]
    roll = static_ref[me]
    begin = static_ref[arc_count + me]
    valid = roll >= 0
    safe = jnp.maximum(roll, 0)
    where_ref[0] = begin
    where_ref[1] = jnp.where(valid, begin, -4 * WIN)
    lift_out[0] = jnp.where(valid, lift_ref[safe], -1e9)
    offset = me * own - HALO + begin
    for step in range(STEPS):
        g = rows_ref[step, pl.ds(safe, 1), :] - offset
        list_ref[step : step + 1, :] = jnp.clip(g, 0, WIN - 1)
    for i in range(source.shape[0]):
        source[i] = -1
    for r in range(rollers):
        source[slot_ref[r]] = static_ref[2 * arc_count + r]

    def line(row, value):
        plan[row : row + 1, :] = jnp.full((1, LANES), value, jnp.int32)

    def index(need):
        ny, _, _, nc = arc_digits(need)
        step = jnp.where((ny >> 1) == (y >> 1), ny ^ y, 2 + (ny ^ y ^ 3))
        return 2 * step + (nc ^ c)

    for way in range(2):
        at = PLAN * way
        for zi in range(4):
            for xr in range(2):
                dest = arc_index(y, z ^ (0, 3, 1, 2)[zi], x ^ xr, c)
                if way == 0:
                    need = slot_ref[jnp.maximum(static_ref[dest], 0)]
                else:
                    need = jnp.maximum(source[dest], 0)
                n = 2 * zi + xr
                line(at + KEEP + n, index(need))
                _, nz, nx, _ = arc_digits(need)
                if n < 4:
                    line(at + FROM_Z + n, (nz == (z ^ 1)).astype(jnp.int32))
                if n < 2:
                    line(at + FAR_Z + n, ((nz != z) & (nz != (z ^ 1))).astype(jnp.int32))
                if n < 1:
                    line(at + SAME_X, (nx == x).astype(jnp.int32))
        line(at + USED, (source[me] >= 0).astype(jnp.int32))


def row_block(field, inner, outer, odd, a, row):
    halo = inner.shape[1]
    own = field.shape[1]
    if row < halo:
        span = slice(row, row + 8)
        return jnp.where(odd, inner[a, span, :], outer[a, span, :])
    if row < halo + own:
        return field[a, row - halo : row - halo + 8, :]
    span = slice(row - halo - own, row - halo - own + 8)
    return jnp.where(odd, outer[a, span, :], inner[a, span, :])


def pack_kernel(field, inner, outer, pack):
    half = field.shape[1] // 2 + inner.shape[1]
    odd = (lax.axis_index("arc") & 1) > 0
    lane = lax.broadcasted_iota(jnp.int32, (8, LANES), 1) // (2 * EDGE)
    for r in range(0, half, 8):
        packed = jnp.zeros((8, LANES), jnp.float32)
        for part in range(2):
            for a in range(8):
                value = row_block(field, inner, outer, odd, a, r + part * half)
                moved = pltpu.roll(value, (8 * a + EDGE + 64 * part) % LANES, 1)
                packed = jnp.where(lane == a + 8 * part, moved, packed)
        pack[r : r + 8, :] = packed


def ring_left(tiles, last):
    a, b = (pltpu.roll(t, LANES - 1, 1) for t in tiles)
    return jnp.where(last, b, a), jnp.where(last, a, b)


def ring_right(tiles, first):
    a, b = (pltpu.roll(t, 1, 1) for t in tiles)
    return jnp.where(first, b, a), jnp.where(first, a, b)


def unpack_block(pack, row, half, a, keep):
    upper = row >= half
    at = pl.multiple_of(jnp.where(upper, row - half, row), 8)
    shift = jnp.where(upper, (2 * LANES - 8 * a - EDGE - 64) % LANES, (2 * LANES - 8 * a - EDGE) % LANES)
    return jnp.where(keep, pltpu.roll(pack[pl.ds(at, 8), :], shift, 1), 0.0)


def clear_tail(state, rows):
    for a in range(3):
        for t in range(2):
            state[a, t, rows : rows + 8, :] = jnp.zeros((8, LANES), jnp.float32)


def load_state(group, source, pack, first_row, base, cycle_total, rows, half, state, vels, coef, ends=False):
    lane = lax.broadcasted_iota(jnp.int32, (8, LANES), 1)
    sub = lax.broadcasted_iota(jnp.int32, (8, LANES), 0)
    keep = (lane < EDGE) | (lane >= LANES - EDGE)
    first = lane == 0
    top = sub == 0

    def body(b, carry):
        r = 8 * b if isinstance(b, int) else pl.multiple_of(b * 8, 8)
        e = first_row + r
        span = pl.ds(r, 8)
        for a in range(3):
            state[a, 0, span, :] = source(a, r)
            state[a, 1, span, :] = unpack_block(pack, e, half, a, keep)
            vels[a, 0, span, :] = TIME_STEP * source(3 + a, r)
            vels[a, 1, span, :] = TIME_STEP * unpack_block(pack, e, half, 3 + a, keep)
        for t, m in enumerate((source(6, r), unpack_block(pack, e, half, 6, keep))):
            coef[0, t, span, :] = (TIME_STEP * TIME_STEP) / jnp.where(m > 0.0, m, 1.0)
        ids = base + e + sub
        inside = (ids >= 0) & (ids < cycle_total - 1)
        k = [
            jnp.where(inside, v, 0.0)
            for v in (source(7, r), unpack_block(pack, e, half, 7, keep))
        ]
        kr = ring_right(k, first)
        new = []
        for t in range(2):
            down = pltpu.roll(k[t], 1, 0)
            coef[1, t, span, :] = k[t]
            coef[2, t, span, :] = 0.5 * (k[t] + kr[t])
            coef[3, t, span, :] = (0.5 * HOOP_GAIN) * (k[t] + jnp.where(top, carry[t], down))
            new.append(down)
        return tuple(new)

    zero = jnp.zeros((8, LANES), jnp.float32)

    def several(b, carry):
        for u in range(group):
            carry = body(b * group + u + int(ends), carry)
        return carry

    carry = (zero, zero)
    if ends:
        carry = body(0, carry)
    carry = lax.fori_loop(0, (rows // 8 - 2 * int(ends)) // group, several, carry)
    if ends:
        body(rows // 8 - 1, carry)
    clear_tail(state, rows)


TABLE, AXIAL, HOOP_GAIN = column_table(2 * LANES)


def advance(table, rows, state, vels, coef, later, vels_later, group, push=None, span_of=None):
    lane = lax.broadcasted_iota(jnp.int32, (8, LANES), 1)
    top = lax.broadcasted_iota(jnp.int32, (8, LANES), 0) == 0
    first, last = lane == 0, lane == LANES - 1

    def const(i):
        return [jnp.broadcast_to(table[2 * i + t : 2 * i + t + 1, :], (8, LANES)) for t in range(2)]

    cj, sj, cb, sb = (const(i) for i in range(4))
    two = range(2)

    def block(r, carry, store=True):
        span, below = pl.ds(r, 8), pl.ds(r + 1, 8)
        x, y, z = ([state[a, t, span, :] for t in two] for a in range(3))
        xn, yn, zn = ([state[a, t, below, :] for t in two] for a in range(3))
        p = [cj[t] * y[t] + sj[t] * z[t] for t in two]
        q = [cb[t] * y[t] + sb[t] * z[t] for t in two]
        ax = [AXIAL * x[t] for t in two]
        pn = [cj[t] * yn[t] + sj[t] * zn[t] for t in two]
        qn = [cb[t] * yn[t] + sb[t] * zn[t] for t in two]
        axn = [AXIAL * xn[t] for t in two]
        q_next = ring_left(q, last)
        anti_next = ring_left([q[t] - ax[t] for t in two], last)
        diag_next = ring_left([qn[t] + axn[t] for t in two], last)
        k = [coef[1, t, span, :] for t in two]
        t_d = [k[t] * (diag_next[t] - (p[t] + ax[t])) for t in two]
        t_a = [k[t] * (anti_next[t] - (pn[t] - axn[t])) for t in two]
        t_h = [coef[3, t, span, :] * (q_next[t] - p[t]) for t in two]
        fx = [coef[2, t, span, :] * (xn[t] - x[t]) for t in two]
        d_left = ring_right(t_d, first)
        a_left = ring_right(t_a, first)
        g_left = ring_right([t_a[t] + t_h[t] for t in two], first)
        new = []
        for t in two:
            up = t_d[t] + t_h[t]
            force = [
                fx[t] + AXIAL * (t_d[t] + a_left[t]),
                cj[t] * up - cb[t] * g_left[t],
                sj[t] * up - sb[t] * g_left[t],
            ]
            low = [
                fx[t] + AXIAL * (d_left[t] + t_a[t]),
                cb[t] * d_left[t] - cj[t] * t_a[t],
                sb[t] * d_left[t] - sj[t] * t_a[t],
            ]
            at = (x[t], y[t], z[t])
            inverse = coef[0, t, span, :]
            for a in range(3):
                moved = pltpu.roll(low[a], 1, 0)
                total = force[a] - jnp.where(top, carry[3 * t + a], moved)
                new.append(moved)
                if not store:
                    continue
                if push is not None and a > 0:
                    total = total + push[a - 1, t, span, :]
                w = vels[a, t, span, :] + inverse * total
                if a == 2:
                    w = w - (GRAVITY * TIME_STEP * TIME_STEP)
                vels_later[a, t, span, :] = w
                later[a, t, span, :] = at[a] + w
        return tuple(new)

    def body(b, carry):
        for u in range(group):
            carry = block(pl.multiple_of(b * (8 * group), 8) + 8 * u, carry)
        return carry

    zero = jnp.zeros((8, LANES), jnp.float32)
    carry = (zero,) * 6
    begin, end = span_of or (0, rows)
    if begin > 0:
        carry = block(begin - 8, carry, store=False)
    if group * 8 == rows:
        for u in range(group):
            carry = block(8 * u, carry)
    else:
        lax.fori_loop(begin // (8 * group), end // (8 * group), body, carry)


def pad_edge_kernel(pad, out):
    lane = lax.broadcasted_iota(jnp.int32, (1, LANES), 1) // (2 * EDGE)
    total = jnp.zeros((1, LANES), jnp.float32)
    slots = pad.shape[1]
    for m in range(slots):
        moved = pltpu.roll(pad[0, m : m + 1, :], LANES - EDGE - 2 * EDGE * m, 1)
        total = jnp.where(lane == slots - 1 - m, moved, total)
    out[...] = jnp.broadcast_to(total, out.shape)


def pad_extend_kernel(pad, edges, *rest):
    out = rest[-1]
    slots = pad.shape[1]
    out[0, :slots, :] = pad[0]
    out[0, slots:, :] = edges[...]


def window_load_kernel(half, base, cycle_total, where_ref, field, inner, outer, columns, state, vels, coef):
    start = pl.multiple_of(where_ref[0], 8)
    halo = inner.shape[1]
    own = field.shape[1]
    odd = (lax.axis_index("arc") & 1) > 0

    def source(a, r):
        row = start + r
        mid = field[a, pl.ds(pl.multiple_of(jnp.clip(row - halo, 0, own - 8), 8), 8), :]
        before = row < halo
        at = jnp.where(before, row, jnp.maximum(row - halo - own, 0))
        span = pl.ds(pl.multiple_of(at, 8), 8)
        end = jnp.where(odd == before, inner[a, span, :], outer[a, span, :])
        return jnp.where(before | (row >= halo + own), end, mid)

    first_id = base(lax.axis_index("arc"))
    load_state(4, source, columns, start, first_id, cycle_total, WIN, half, state, vels, coef)


def contact(table, lift, list_ref, step, state, push, taken, given, held):
    slots = held.shape[1]
    push[...] = jnp.zeros_like(push)
    for m in range(slots):
        g = list_ref[step, m]
        for a in range(2):
            for t in range(2):
                taken[a, t, m : m + 1, :] = state[a + 1, t, pl.ds(g, 1), :]
    for t in range(2):
        sin_angle, cos_angle = table[8 + t : 9 + t, :], table[10 + t : 11 + t, :]
        lateral = sin_angle + taken[0, t]
        q = held[t]
        intrusion = lift + CRADLE_CURVE * lateral * lateral - (1.0 - cos_angle) - taken[1, t] - q
        load = CONTACT_STIFF * jnp.maximum(intrusion, 0.0)
        normal = load / jnp.sqrt(1.0 + 4.0 * CRADLE_CURVE * CRADLE_CURVE * lateral * lateral)
        given[0, t] = -2.0 * CRADLE_CURVE * lateral * normal
        given[1, t] = normal
        held[t] = q + PAD_RATE * (load - PAD_STIFF * q)
    for m in range(slots):
        g = list_ref[step, m]
        for a in range(2):
            for t in range(2):
                push[a, t, pl.ds(g, 1), :] += given[a, t, m : m + 1, :]


def window_kernel(
    list_ref, lift_ref, plan, table, state, vels, coef, pads, handed, *rest
):
    state_out, vels_out, push, pad_out, spare, vels_spare, taken, given, held = rest[-9:]
    same = plan[SAME_X : SAME_X + 1, :] > 0
    slots = held.shape[1]
    lane = lax.broadcasted_iota(jnp.int32, (8, LANES), 1)
    keep = (lane < EDGE) | (lane >= LANES - EDGE)
    both = jnp.where(same, pads[0], handed[0])
    held[0] = both[:slots]
    for part in range(2):
        moved = pltpu.roll(both[slots:], EDGE + 64 * part, 1, stride=2 * EDGE, stride_axis=0)
        held[1, 8 * part : 8 * part + 8, :] = jnp.where(keep, moved, 0.0)
    lift = lift_ref[0]
    clear_tail(spare, WIN)
    clear_tail(state_out, WIN)
    now = (state, vels)
    for step in range(STEPS):
        contact(table, lift, list_ref, step, now[0], push, taken, given, held)
        if step < STEPS - 1:
            later = (spare, vels_spare) if (STEPS - step) % 2 else (state_out, vels_out)
            advance(table, WIN, *now, coef, *later, WIN // 8, push)
            now = later
    pad_out[0] = held[0]


def window_last_kernel(table, state, vels, coef, push, result, later, vels_later):
    advance(table, WIN, state, vels, coef, later, vels_later, WIN // 8, push)
    for a in range(3):
        result[a] = later[a, 0, :WIN, :]
        result[3 + a] = vels_later[a, 0] * (1.0 / TIME_STEP)


def bulk_load_kernel(half, base, cycle_total, rows, field, inner, outer, columns, state, vels, coef):
    first_row = HALO - 8
    odd = (lax.axis_index("arc") & 1) > 0

    def source(a, r):
        if isinstance(r, int):
            return row_block(field, inner, outer, odd, a, first_row + r)
        return field[a, pl.ds(pl.multiple_of(r - 8, 8), 8), :]

    first_id = base(lax.axis_index("arc"))
    load_state(
        LOAD_GROUP, source, columns, first_row, first_id, cycle_total, rows, half, state, vels, coef, ends=True
    )


def bulk_step_kernel(rows, part, table, state, vels, coef, *rest):
    later, vels_later = rest[-2:]
    third = rows // PARTS
    advance(table, rows, state, vels, coef, later, vels_later, GROUP, span_of=(part * third, (part + 1) * third))
    if part == 0:
        clear_tail(later, rows)


def bulk_store_kernel(rows, where_ref, state, vels, window, *rest):
    disp_out, vel_out, token, result, sems = rest[-5:]
    token[...] = jnp.zeros_like(token)
    count = (rows - 16) // CHUNKS
    start = where_ref[1]
    sub = lax.broadcasted_iota(jnp.int32, (8, LANES), 0)

    def body(b, carry):
        r = pl.multiple_of(b * 8, 8)
        inner = pl.ds(pl.multiple_of(r + 8, 8), 8)
        rel = HALO + r - start
        at = pl.ds(pl.multiple_of(jnp.clip(rel, 0, WIN - 8), 8), 8)
        ids = rel + sub
        use = (ids >= STEPS) & (ids < WIN - STEPS)
        for a in range(3):
            result[a, pl.ds(r, 8), :] = jnp.where(use, window[a, at, :], state[a, 0, inner, :])
            result[3 + a, pl.ds(r, 8), :] = jnp.where(
                use, window[3 + a, at, :], vels[a, 0, inner, :] * (1.0 / TIME_STEP)
            )
        return carry

    copies = []
    for chunk in range(CHUNKS):
        lax.fori_loop(chunk * count // 8, (chunk + 1) * count // 8, body, 0)
        span = pl.ds(chunk * count, count)
        for n, out in enumerate((disp_out, vel_out)):
            copy = pltpu.make_async_copy(
                result.at[3 * n : 3 * n + 3, span, :], out.at[:, span, :], sems.at[2 * chunk + n]
            )
            copy.start()
            copies.append(copy)
    for copy in copies:
        copy.wait()


def stack_kernel(first, second, *rest):
    count = first.shape[0]
    rest[-1][:count] = first[...]
    rest[-1][count:] = second[...]


def pick_kernel(way, plan, first, second, *rest):
    keep, send = rest[-2:]
    parts = [ref[n] for ref in (first, second) for n in range(4)]
    for out, row in ((keep, KEEP), (send, SEND)):
        for n in range(4):
            at = PLAN * way + row + n
            index = plan[at : at + 1, :]
            value = parts[0]
            for m in range(1, 8):
                value = jnp.where(index == m, parts[m], value)
            out[n] = value


def choose_kernel(way, row, plan, kept, got, *rest):
    keep, send = rest[-2:]
    count = got.shape[0]
    for n in range(count):
        at = PLAN * way + row + n
        value = jnp.where(plan[at : at + 1, :] > 0, got[n], kept[n])
        if n < count // 2:
            keep[n] = value
        else:
            send[n - count // 2] = value


def last_kernel(plan, mine, handed, before, *rest):
    out = rest[-1]
    used = plan[PLAN + USED : PLAN + USED + 1, :] > 0
    same = plan[PLAN + SAME_X : PLAN + SAME_X + 1, :] > 0
    out[0] = jnp.where(used, jnp.where(same, mine[0], handed[0]), before[0])


VMEM = pl.BlockSpec(memory_space=pltpu.VMEM)
SMEM = pl.BlockSpec(memory_space=pltpu.SMEM)
ANY = pl.BlockSpec(memory_space=pl.ANY)
HBM = pl.BlockSpec(memory_space=pltpu.HBM)


def real(*shape):
    return jax.ShapeDtypeStruct(shape, jnp.float32)


def whole(*shape):
    return jax.ShapeDtypeStruct(shape, jnp.int32)


def call(kernel, name, outs, ins, in_specs=None, out_specs=None, scratch=(), micros=0.1, after=(), limit=LIMIT, aliases=()):
    single = not isinstance(outs, tuple)
    shapes = (outs,) if single else outs
    result = pl.pallas_call(
        kernel,
        out_shape=shapes,
        in_specs=list(in_specs or [VMEM] * len(ins)) + [ANY] * len(after),
        out_specs=tuple(out_specs or [VMEM] * len(shapes)),
        scratch_shapes=list(scratch),
        compiler_params=pltpu.CompilerParams(vmem_limit_bytes=limit),
        cost_estimate=pl.CostEstimate(flops=0, bytes_accessed=int(micros * 3.6e6), transcendentals=0),
        input_output_aliases=dict(aliases),
        name=name,
    )(*ins, *after)
    return result[0] if single else result


def route(value, plan, way, between):
    shape = value.shape[1:]
    got = lax.ppermute(value, "arc", flips(c=1))
    held = call(stack_kernel, "stack", real(2, *shape), (value, got), after=between(0, value))
    got = lax.ppermute(held, "arc", flips(y=1))
    held = call(stack_kernel, "stack", real(4, *shape), (held, got), after=between(1, held))
    got = lax.ppermute(held, "arc", flips(y=3))
    keep, send = call(
        functools.partial(pick_kernel, way), "pick", (real(4, *shape),) * 2, (plan, held, got), after=between(2, held)
    )
    got = lax.ppermute(send, "arc", flips(z=1))
    keep, send = call(
        functools.partial(choose_kernel, way, FROM_Z), "choose", (real(2, *shape),) * 2, (plan, keep, got),
        after=between(3, send),
    )
    got = lax.ppermute(send, "arc", flips(z=3))
    keep, send = call(
        functools.partial(choose_kernel, way, FAR_Z), "choose", (real(1, *shape),) * 2, (plan, keep, got),
        after=between(4, send),
    )
    return keep, lax.ppermute(send, "arc", flips(x=1)), between(5, send)


def static_tables(arc_count, cycle_dev, roller_total):
    cycle_total = arc_count * cycle_dev
    centres = [r * (cycle_total - 1) // (roller_total - 1) for r in range(roller_total)]
    span = REACH + STEPS - 1
    near = np.full(arc_count, -1, np.int32)
    start = np.zeros(arc_count, np.int32)
    for d in range(arc_count):
        base = d * cycle_dev
        touching = [r for r, c in enumerate(centres) if base - span <= c < base + cycle_dev + span]
        assert len(touching) <= 1
        if touching:
            near[d] = touching[0]
            offset = centres[touching[0]] - base - REACH - STEPS - STEPS + 1 + HALO
            start[d] = offset // 8 * 8
            assert 0 <= start[d] <= cycle_dev + 2 * HALO - WIN
    home = np.array([c // cycle_dev for c in centres], np.int32)
    return near, start, home


def local(displacement, velocity, node_mass, wall_stiff, pad_state, roller_lift, contact_rows, roller_slot):
    cycle_dev = displacement.shape[1]
    slots = pad_state.shape[1]
    roller_total = roller_lift.shape[0]
    arc_count = lax.axis_size("arc")
    cycle_total = cycle_dev * arc_count
    half = cycle_dev // 2 + HALO
    rows = cycle_dev + 16
    fields = (displacement, velocity, node_mass, wall_stiff)
    static = np.concatenate(static_tables(arc_count, cycle_dev, roller_total)).astype(np.int32)
    swap = [(0, 1), (1, 0)]
    table = jnp.asarray(TABLE)[lax.axis_index("circ")]

    def base(me):
        return me * cycle_dev - HALO

    def buffers(count):
        return real(3, 2, count + 8, LANES), real(3, 2, count, LANES), real(4, 2, count, LANES)

    def room(count):
        return [pltpu.VMEM(shape.shape, jnp.float32) for shape in buffers(count)[:2]]

    pad_edges = call(pad_edge_kernel, "pad_edge", real(8, LANES), (pad_state,))
    pad_edges = lax.ppermute(pad_edges, "circ", swap)
    field, inner, outer = call(
        functools.partial(edge_kernel, HALO), "edge",
        (real(8, cycle_dev, LANES), real(8, HALO, LANES), real(8, HALO, LANES)), fields,
        in_specs=[HBM] * 4, scratch=[pltpu.SemaphoreType.DMA((12,))], micros=2.0, limit=MOST,
    )
    plan, where, rows_in, lift = call(
        functools.partial(plan_kernel, arc_count, cycle_dev), "plan",
        (whole(2 * PLAN, LANES), whole(2), whole(STEPS, slots), real(1)),
        (roller_slot, roller_lift, contact_rows, jnp.asarray(static)),
        in_specs=[SMEM, SMEM, VMEM, SMEM], out_specs=[VMEM, SMEM, VMEM, SMEM],
        scratch=[pltpu.SMEM((arc_count,), jnp.int32)], micros=3.0,
    )

    outward = [pair for i in range(1, arc_count, 2) for pair in ((i, (i + 1) % arc_count), ((i + 1) % arc_count, i))]
    token = inner
    inner = lax.ppermute(inner, "arc", flips(c=1))
    outer = lax.ppermute(outer, "arc", outward)
    pack = call(pack_kernel, "pack", real(half, LANES), (field, inner, outer), micros=2.0)
    columns = lax.ppermute(pack, "circ", swap)
    kept = {"done": 0}

    def load_window():
        return call(
            functools.partial(window_load_kernel, half, base, cycle_total), "window_load", buffers(WIN),
            (where, field, inner, outer, columns), in_specs=[SMEM] + [VMEM] * 4, micros=0.8,
        )

    def load_bulk():
        return call(
            functools.partial(bulk_load_kernel, half, base, cycle_total, rows), "bulk_load", buffers(rows),
            (field, inner, outer, columns), micros=2.0,
        )

    def step_bulk(value, count):
        for _ in range(count):
            step, part = divmod(kept["done"], PARTS)
            state, vels, coef = kept["bulk"]
            before = kept["next"] if part else ()
            kept["next"] = call(
                functools.partial(bulk_step_kernel, rows, part), "bulk_step", buffers(rows)[:2],
                (table, state, vels, coef, *before), micros=2.4 / PARTS, after=(value,),
                aliases={4: 0, 5: 1} if part else {},
            )
            kept["done"] += 1
            if part == PARTS - 1:
                kept["bulk"] = (*kept["next"], coef)
        return kept["next"][:1]

    def store_bulk(value):
        state, vels, _ = kept["bulk"]
        outs = call(
            functools.partial(bulk_store_kernel, rows), "bulk_store",
            (real(3, cycle_dev, LANES), real(3, cycle_dev, LANES), real(8, LANES)),
            (where, state, vels, kept["last"], value),
            in_specs=[SMEM] + [VMEM] * 3 + [ANY], out_specs=[HBM] * 2 + [VMEM],
            scratch=[pltpu.VMEM((6, cycle_dev, LANES), jnp.float32), pltpu.SemaphoreType.DMA((2 * CHUNKS,))],
            micros=2.0,
        )
        kept["outs"] = outs[:2]
        return outs[2:]

    def going(stage, value):
        if stage == 1:
            return (pack,)
        if stage == 3:
            kept["window"] = load_window()
            kept["bulk"] = load_bulk()
            return (kept["window"][0], kept["bulk"][0])
        return step_bulk(value, 2) if stage > 3 else ()

    value = call(
        pad_extend_kernel, "pad_extend", real(1, slots + 8, LANES), (pad_state, pad_edges), after=(plan, token)
    )
    pads, handed, done = route(value, plan, 0, going)

    win_state, win_vels, win_coef = kept["window"]
    win_state, win_vels, push, pad_new = call(
        window_kernel, "window", (*buffers(WIN)[:2], real(2, 2, WIN, LANES), real(1, slots, LANES)),
        (rows_in, lift, plan, table, win_state, win_vels, win_coef, pads, handed),
        after=done,
        in_specs=[SMEM] * 2 + [VMEM] * 7,
        scratch=room(WIN)
        + [
            pltpu.VMEM((2, 2, slots, LANES), jnp.float32),
            pltpu.VMEM((2, 2, slots, LANES), jnp.float32),
            pltpu.VMEM((2, slots, LANES), jnp.float32),
        ],
        micros=2.0,
    )

    def coming(stage, value):
        if stage == 0:
            kept["last"] = call(
                window_last_kernel, "window_last", real(6, WIN, LANES), (table, win_state, win_vels, win_coef, push),
                scratch=room(WIN), micros=0.6,
            )
            return (kept["last"],)
        return store_bulk(value) if stage == 5 else step_bulk(value, 2)

    pads, handed, done = route(pad_new, plan, 1, coming)
    pad_result = call(last_kernel, "last", real(1, slots, LANES), (plan, pads, handed, pad_state), after=done)
    return *kept["outs"], pad_result


def solution(mesh):
    placed = (
        P(None, "arc", "circ"),
        P(None, "arc", "circ"),
        P("arc", "circ"),
        P("arc", "circ"),
        P("arc", None, "circ"),
        P(),
        P(),
        P(),
    )
    return jax.shard_map(
        local,
        mesh=mesh,
        in_specs=placed,
        out_specs=(P(None, "arc", "circ"), P(None, "arc", "circ"), P("arc", None, "circ")),
        check_vma=False,
    )
```

```python
import functools
import math

import jax
import jax.numpy as jnp
import numpy as np
from jax import lax
from jax.experimental import pallas as pl
from jax.experimental.pallas import tpu as pltpu
from jax.sharding import PartitionSpec as P

STEPS = 4
REACH = 20
TIME_STEP = 0.1
GRAVITY = 0.2
CONTACT_STIFF = 2.0
CRADLE_CURVE = 0.5
PAD_RATE = 0.2
PAD_STIFF = 1.0

LANES = 128
EDGE = 4
HALO = 48
WIN = 64
CHUNKS = 4
GROUP = 11
PARTS = 3
LOAD_GROUP = 4
LIMIT = 16 * 1024 * 1024
MOST = 60 * 1024 * 1024


def arc_digits(index):
    return (index >> 4, (index >> 2) & 3, (index >> 1) & 1, index & 1)


def arc_index(y, z, x, c):
    return (y << 4) + (z << 2) + (x << 1) + c


def flips(y=0, z=0, x=0, c=0):
    out = []
    for i in range(64):
        iy, iz, ix, ic = arc_digits(i)
        out.append((i, arc_index(iy ^ y, iz ^ z, ix ^ x, ic ^ c)))
    return out


def column_table(circ_total):
    step = 2.0 * math.pi / circ_total
    chord = 2.0 * math.sin(step / 2.0)
    length = math.sqrt(step * step + chord * chord)
    rows = []
    for half in range(2):
        cols = (half * LANES + np.arange(2 * LANES)) % circ_total
        phase = step * (cols + 0.5)
        before = step * (cols - 0.5)
        theta = step * cols
        parts = [
            chord / length * np.cos(phase),
            chord / length * np.sin(phase),
            chord / length * np.cos(before),
            chord / length * np.sin(before),
            np.sin(theta),
            np.cos(theta),
            np.zeros_like(theta),
            np.zeros_like(theta),
        ]
        rows.append(np.concatenate([p.reshape(2, LANES) for p in parts], axis=0))
    axial = step / length
    hoop_gain = 1.0 / (chord / length) ** 2
    return np.stack(rows).astype(np.float32), axial, hoop_gain


def edge_kernel(halo, disp, vel, mass, stiff, *rest):
    inner, outer, sems = rest[-3:]
    own = disp.shape[1]
    odd = lax.axis_index("arc") & 1
    copies = []
    for n, (edge, at) in enumerate(((inner, (1 - odd) * (own - halo)), (outer, odd * (own - halo)))):
        span = pl.ds(pl.multiple_of(at, 8), halo)
        copies += [
            pltpu.make_async_copy(disp.at[:, span, :], edge.at[0:3], sems.at[4 * n]),
            pltpu.make_async_copy(vel.at[:, span, :], edge.at[3:6], sems.at[4 * n + 1]),
            pltpu.make_async_copy(mass.at[span, :], edge.at[6], sems.at[4 * n + 2]),
            pltpu.make_async_copy(stiff.at[span, :], edge.at[7], sems.at[4 * n + 3]),
        ]
    for copy in copies:
        copy.start()
    for copy in copies:
        copy.wait()


KEEP, SEND, FROM_Z, FAR_Z, SAME_X, USED, PLAN = 0, 4, 8, 12, 14, 15, 16


def plan_kernel(
    arc_count, own, slot_ref, lift_ref, rows_ref, static_ref, plan, where_ref, list_ref, lift_out, source
):
    me = lax.axis_index("arc")
    y, z, x, c = arc_digits(me)
    rollers = slot_ref.shape[0]
    roll = static_ref[me]
    begin = static_ref[arc_count + me]
    valid = roll >= 0
    safe = jnp.maximum(roll, 0)
    where_ref[0] = begin
    where_ref[1] = jnp.where(valid, begin, -4 * WIN)
    lift_out[0] = jnp.where(valid, lift_ref[safe], -1e9)
    offset = me * own - HALO + begin
    for step in range(STEPS):
        g = rows_ref[step, pl.ds(safe, 1), :] - offset
        list_ref[step : step + 1, :] = jnp.clip(g, 0, WIN - 1)
    for i in range(source.shape[0]):
        source[i] = -1
    for r in range(rollers):
        source[slot_ref[r]] = static_ref[2 * arc_count + r]

    def line(row, value):
        plan[row : row + 1, :] = jnp.full((1, LANES), value, jnp.int32)

    def index(need):
        ny, _, _, nc = arc_digits(need)
        step = jnp.where((ny >> 1) == (y >> 1), ny ^ y, 2 + (ny ^ y ^ 3))
        return 2 * step + (nc ^ c)

    for way in range(2):
        at = PLAN * way
        for zi in range(4):
            for xr in range(2):
                dest = arc_index(y, z ^ (0, 3, 1, 2)[zi], x ^ xr, c)
                if way == 0:
                    need = slot_ref[jnp.maximum(static_ref[dest], 0)]
                else:
                    need = jnp.maximum(source[dest], 0)
                n = 2 * zi + xr
                line(at + KEEP + n, index(need))
                _, nz, nx, _ = arc_digits(need)
                if n < 4:
                    line(at + FROM_Z + n, (nz == (z ^ 1)).astype(jnp.int32))
                if n < 2:
                    line(at + FAR_Z + n, ((nz != z) & (nz != (z ^ 1))).astype(jnp.int32))
                if n < 1:
                    line(at + SAME_X, (nx == x).astype(jnp.int32))
        line(at + USED, (source[me] >= 0).astype(jnp.int32))


def take(fields, a, span):
    disp, vel, mass, stiff = fields
    if a < 3:
        return disp[a, span, :]
    if a < 6:
        return vel[a - 3, span, :]
    return mass[span, :] if a == 6 else stiff[span, :]


def row_block(fields, inner, outer, odd, a, row):
    halo = inner.shape[1]
    own = fields[0].shape[1]
    if row < halo:
        span = slice(row, row + 8)
        return jnp.where(odd, inner[a, span, :], outer[a, span, :])
    if row < halo + own:
        return take(fields, a, slice(row - halo, row - halo + 8))
    span = slice(row - halo - own, row - halo - own + 8)
    return jnp.where(odd, outer[a, span, :], inner[a, span, :])


def pack_kernel(*refs):
    fields, inner, outer, pack = refs[:4], refs[4], refs[5], refs[-1]
    half = fields[0].shape[1] // 2 + inner.shape[1]
    odd = (lax.axis_index("arc") & 1) > 0
    lane = lax.broadcasted_iota(jnp.int32, (8, LANES), 1) // (2 * EDGE)
    for r in range(0, half, 8):
        packed = jnp.zeros((8, LANES), jnp.float32)
        for part in range(2):
            for a in range(8):
                value = row_block(fields, inner, outer, odd, a, r + part * half)
                moved = pltpu.roll(value, (8 * a + EDGE + 64 * part) % LANES, 1)
                packed = jnp.where(lane == a + 8 * part, moved, packed)
        pack[r : r + 8, :] = packed


def ring_left(tiles, last):
    a, b = (pltpu.roll(t, LANES - 1, 1) for t in tiles)
    return jnp.where(last, b, a), jnp.where(last, a, b)


def ring_right(tiles, first):
    a, b = (pltpu.roll(t, 1, 1) for t in tiles)
    return jnp.where(first, b, a), jnp.where(first, a, b)


def unpack_block(pack, row, half, a, keep):
    upper = row >= half
    at = pl.multiple_of(jnp.where(upper, row - half, row), 8)
    shift = jnp.where(upper, (2 * LANES - 8 * a - EDGE - 64) % LANES, (2 * LANES - 8 * a - EDGE) % LANES)
    return jnp.where(keep, pltpu.roll(pack[pl.ds(at, 8), :], shift, 1), 0.0)


def clear_tail(state, rows):
    for a in range(3):
        for t in range(2):
            state[a, t, rows : rows + 8, :] = jnp.zeros((8, LANES), jnp.float32)


def load_state(group, source, pack, first_row, base, cycle_total, rows, half, state, vels, coef, ends=False):
    lane = lax.broadcasted_iota(jnp.int32, (8, LANES), 1)
    sub = lax.broadcasted_iota(jnp.int32, (8, LANES), 0)
    keep = (lane < EDGE) | (lane >= LANES - EDGE)
    first = lane == 0
    top = sub == 0

    def body(b, carry):
        r = 8 * b if isinstance(b, int) else pl.multiple_of(b * 8, 8)
        e = first_row + r
        span = pl.ds(r, 8)
        for a in range(3):
            state[a, 0, span, :] = source(a, r)
            state[a, 1, span, :] = unpack_block(pack, e, half, a, keep)
            vels[a, 0, span, :] = TIME_STEP * source(3 + a, r)
            vels[a, 1, span, :] = TIME_STEP * unpack_block(pack, e, half, 3 + a, keep)
        for t, m in enumerate((source(6, r), unpack_block(pack, e, half, 6, keep))):
            coef[0, t, span, :] = (TIME_STEP * TIME_STEP) / jnp.where(m > 0.0, m, 1.0)
        ids = base + e + sub
        inside = (ids >= 0) & (ids < cycle_total - 1)
        k = [
            jnp.where(inside, v, 0.0)
            for v in (source(7, r), unpack_block(pack, e, half, 7, keep))
        ]
        kr = ring_right(k, first)
        new = []
        for t in range(2):
            down = pltpu.roll(k[t], 1, 0)
            coef[1, t, span, :] = k[t]
            coef[2, t, span, :] = 0.5 * (k[t] + kr[t])
            coef[3, t, span, :] = (0.5 * HOOP_GAIN) * (k[t] + jnp.where(top, carry[t], down))
            new.append(down)
        return tuple(new)

    zero = jnp.zeros((8, LANES), jnp.float32)

    def several(b, carry):
        for u in range(group):
            carry = body(b * group + u + int(ends), carry)
        return carry

    carry = (zero, zero)
    if ends:
        carry = body(0, carry)
    carry = lax.fori_loop(0, (rows // 8 - 2 * int(ends)) // group, several, carry)
    if ends:
        body(rows // 8 - 1, carry)
    clear_tail(state, rows)


TABLE, AXIAL, HOOP_GAIN = column_table(2 * LANES)


def advance(table, rows, state, vels, coef, later, vels_later, group, push=None, span_of=None):
    lane = lax.broadcasted_iota(jnp.int32, (8, LANES), 1)
    top = lax.broadcasted_iota(jnp.int32, (8, LANES), 0) == 0
    first, last = lane == 0, lane == LANES - 1

    def const(i):
        return [jnp.broadcast_to(table[2 * i + t : 2 * i + t + 1, :], (8, LANES)) for t in range(2)]

    cj, sj, cb, sb = (const(i) for i in range(4))
    two = range(2)

    def block(r, carry, store=True):
        span, below = pl.ds(r, 8), pl.ds(r + 1, 8)
        x, y, z = ([state[a, t, span, :] for t in two] for a in range(3))
        xn, yn, zn = ([state[a, t, below, :] for t in two] for a in range(3))
        p = [cj[t] * y[t] + sj[t] * z[t] for t in two]
        q = [cb[t] * y[t] + sb[t] * z[t] for t in two]
        ax = [AXIAL * x[t] for t in two]
        pn = [cj[t] * yn[t] + sj[t] * zn[t] for t in two]
        qn = [cb[t] * yn[t] + sb[t] * zn[t] for t in two]
        axn = [AXIAL * xn[t] for t in two]
        q_next = ring_left(q, last)
        anti_next = ring_left([q[t] - ax[t] for t in two], last)
        diag_next = ring_left([qn[t] + axn[t] for t in two], last)
        k = [coef[1, t, span, :] for t in two]
        t_d = [k[t] * (diag_next[t] - (p[t] + ax[t])) for t in two]
        t_a = [k[t] * (anti_next[t] - (pn[t] - axn[t])) for t in two]
        t_h = [coef[3, t, span, :] * (q_next[t] - p[t]) for t in two]
        fx = [coef[2, t, span, :] * (xn[t] - x[t]) for t in two]
        d_left = ring_right(t_d, first)
        a_left = ring_right(t_a, first)
        g_left = ring_right([t_a[t] + t_h[t] for t in two], first)
        new = []
        for t in two:
            up = t_d[t] + t_h[t]
            force = [
                fx[t] + AXIAL * (t_d[t] + a_left[t]),
                cj[t] * up - cb[t] * g_left[t],
                sj[t] * up - sb[t] * g_left[t],
            ]
            low = [
                fx[t] + AXIAL * (d_left[t] + t_a[t]),
                cb[t] * d_left[t] - cj[t] * t_a[t],
                sb[t] * d_left[t] - sj[t] * t_a[t],
            ]
            at = (x[t], y[t], z[t])
            inverse = coef[0, t, span, :]
            for a in range(3):
                moved = pltpu.roll(low[a], 1, 0)
                total = force[a] - jnp.where(top, carry[3 * t + a], moved)
                new.append(moved)
                if not store:
                    continue
                if push is not None and a > 0:
                    total = total + push[a - 1, t, span, :]
                w = vels[a, t, span, :] + inverse * total
                if a == 2:
                    w = w - (GRAVITY * TIME_STEP * TIME_STEP)
                vels_later[a, t, span, :] = w
                later[a, t, span, :] = at[a] + w
        return tuple(new)

    def body(b, carry):
        for u in range(group):
            carry = block(pl.multiple_of(b * (8 * group), 8) + 8 * u, carry)
        return carry

    zero = jnp.zeros((8, LANES), jnp.float32)
    carry = (zero,) * 6
    begin, end = span_of or (0, rows)
    if begin > 0:
        carry = block(begin - 8, carry, store=False)
    if group * 8 == rows:
        for u in range(group):
            carry = block(8 * u, carry)
    else:
        lax.fori_loop(begin // (8 * group), end // (8 * group), body, carry)


def pad_edge_kernel(pad, out):
    lane = lax.broadcasted_iota(jnp.int32, (1, LANES), 1) // (2 * EDGE)
    total = jnp.zeros((1, LANES), jnp.float32)
    slots = pad.shape[1]
    for m in range(slots):
        moved = pltpu.roll(pad[0, m : m + 1, :], LANES - EDGE - 2 * EDGE * m, 1)
        total = jnp.where(lane == slots - 1 - m, moved, total)
    out[...] = jnp.broadcast_to(total, out.shape)


def pad_extend_kernel(pad, edges, *rest):
    out = rest[-1]
    slots = pad.shape[1]
    out[0, :slots, :] = pad[0]
    out[0, slots:, :] = edges[...]


def window_load_kernel(half, base, cycle_total, where_ref, *refs):
    fields, (inner, outer, columns, state, vels, coef) = refs[:4], refs[4:]
    start = pl.multiple_of(where_ref[0], 8)
    halo = inner.shape[1]
    own = fields[0].shape[1]
    odd = (lax.axis_index("arc") & 1) > 0

    def source(a, r):
        row = start + r
        mid = take(fields, a, pl.ds(pl.multiple_of(jnp.clip(row - halo, 0, own - 8), 8), 8))
        before = row < halo
        at = jnp.where(before, row, jnp.maximum(row - halo - own, 0))
        span = pl.ds(pl.multiple_of(at, 8), 8)
        end = jnp.where(odd == before, inner[a, span, :], outer[a, span, :])
        return jnp.where(before | (row >= halo + own), end, mid)

    first_id = base(lax.axis_index("arc"))
    load_state(4, source, columns, start, first_id, cycle_total, WIN, half, state, vels, coef)


def contact(table, lift, list_ref, step, state, push, taken, given, held):
    slots = held.shape[1]
    push[...] = jnp.zeros_like(push)
    for m in range(slots):
        g = list_ref[step, m]
        for a in range(2):
            for t in range(2):
                taken[a, t, m : m + 1, :] = state[a + 1, t, pl.ds(g, 1), :]
    for t in range(2):
        sin_angle, cos_angle = table[8 + t : 9 + t, :], table[10 + t : 11 + t, :]
        lateral = sin_angle + taken[0, t]
        q = held[t]
        intrusion = lift + CRADLE_CURVE * lateral * lateral - (1.0 - cos_angle) - taken[1, t] - q
        load = CONTACT_STIFF * jnp.maximum(intrusion, 0.0)
        normal = load / jnp.sqrt(1.0 + 4.0 * CRADLE_CURVE * CRADLE_CURVE * lateral * lateral)
        given[0, t] = -2.0 * CRADLE_CURVE * lateral * normal
        given[1, t] = normal
        held[t] = q + PAD_RATE * (load - PAD_STIFF * q)
    for m in range(slots):
        g = list_ref[step, m]
        for a in range(2):
            for t in range(2):
                push[a, t, pl.ds(g, 1), :] += given[a, t, m : m + 1, :]


def window_kernel(
    list_ref, lift_ref, plan, table, state, vels, coef, pads, handed, *rest
):
    state_out, vels_out, push, pad_out, spare, vels_spare, taken, given, held = rest[-9:]
    same = plan[SAME_X : SAME_X + 1, :] > 0
    slots = held.shape[1]
    lane = lax.broadcasted_iota(jnp.int32, (8, LANES), 1)
    keep = (lane < EDGE) | (lane >= LANES - EDGE)
    both = jnp.where(same, pads[0], handed[0])
    held[0] = both[:slots]
    for part in range(2):
        moved = pltpu.roll(both[slots:], EDGE + 64 * part, 1, stride=2 * EDGE, stride_axis=0)
        held[1, 8 * part : 8 * part + 8, :] = jnp.where(keep, moved, 0.0)
    lift = lift_ref[0]
    clear_tail(spare, WIN)
    clear_tail(state_out, WIN)
    now = (state, vels)
    for step in range(STEPS):
        contact(table, lift, list_ref, step, now[0], push, taken, given, held)
        if step < STEPS - 1:
            later = (spare, vels_spare) if (STEPS - step) % 2 else (state_out, vels_out)
            advance(table, WIN, *now, coef, *later, WIN // 8, push)
            now = later
    pad_out[0] = held[0]


def window_last_kernel(table, state, vels, coef, push, result, later, vels_later):
    advance(table, WIN, state, vels, coef, later, vels_later, WIN // 8, push)
    for a in range(3):
        result[a] = later[a, 0, :WIN, :]
        result[3 + a] = vels_later[a, 0] * (1.0 / TIME_STEP)


def bulk_load_kernel(half, base, cycle_total, rows, *refs):
    fields, (inner, outer, columns, state, vels, coef) = refs[:4], refs[4:]
    first_row = HALO - 8
    odd = (lax.axis_index("arc") & 1) > 0

    def source(a, r):
        if isinstance(r, int):
            return row_block(fields, inner, outer, odd, a, first_row + r)
        return take(fields, a, pl.ds(pl.multiple_of(r - 8, 8), 8))

    first_id = base(lax.axis_index("arc"))
    load_state(
        LOAD_GROUP, source, columns, first_row, first_id, cycle_total, rows, half, state, vels, coef, ends=True
    )


def bulk_step_kernel(rows, part, table, state, vels, coef, *rest):
    later, vels_later = rest[-2:]
    third = rows // PARTS
    advance(table, rows, state, vels, coef, later, vels_later, GROUP, span_of=(part * third, (part + 1) * third))
    if part == 0:
        clear_tail(later, rows)


def bulk_store_kernel(rows, where_ref, state, vels, window, *rest):
    disp_out, vel_out, token, result, sems = rest[-5:]
    token[...] = jnp.zeros_like(token)
    count = (rows - 16) // CHUNKS
    start = where_ref[1]
    sub = lax.broadcasted_iota(jnp.int32, (8, LANES), 0)

    def body(b, carry):
        r = pl.multiple_of(b * 8, 8)
        inner = pl.ds(pl.multiple_of(r + 8, 8), 8)
        rel = HALO + r - start
        at = pl.ds(pl.multiple_of(jnp.clip(rel, 0, WIN - 8), 8), 8)
        ids = rel + sub
        use = (ids >= STEPS) & (ids < WIN - STEPS)
        for a in range(3):
            result[a, pl.ds(r, 8), :] = jnp.where(use, window[a, at, :], state[a, 0, inner, :])
            result[3 + a, pl.ds(r, 8), :] = jnp.where(
                use, window[3 + a, at, :], vels[a, 0, inner, :] * (1.0 / TIME_STEP)
            )
        return carry

    copies = []
    for chunk in range(CHUNKS):
        lax.fori_loop(chunk * count // 8, (chunk + 1) * count // 8, body, 0)
        span = pl.ds(chunk * count, count)
        for n, out in enumerate((disp_out, vel_out)):
            copy = pltpu.make_async_copy(
                result.at[3 * n : 3 * n + 3, span, :], out.at[:, span, :], sems.at[2 * chunk + n]
            )
            copy.start()
            copies.append(copy)
    for copy in copies:
        copy.wait()


def stack_kernel(first, second, *rest):
    count = first.shape[0]
    rest[-1][:count] = first[...]
    rest[-1][count:] = second[...]


def pick_kernel(way, plan, first, second, *rest):
    keep, send = rest[-2:]
    parts = [ref[n] for ref in (first, second) for n in range(4)]
    for out, row in ((keep, KEEP), (send, SEND)):
        for n in range(4):
            at = PLAN * way + row + n
            index = plan[at : at + 1, :]
            value = parts[0]
            for m in range(1, 8):
                value = jnp.where(index == m, parts[m], value)
            out[n] = value


def choose_kernel(way, row, plan, kept, got, *rest):
    keep, send = rest[-2:]
    count = got.shape[0]
    for n in range(count):
        at = PLAN * way + row + n
        value = jnp.where(plan[at : at + 1, :] > 0, got[n], kept[n])
        if n < count // 2:
            keep[n] = value
        else:
            send[n - count // 2] = value


def last_kernel(plan, mine, handed, before, *rest):
    out = rest[-1]
    used = plan[PLAN + USED : PLAN + USED + 1, :] > 0
    same = plan[PLAN + SAME_X : PLAN + SAME_X + 1, :] > 0
    out[0] = jnp.where(used, jnp.where(same, mine[0], handed[0]), before[0])


VMEM = pl.BlockSpec(memory_space=pltpu.VMEM)
SMEM = pl.BlockSpec(memory_space=pltpu.SMEM)
ANY = pl.BlockSpec(memory_space=pl.ANY)
HBM = pl.BlockSpec(memory_space=pltpu.HBM)


def real(*shape):
    return jax.ShapeDtypeStruct(shape, jnp.float32)


def whole(*shape):
    return jax.ShapeDtypeStruct(shape, jnp.int32)


def call(kernel, name, outs, ins, in_specs=None, out_specs=None, scratch=(), micros=0.1, after=(), limit=LIMIT, aliases=()):
    single = not isinstance(outs, tuple)
    shapes = (outs,) if single else outs
    result = pl.pallas_call(
        kernel,
        out_shape=shapes,
        in_specs=list(in_specs or [VMEM] * len(ins)) + [ANY] * len(after),
        out_specs=tuple(out_specs or [VMEM] * len(shapes)),
        scratch_shapes=list(scratch),
        compiler_params=pltpu.CompilerParams(vmem_limit_bytes=limit),
        cost_estimate=pl.CostEstimate(flops=0, bytes_accessed=int(micros * 3.6e6), transcendentals=0),
        input_output_aliases=dict(aliases),
        name=name,
    )(*ins, *after)
    return result[0] if single else result


def route(value, plan, way, between):
    shape = value.shape[1:]
    got = lax.ppermute(value, "arc", flips(c=1))
    held = call(stack_kernel, "stack", real(2, *shape), (value, got), after=between(0, value))
    got = lax.ppermute(held, "arc", flips(y=1))
    held = call(stack_kernel, "stack", real(4, *shape), (held, got), after=between(1, held))
    got = lax.ppermute(held, "arc", flips(y=3))
    keep, send = call(
        functools.partial(pick_kernel, way), "pick", (real(4, *shape),) * 2, (plan, held, got), after=between(2, held)
    )
    got = lax.ppermute(send, "arc", flips(z=1))
    keep, send = call(
        functools.partial(choose_kernel, way, FROM_Z), "choose", (real(2, *shape),) * 2, (plan, keep, got),
        after=between(3, send),
    )
    got = lax.ppermute(send, "arc", flips(z=3))
    keep, send = call(
        functools.partial(choose_kernel, way, FAR_Z), "choose", (real(1, *shape),) * 2, (plan, keep, got),
        after=between(4, send),
    )
    return keep, lax.ppermute(send, "arc", flips(x=1)), between(5, send)


def static_tables(arc_count, cycle_dev, roller_total):
    cycle_total = arc_count * cycle_dev
    centres = [r * (cycle_total - 1) // (roller_total - 1) for r in range(roller_total)]
    span = REACH + STEPS - 1
    near = np.full(arc_count, -1, np.int32)
    start = np.zeros(arc_count, np.int32)
    for d in range(arc_count):
        base = d * cycle_dev
        touching = [r for r, c in enumerate(centres) if base - span <= c < base + cycle_dev + span]
        assert len(touching) <= 1
        if touching:
            near[d] = touching[0]
            offset = centres[touching[0]] - base - REACH - STEPS - STEPS + 1 + HALO
            start[d] = offset // 8 * 8
            assert 0 <= start[d] <= cycle_dev + 2 * HALO - WIN
    home = np.array([c // cycle_dev for c in centres], np.int32)
    return near, start, home


def local(displacement, velocity, node_mass, wall_stiff, pad_state, roller_lift, contact_rows, roller_slot):
    cycle_dev = displacement.shape[1]
    slots = pad_state.shape[1]
    roller_total = roller_lift.shape[0]
    arc_count = lax.axis_size("arc")
    cycle_total = cycle_dev * arc_count
    half = cycle_dev // 2 + HALO
    rows = cycle_dev + 16
    fields = (displacement, velocity, node_mass, wall_stiff)
    static = np.concatenate(static_tables(arc_count, cycle_dev, roller_total)).astype(np.int32)
    swap = [(0, 1), (1, 0)]
    table = jnp.asarray(TABLE)[lax.axis_index("circ")]

    def base(me):
        return me * cycle_dev - HALO

    def buffers(count):
        return real(3, 2, count + 8, LANES), real(3, 2, count, LANES), real(4, 2, count, LANES)

    def room(count):
        return [pltpu.VMEM(shape.shape, jnp.float32) for shape in buffers(count)[:2]]

    pad_edges = call(pad_edge_kernel, "pad_edge", real(8, LANES), (pad_state,))
    pad_edges = lax.ppermute(pad_edges, "circ", swap)
    inner, outer = call(
        functools.partial(edge_kernel, HALO), "edge",
        (real(8, HALO, LANES), real(8, HALO, LANES)), fields,
        in_specs=[HBM] * 4, scratch=[pltpu.SemaphoreType.DMA((8,))], micros=2.0, limit=MOST,
    )
    plan, where, rows_in, lift = call(
        functools.partial(plan_kernel, arc_count, cycle_dev), "plan",
        (whole(2 * PLAN, LANES), whole(2), whole(STEPS, slots), real(1)),
        (roller_slot, roller_lift, contact_rows, jnp.asarray(static)),
        in_specs=[SMEM, SMEM, VMEM, SMEM], out_specs=[VMEM, SMEM, VMEM, SMEM],
        scratch=[pltpu.SMEM((arc_count,), jnp.int32)], micros=3.0,
    )

    outward = [pair for i in range(1, arc_count, 2) for pair in ((i, (i + 1) % arc_count), ((i + 1) % arc_count, i))]
    inner = lax.ppermute(inner, "arc", flips(c=1))
    outer = lax.ppermute(outer, "arc", outward)
    kept = {"done": 0}

    def load_window():
        return call(
            functools.partial(window_load_kernel, half, base, cycle_total), "window_load", buffers(WIN),
            (where, *fields, inner, outer, kept["columns"]), in_specs=[SMEM] + [VMEM] * 7, micros=0.8,
        )

    def load_bulk():
        return call(
            functools.partial(bulk_load_kernel, half, base, cycle_total, rows), "bulk_load", buffers(rows),
            (*fields, inner, outer, kept["columns"]), micros=2.0,
        )

    def step_bulk(value, count):
        for _ in range(count):
            step, part = divmod(kept["done"], PARTS)
            state, vels, coef = kept["bulk"]
            before = kept["next"] if part else ()
            kept["next"] = call(
                functools.partial(bulk_step_kernel, rows, part), "bulk_step", buffers(rows)[:2],
                (table, state, vels, coef, *before), micros=2.4 / PARTS, after=(value,),
                aliases={4: 0, 5: 1} if part else {},
            )
            kept["done"] += 1
            if part == PARTS - 1:
                kept["bulk"] = (*kept["next"], coef)
        return kept["next"][:1]

    def store_bulk(value):
        state, vels, _ = kept["bulk"]
        outs = call(
            functools.partial(bulk_store_kernel, rows), "bulk_store",
            (real(3, cycle_dev, LANES), real(3, cycle_dev, LANES), real(8, LANES)),
            (where, state, vels, kept["last"], value),
            in_specs=[SMEM] + [VMEM] * 3 + [ANY], out_specs=[HBM] * 2 + [VMEM],
            scratch=[pltpu.VMEM((6, cycle_dev, LANES), jnp.float32), pltpu.SemaphoreType.DMA((2 * CHUNKS,))],
            micros=2.0,
        )
        kept["outs"] = outs[:2]
        return outs[2:]

    def going(stage, value):
        if stage == 1:
            pack = call(pack_kernel, "pack", real(half, LANES), (*fields, inner, outer), micros=2.0, after=(value,))
            kept["columns"] = lax.ppermute(pack, "circ", swap)
            return (pack,)
        if stage == 3:
            kept["window"] = load_window()
            kept["bulk"] = load_bulk()
            return (kept["window"][0], kept["bulk"][0])
        return step_bulk(value, 3) if stage > 3 else ()

    value = call(
        pad_extend_kernel, "pad_extend", real(1, slots + 8, LANES), (pad_state, pad_edges), after=(plan,)
    )
    pads, handed, done = route(value, plan, 0, going)

    win_state, win_vels, win_coef = kept["window"]
    win_state, win_vels, push, pad_new = call(
        window_kernel, "window", (*buffers(WIN)[:2], real(2, 2, WIN, LANES), real(1, slots, LANES)),
        (rows_in, lift, plan, table, win_state, win_vels, win_coef, pads, handed),
        after=done,
        in_specs=[SMEM] * 2 + [VMEM] * 7,
        scratch=room(WIN)
        + [
            pltpu.VMEM((2, 2, slots, LANES), jnp.float32),
            pltpu.VMEM((2, 2, slots, LANES), jnp.float32),
            pltpu.VMEM((2, slots, LANES), jnp.float32),
        ],
        micros=2.0,
    )

    def coming(stage, value):
        if stage == 0:
            kept["last"] = call(
                window_last_kernel, "window_last", real(6, WIN, LANES), (table, win_state, win_vels, win_coef, push),
                scratch=room(WIN), micros=0.6,
            )
            return (kept["last"],)
        if stage == 4:
            return store_bulk(value)
        return step_bulk(value, 2) if stage < 4 else ()

    pads, handed, done = route(pad_new, plan, 1, coming)
    pad_result = call(last_kernel, "last", real(1, slots, LANES), (plan, pads, handed, pad_state), after=done)
    return *kept["outs"], pad_result


def solution(mesh):
    placed = (
        P(None, "arc", "circ"),
        P(None, "arc", "circ"),
        P("arc", "circ"),
        P("arc", "circ"),
        P("arc", None, "circ"),
        P(),
        P(),
        P(),
    )
    return jax.shard_map(
        local,
        mesh=mesh,
        in_specs=placed,
        out_specs=(P(None, "arc", "circ"), P(None, "arc", "circ"), P("arc", None, "circ")),
        check_vma=False,
    )
```

```python
import functools
import math

import jax
import jax.numpy as jnp
import numpy as np
from jax import lax
from jax.experimental import pallas as pl
from jax.experimental.pallas import tpu as pltpu
from jax.sharding import PartitionSpec as P

STEPS = 4
REACH = 20
TIME_STEP = 0.1
GRAVITY = 0.2
CONTACT_STIFF = 2.0
CRADLE_CURVE = 0.5
PAD_RATE = 0.2
PAD_STIFF = 1.0

LANES = 128
EDGE = 4
HALO = 48
WIN = 64
CHUNKS = 4
GROUP = 11
PARTS = 3
LOAD_GROUP = 4
LIMIT = 16 * 1024 * 1024
MOST = 60 * 1024 * 1024


def arc_digits(index):
    return (index >> 4, (index >> 2) & 3, (index >> 1) & 1, index & 1)


def arc_index(y, z, x, c):
    return (y << 4) + (z << 2) + (x << 1) + c


def flips(y=0, z=0, x=0, c=0):
    out = []
    for i in range(64):
        iy, iz, ix, ic = arc_digits(i)
        out.append((i, arc_index(iy ^ y, iz ^ z, ix ^ x, ic ^ c)))
    return out


def column_table(circ_total):
    step = 2.0 * math.pi / circ_total
    chord = 2.0 * math.sin(step / 2.0)
    length = math.sqrt(step * step + chord * chord)
    rows = []
    for half in range(2):
        cols = (half * LANES + np.arange(2 * LANES)) % circ_total
        phase = step * (cols + 0.5)
        before = step * (cols - 0.5)
        theta = step * cols
        parts = [
            chord / length * np.cos(phase),
            chord / length * np.sin(phase),
            chord / length * np.cos(before),
            chord / length * np.sin(before),
            np.sin(theta),
            np.cos(theta),
            np.zeros_like(theta),
            np.zeros_like(theta),
        ]
        rows.append(np.concatenate([p.reshape(2, LANES) for p in parts], axis=0))
    axial = step / length
    hoop_gain = 1.0 / (chord / length) ** 2
    return np.stack(rows).astype(np.float32), axial, hoop_gain


def edge_kernel(halo, disp, vel, mass, stiff, *rest):
    inner, outer, sems = rest[-3:]
    own = disp.shape[1]
    odd = lax.axis_index("arc") & 1
    copies = []
    for n, (edge, at) in enumerate(((inner, (1 - odd) * (own - halo)), (outer, odd * (own - halo)))):
        span = pl.ds(pl.multiple_of(at, 8), halo)
        copies += [
            pltpu.make_async_copy(disp.at[:, span, :], edge.at[0:3], sems.at[4 * n]),
            pltpu.make_async_copy(vel.at[:, span, :], edge.at[3:6], sems.at[4 * n + 1]),
            pltpu.make_async_copy(mass.at[span, :], edge.at[6], sems.at[4 * n + 2]),
            pltpu.make_async_copy(stiff.at[span, :], edge.at[7], sems.at[4 * n + 3]),
        ]
    for copy in copies:
        copy.start()
    for copy in copies:
        copy.wait()


KEEP, SEND, FROM_Z, FAR_Z, SAME_X, USED, PLAN = 0, 4, 8, 12, 14, 15, 16


def plan_kernel(
    arc_count, own, slot_ref, lift_ref, rows_ref, static_ref, *rest
):
    plan, where_ref, list_ref, lift_out, source = rest[-5:]
    me = lax.axis_index("arc")
    y, z, x, c = arc_digits(me)
    rollers = slot_ref.shape[0]
    roll = static_ref[me]
    begin = static_ref[arc_count + me]
    valid = roll >= 0
    safe = jnp.maximum(roll, 0)
    where_ref[0] = begin
    where_ref[1] = jnp.where(valid, begin, -4 * WIN)
    lift_out[0] = jnp.where(valid, lift_ref[safe], -1e9)
    offset = me * own - HALO + begin
    for step in range(STEPS):
        g = rows_ref[step, pl.ds(safe, 1), :] - offset
        list_ref[step : step + 1, :] = jnp.clip(g, 0, WIN - 1)
    for i in range(source.shape[0]):
        source[i] = -1
    for r in range(rollers):
        source[slot_ref[r]] = static_ref[2 * arc_count + r]

    def line(row, value):
        plan[row : row + 1, :] = jnp.full((1, LANES), value, jnp.int32)

    def index(need):
        ny, _, _, nc = arc_digits(need)
        step = jnp.where((ny >> 1) == (y >> 1), ny ^ y, 2 + (ny ^ y ^ 3))
        return 2 * step + (nc ^ c)

    for way in range(2):
        at = PLAN * way
        for zi in range(4):
            for xr in range(2):
                dest = arc_index(y, z ^ (0, 3, 1, 2)[zi], x ^ xr, c)
                if way == 0:
                    need = slot_ref[jnp.maximum(static_ref[dest], 0)]
                else:
                    need = jnp.maximum(source[dest], 0)
                n = 2 * zi + xr
                line(at + KEEP + n, index(need))
                _, nz, nx, _ = arc_digits(need)
                if n < 4:
                    line(at + FROM_Z + n, (nz == (z ^ 1)).astype(jnp.int32))
                if n < 2:
                    line(at + FAR_Z + n, ((nz != z) & (nz != (z ^ 1))).astype(jnp.int32))
                if n < 1:
                    line(at + SAME_X, (nx == x).astype(jnp.int32))
        line(at + USED, (source[me] >= 0).astype(jnp.int32))


def take(fields, a, span):
    disp, vel, mass, stiff = fields
    if a < 3:
        return disp[a, span, :]
    if a < 6:
        return vel[a - 3, span, :]
    return mass[span, :] if a == 6 else stiff[span, :]


def row_block(fields, inner, outer, odd, a, row):
    halo = inner.shape[1]
    own = fields[0].shape[1]
    if row < halo:
        span = slice(row, row + 8)
        return jnp.where(odd, inner[a, span, :], outer[a, span, :])
    if row < halo + own:
        return take(fields, a, slice(row - halo, row - halo + 8))
    span = slice(row - halo - own, row - halo - own + 8)
    return jnp.where(odd, outer[a, span, :], inner[a, span, :])


def pack_kernel(*refs):
    fields, inner, outer, pack = refs[:4], refs[4], refs[5], refs[-1]
    half = fields[0].shape[1] // 2 + inner.shape[1]
    odd = (lax.axis_index("arc") & 1) > 0
    lane = lax.broadcasted_iota(jnp.int32, (8, LANES), 1) // (2 * EDGE)
    for r in range(0, half, 8):
        packed = jnp.zeros((8, LANES), jnp.float32)
        for part in range(2):
            for a in range(8):
                value = row_block(fields, inner, outer, odd, a, r + part * half)
                moved = pltpu.roll(value, (8 * a + EDGE + 64 * part) % LANES, 1)
                packed = jnp.where(lane == a + 8 * part, moved, packed)
        pack[r : r + 8, :] = packed


def ring_left(tiles, last):
    a, b = (pltpu.roll(t, LANES - 1, 1) for t in tiles)
    return jnp.where(last, b, a), jnp.where(last, a, b)


def ring_right(tiles, first):
    a, b = (pltpu.roll(t, 1, 1) for t in tiles)
    return jnp.where(first, b, a), jnp.where(first, a, b)


def unpack_block(pack, row, half, a, keep):
    upper = row >= half
    at = pl.multiple_of(jnp.where(upper, row - half, row), 8)
    shift = jnp.where(upper, (2 * LANES - 8 * a - EDGE - 64) % LANES, (2 * LANES - 8 * a - EDGE) % LANES)
    return jnp.where(keep, pltpu.roll(pack[pl.ds(at, 8), :], shift, 1), 0.0)


def clear_tail(state, rows):
    for a in range(3):
        for t in range(2):
            state[a, t, rows : rows + 8, :] = jnp.zeros((8, LANES), jnp.float32)


def load_state(group, source, pack, first_row, base, cycle_total, rows, half, state, vels, coef, ends=False):
    lane = lax.broadcasted_iota(jnp.int32, (8, LANES), 1)
    sub = lax.broadcasted_iota(jnp.int32, (8, LANES), 0)
    keep = (lane < EDGE) | (lane >= LANES - EDGE)
    first = lane == 0
    top = sub == 0

    def body(b, carry):
        r = 8 * b if isinstance(b, int) else pl.multiple_of(b * 8, 8)
        e = first_row + r
        span = pl.ds(r, 8)
        for a in range(3):
            state[a, 0, span, :] = source(a, r)
            state[a, 1, span, :] = unpack_block(pack, e, half, a, keep)
            vels[a, 0, span, :] = TIME_STEP * source(3 + a, r)
            vels[a, 1, span, :] = TIME_STEP * unpack_block(pack, e, half, 3 + a, keep)
        for t, m in enumerate((source(6, r), unpack_block(pack, e, half, 6, keep))):
            coef[0, t, span, :] = (TIME_STEP * TIME_STEP) / jnp.where(m > 0.0, m, 1.0)
        ids = base + e + sub
        inside = (ids >= 0) & (ids < cycle_total - 1)
        k = [
            jnp.where(inside, v, 0.0)
            for v in (source(7, r), unpack_block(pack, e, half, 7, keep))
        ]
        kr = ring_right(k, first)
        new = []
        for t in range(2):
            down = pltpu.roll(k[t], 1, 0)
            coef[1, t, span, :] = k[t]
            coef[2, t, span, :] = 0.5 * (k[t] + kr[t])
            coef[3, t, span, :] = (0.5 * HOOP_GAIN) * (k[t] + jnp.where(top, carry[t], down))
            new.append(down)
        return tuple(new)

    zero = jnp.zeros((8, LANES), jnp.float32)

    def several(b, carry):
        for u in range(group):
            carry = body(b * group + u + int(ends), carry)
        return carry

    carry = (zero, zero)
    if ends:
        carry = body(0, carry)
    carry = lax.fori_loop(0, (rows // 8 - 2 * int(ends)) // group, several, carry)
    if ends:
        body(rows // 8 - 1, carry)
    clear_tail(state, rows)


TABLE, AXIAL, HOOP_GAIN = column_table(2 * LANES)


def advance(table, rows, state, vels, coef, later, vels_later, group, push=None, span_of=None):
    lane = lax.broadcasted_iota(jnp.int32, (8, LANES), 1)
    top = lax.broadcasted_iota(jnp.int32, (8, LANES), 0) == 0
    first, last = lane == 0, lane == LANES - 1

    def const(i):
        return [jnp.broadcast_to(table[2 * i + t : 2 * i + t + 1, :], (8, LANES)) for t in range(2)]

    cj, sj, cb, sb = (const(i) for i in range(4))
    two = range(2)

    def block(r, carry, store=True):
        span, below = pl.ds(r, 8), pl.ds(r + 1, 8)
        x, y, z = ([state[a, t, span, :] for t in two] for a in range(3))
        xn, yn, zn = ([state[a, t, below, :] for t in two] for a in range(3))
        p = [cj[t] * y[t] + sj[t] * z[t] for t in two]
        q = [cb[t] * y[t] + sb[t] * z[t] for t in two]
        ax = [AXIAL * x[t] for t in two]
        pn = [cj[t] * yn[t] + sj[t] * zn[t] for t in two]
        qn = [cb[t] * yn[t] + sb[t] * zn[t] for t in two]
        axn = [AXIAL * xn[t] for t in two]
        q_next = ring_left(q, last)
        anti_next = ring_left([q[t] - ax[t] for t in two], last)
        diag_next = ring_left([qn[t] + axn[t] for t in two], last)
        k = [coef[1, t, span, :] for t in two]
        t_d = [k[t] * (diag_next[t] - (p[t] + ax[t])) for t in two]
        t_a = [k[t] * (anti_next[t] - (pn[t] - axn[t])) for t in two]
        t_h = [coef[3, t, span, :] * (q_next[t] - p[t]) for t in two]
        fx = [coef[2, t, span, :] * (xn[t] - x[t]) for t in two]
        d_left = ring_right(t_d, first)
        a_left = ring_right(t_a, first)
        g_left = ring_right([t_a[t] + t_h[t] for t in two], first)
        new = []
        for t in two:
            up = t_d[t] + t_h[t]
            force = [
                fx[t] + AXIAL * (t_d[t] + a_left[t]),
                cj[t] * up - cb[t] * g_left[t],
                sj[t] * up - sb[t] * g_left[t],
            ]
            low = [
                fx[t] + AXIAL * (d_left[t] + t_a[t]),
                cb[t] * d_left[t] - cj[t] * t_a[t],
                sb[t] * d_left[t] - sj[t] * t_a[t],
            ]
            at = (x[t], y[t], z[t])
            inverse = coef[0, t, span, :]
            for a in range(3):
                moved = pltpu.roll(low[a], 1, 0)
                total = force[a] - jnp.where(top, carry[3 * t + a], moved)
                new.append(moved)
                if not store:
                    continue
                if push is not None and a > 0:
                    total = total + push[a - 1, t, span, :]
                w = vels[a, t, span, :] + inverse * total
                if a == 2:
                    w = w - (GRAVITY * TIME_STEP * TIME_STEP)
                vels_later[a, t, span, :] = w
                later[a, t, span, :] = at[a] + w
        return tuple(new)

    def body(b, carry):
        for u in range(group):
            carry = block(pl.multiple_of(b * (8 * group), 8) + 8 * u, carry)
        return carry

    zero = jnp.zeros((8, LANES), jnp.float32)
    carry = (zero,) * 6
    begin, end = span_of or (0, rows)
    if begin > 0:
        carry = block(begin - 8, carry, store=False)
    if group * 8 == rows:
        for u in range(group):
            carry = block(8 * u, carry)
    else:
        lax.fori_loop(begin // (8 * group), end // (8 * group), body, carry)


def pad_edge_kernel(plan, kept, got, *rest):
    out, edges = rest[-2:]
    pad = jnp.where(plan[SAME_X : SAME_X + 1, :] > 0, kept[0], got[0])
    out[...] = pad
    lane = lax.broadcasted_iota(jnp.int32, (1, LANES), 1) // (2 * EDGE)
    total = jnp.zeros((1, LANES), jnp.float32)
    slots = pad.shape[0]
    for m in range(slots):
        moved = pltpu.roll(pad[m : m + 1, :], LANES - EDGE - 2 * EDGE * m, 1)
        total = jnp.where(lane == slots - 1 - m, moved, total)
    edges[...] = jnp.broadcast_to(total, edges.shape)


def window_load_kernel(half, base, cycle_total, where_ref, *refs):
    fields, (inner, outer, columns, state, vels, coef) = refs[:4], refs[4:]
    start = pl.multiple_of(where_ref[0], 8)
    halo = inner.shape[1]
    own = fields[0].shape[1]
    odd = (lax.axis_index("arc") & 1) > 0

    def source(a, r):
        row = start + r
        mid = take(fields, a, pl.ds(pl.multiple_of(jnp.clip(row - halo, 0, own - 8), 8), 8))
        before = row < halo
        at = jnp.where(before, row, jnp.maximum(row - halo - own, 0))
        span = pl.ds(pl.multiple_of(at, 8), 8)
        end = jnp.where(odd == before, inner[a, span, :], outer[a, span, :])
        return jnp.where(before | (row >= halo + own), end, mid)

    first_id = base(lax.axis_index("arc"))
    load_state(4, source, columns, start, first_id, cycle_total, WIN, half, state, vels, coef)


def contact(table, lift, list_ref, step, state, push, taken, given, held):
    slots = held.shape[1]
    push[...] = jnp.zeros_like(push)
    for m in range(slots):
        g = list_ref[step, m]
        for a in range(2):
            for t in range(2):
                taken[a, t, m : m + 1, :] = state[a + 1, t, pl.ds(g, 1), :]
    for t in range(2):
        sin_angle, cos_angle = table[8 + t : 9 + t, :], table[10 + t : 11 + t, :]
        lateral = sin_angle + taken[0, t]
        q = held[t]
        intrusion = lift + CRADLE_CURVE * lateral * lateral - (1.0 - cos_angle) - taken[1, t] - q
        load = CONTACT_STIFF * jnp.maximum(intrusion, 0.0)
        normal = load / jnp.sqrt(1.0 + 4.0 * CRADLE_CURVE * CRADLE_CURVE * lateral * lateral)
        given[0, t] = -2.0 * CRADLE_CURVE * lateral * normal
        given[1, t] = normal
        held[t] = q + PAD_RATE * (load - PAD_STIFF * q)
    for m in range(slots):
        g = list_ref[step, m]
        for a in range(2):
            for t in range(2):
                push[a, t, pl.ds(g, 1), :] += given[a, t, m : m + 1, :]


def window_kernel(
    list_ref, lift_ref, table, state, vels, coef, pads, edges, *rest
):
    state_out, vels_out, push, pad_out, spare, vels_spare, taken, given, held = rest[-9:]
    lane = lax.broadcasted_iota(jnp.int32, (8, LANES), 1)
    keep = (lane < EDGE) | (lane >= LANES - EDGE)
    held[0] = pads[...]
    for part in range(2):
        moved = pltpu.roll(edges[...], EDGE + 64 * part, 1, stride=2 * EDGE, stride_axis=0)
        held[1, 8 * part : 8 * part + 8, :] = jnp.where(keep, moved, 0.0)
    lift = lift_ref[0]
    clear_tail(spare, WIN)
    clear_tail(state_out, WIN)
    now = (state, vels)
    for step in range(STEPS):
        contact(table, lift, list_ref, step, now[0], push, taken, given, held)
        if step < STEPS - 1:
            later = (spare, vels_spare) if (STEPS - step) % 2 else (state_out, vels_out)
            advance(table, WIN, *now, coef, *later, WIN // 8, push)
            now = later
    pad_out[0] = held[0]


def window_last_kernel(table, state, vels, coef, push, result, later, vels_later):
    advance(table, WIN, state, vels, coef, later, vels_later, WIN // 8, push)
    for a in range(3):
        result[a] = later[a, 0, :WIN, :]
        result[3 + a] = vels_later[a, 0] * (1.0 / TIME_STEP)


def bulk_load_kernel(half, base, cycle_total, rows, *refs):
    fields, (inner, outer, columns, state, vels, coef) = refs[:4], refs[4:]
    first_row = HALO - 8
    odd = (lax.axis_index("arc") & 1) > 0

    def source(a, r):
        if isinstance(r, int):
            return row_block(fields, inner, outer, odd, a, first_row + r)
        return take(fields, a, pl.ds(pl.multiple_of(r - 8, 8), 8))

    first_id = base(lax.axis_index("arc"))
    load_state(
        LOAD_GROUP, source, columns, first_row, first_id, cycle_total, rows, half, state, vels, coef, ends=True
    )


def bulk_step_kernel(rows, part, table, state, vels, coef, *rest):
    later, vels_later = rest[-2:]
    third = rows // PARTS
    advance(table, rows, state, vels, coef, later, vels_later, GROUP, span_of=(part * third, (part + 1) * third))
    if part == 0:
        clear_tail(later, rows)


def bulk_store_kernel(rows, where_ref, state, vels, window, *rest):
    disp_out, vel_out, token, result, sems = rest[-5:]
    token[...] = jnp.zeros_like(token)
    count = (rows - 16) // CHUNKS
    start = where_ref[1]
    sub = lax.broadcasted_iota(jnp.int32, (8, LANES), 0)

    def body(b, carry):
        r = pl.multiple_of(b * 8, 8)
        inner = pl.ds(pl.multiple_of(r + 8, 8), 8)
        rel = HALO + r - start
        at = pl.ds(pl.multiple_of(jnp.clip(rel, 0, WIN - 8), 8), 8)
        ids = rel + sub
        use = (ids >= STEPS) & (ids < WIN - STEPS)
        for a in range(3):
            result[a, pl.ds(r, 8), :] = jnp.where(use, window[a, at, :], state[a, 0, inner, :])
            result[3 + a, pl.ds(r, 8), :] = jnp.where(
                use, window[3 + a, at, :], vels[a, 0, inner, :] * (1.0 / TIME_STEP)
            )
        return carry

    copies = []
    for chunk in range(CHUNKS):
        lax.fori_loop(chunk * count // 8, (chunk + 1) * count // 8, body, 0)
        span = pl.ds(chunk * count, count)
        for n, out in enumerate((disp_out, vel_out)):
            copy = pltpu.make_async_copy(
                result.at[3 * n : 3 * n + 3, span, :], out.at[:, span, :], sems.at[2 * chunk + n]
            )
            copy.start()
            copies.append(copy)
    for copy in copies:
        copy.wait()


def stack_kernel(first, second, *rest):
    count = first.shape[0]
    rest[-1][:count] = first[...]
    rest[-1][count:] = second[...]


def pick_kernel(way, plan, first, second, *rest):
    keep, send = rest[-2:]
    parts = [ref[n] for ref in (first, second) for n in range(4)]
    for out, row in ((keep, KEEP), (send, SEND)):
        for n in range(4):
            at = PLAN * way + row + n
            index = plan[at : at + 1, :]
            value = parts[0]
            for m in range(1, 8):
                value = jnp.where(index == m, parts[m], value)
            out[n] = value


def choose_kernel(way, row, plan, kept, got, *rest):
    keep, send = rest[-2:]
    count = got.shape[0]
    for n in range(count):
        at = PLAN * way + row + n
        value = jnp.where(plan[at : at + 1, :] > 0, got[n], kept[n])
        if n < count // 2:
            keep[n] = value
        else:
            send[n - count // 2] = value


def last_kernel(plan, mine, handed, before, *rest):
    out = rest[-1]
    used = plan[PLAN + USED : PLAN + USED + 1, :] > 0
    same = plan[PLAN + SAME_X : PLAN + SAME_X + 1, :] > 0
    out[0] = jnp.where(used, jnp.where(same, mine[0], handed[0]), before[0])


VMEM = pl.BlockSpec(memory_space=pltpu.VMEM)
SMEM = pl.BlockSpec(memory_space=pltpu.SMEM)
ANY = pl.BlockSpec(memory_space=pl.ANY)
HBM = pl.BlockSpec(memory_space=pltpu.HBM)


def real(*shape):
    return jax.ShapeDtypeStruct(shape, jnp.float32)


def whole(*shape):
    return jax.ShapeDtypeStruct(shape, jnp.int32)


def call(kernel, name, outs, ins, in_specs=None, out_specs=None, scratch=(), micros=0.1, after=(), limit=LIMIT, aliases=()):
    single = not isinstance(outs, tuple)
    shapes = (outs,) if single else outs
    result = pl.pallas_call(
        kernel,
        out_shape=shapes,
        in_specs=list(in_specs or [VMEM] * len(ins)) + [ANY] * len(after),
        out_specs=tuple(out_specs or [VMEM] * len(shapes)),
        scratch_shapes=list(scratch),
        compiler_params=pltpu.CompilerParams(vmem_limit_bytes=limit),
        cost_estimate=pl.CostEstimate(flops=0, bytes_accessed=int(micros * 3.6e6), transcendentals=0),
        input_output_aliases=dict(aliases),
        name=name,
    )(*ins, *after)
    return result[0] if single else result


def route(value, kept, way, between):
    shape = value.shape[1:]
    got = lax.ppermute(value, "arc", flips(c=1))
    held = call(stack_kernel, "stack", real(2, *shape), (value, got), after=between(0, value))
    got = lax.ppermute(held, "arc", flips(y=1))
    held = call(stack_kernel, "stack", real(4, *shape), (held, got), after=between(1, held))
    got = lax.ppermute(held, "arc", flips(y=3))
    ready = between(2, held)
    plan = kept["plan"][0]
    keep, send = call(
        functools.partial(pick_kernel, way), "pick", (real(4, *shape),) * 2, (plan, held, got), after=ready
    )
    got = lax.ppermute(send, "arc", flips(z=1))
    keep, send = call(
        functools.partial(choose_kernel, way, FROM_Z), "choose", (real(2, *shape),) * 2, (plan, keep, got),
        after=between(3, send),
    )
    got = lax.ppermute(send, "arc", flips(z=3))
    keep, send = call(
        functools.partial(choose_kernel, way, FAR_Z), "choose", (real(1, *shape),) * 2, (plan, keep, got),
        after=between(4, send),
    )
    return keep, lax.ppermute(send, "arc", flips(x=1)), between(5, send)


def static_tables(arc_count, cycle_dev, roller_total):
    cycle_total = arc_count * cycle_dev
    centres = [r * (cycle_total - 1) // (roller_total - 1) for r in range(roller_total)]
    span = REACH + STEPS - 1
    near = np.full(arc_count, -1, np.int32)
    start = np.zeros(arc_count, np.int32)
    for d in range(arc_count):
        base = d * cycle_dev
        touching = [r for r, c in enumerate(centres) if base - span <= c < base + cycle_dev + span]
        assert len(touching) <= 1
        if touching:
            near[d] = touching[0]
            offset = centres[touching[0]] - base - REACH - STEPS - STEPS + 1 + HALO
            start[d] = offset // 8 * 8
            assert 0 <= start[d] <= cycle_dev + 2 * HALO - WIN
    home = np.array([c // cycle_dev for c in centres], np.int32)
    return near, start, home


def local(displacement, velocity, node_mass, wall_stiff, pad_state, roller_lift, contact_rows, roller_slot):
    cycle_dev = displacement.shape[1]
    slots = pad_state.shape[1]
    roller_total = roller_lift.shape[0]
    arc_count = lax.axis_size("arc")
    cycle_total = cycle_dev * arc_count
    half = cycle_dev // 2 + HALO
    rows = cycle_dev + 16
    fields = (displacement, velocity, node_mass, wall_stiff)
    static = np.concatenate(static_tables(arc_count, cycle_dev, roller_total)).astype(np.int32)
    swap = [(0, 1), (1, 0)]
    table = jnp.asarray(TABLE)[lax.axis_index("circ")]

    def base(me):
        return me * cycle_dev - HALO

    def buffers(count):
        return real(3, 2, count + 8, LANES), real(3, 2, count, LANES), real(4, 2, count, LANES)

    def room(count):
        return [pltpu.VMEM(shape.shape, jnp.float32) for shape in buffers(count)[:2]]

    outward = [pair for i in range(1, arc_count, 2) for pair in ((i, (i + 1) % arc_count), ((i + 1) % arc_count, i))]

    inner, outer = call(
        functools.partial(edge_kernel, HALO), "edge", (real(8, HALO, LANES), real(8, HALO, LANES)), fields,
        in_specs=[HBM] * 4, scratch=[pltpu.SemaphoreType.DMA((8,))], micros=2.0, limit=MOST,
    )
    ends = lax.ppermute(inner, "arc", flips(c=1)), lax.ppermute(outer, "arc", outward)

    def make_plan(value):
        kept["plan"] = call(
            functools.partial(plan_kernel, arc_count, cycle_dev), "plan",
            (whole(2 * PLAN, LANES), whole(2), whole(STEPS, slots), real(1)),
            (roller_slot, roller_lift, contact_rows, jnp.asarray(static)),
            in_specs=[SMEM, SMEM, VMEM, SMEM], out_specs=[VMEM, SMEM, VMEM, SMEM],
            scratch=[pltpu.SMEM((arc_count,), jnp.int32)], micros=1.5, after=(value,),
        )
        return kept["plan"][:1]

    kept = {"done": 0}

    def load_window():
        return call(
            functools.partial(window_load_kernel, half, base, cycle_total), "window_load", buffers(WIN),
            (kept["plan"][1], *fields, *ends, kept["columns"]), in_specs=[SMEM] + [VMEM] * 7, micros=0.8,
        )

    def load_bulk():
        return call(
            functools.partial(bulk_load_kernel, half, base, cycle_total, rows), "bulk_load", buffers(rows),
            (*fields, *ends, kept["columns"]), micros=2.0,
        )

    def step_bulk(value, count):
        for _ in range(count):
            step, part = divmod(kept["done"], PARTS)
            state, vels, coef = kept["bulk"]
            before = kept["next"] if part else ()
            kept["next"] = call(
                functools.partial(bulk_step_kernel, rows, part), "bulk_step", buffers(rows)[:2],
                (table, state, vels, coef, *before), micros=2.4 / PARTS, after=(value,),
                aliases={4: 0, 5: 1} if part else {},
            )
            kept["done"] += 1
            if part == PARTS - 1:
                kept["bulk"] = (*kept["next"], coef)
        return kept["next"][:1]

    def store_bulk(value):
        state, vels, _ = kept["bulk"]
        outs = call(
            functools.partial(bulk_store_kernel, rows), "bulk_store",
            (real(3, cycle_dev, LANES), real(3, cycle_dev, LANES), real(8, LANES)),
            (kept["plan"][1], state, vels, kept["last"], value),
            in_specs=[SMEM] + [VMEM] * 3 + [ANY], out_specs=[HBM] * 2 + [VMEM],
            scratch=[pltpu.VMEM((6, cycle_dev, LANES), jnp.float32), pltpu.SemaphoreType.DMA((2 * CHUNKS,))],
            micros=2.0,
        )
        kept["outs"] = outs[:2]
        return outs[2:]

    def going(stage, value):
        if stage == 1:
            return make_plan(value)
        if stage == 2:
            pack = call(pack_kernel, "pack", real(half, LANES), (*fields, *ends), micros=2.0, after=(value,))
            kept["columns"] = lax.ppermute(pack, "circ", swap)
            return (pack,)
        if stage == 6:
            kept["window"] = load_window()
            kept["bulk"] = load_bulk()
            return (kept["window"][0], kept["bulk"][0])
        return ()

    pads, handed, _ = route(pad_state, kept, 0, going)
    pads, edges = call(
        pad_edge_kernel, "pad_edge", (real(slots, LANES), real(8, LANES)), (kept["plan"][0], pads, handed)
    )
    done = going(6, edges)
    edges = lax.ppermute(edges, "circ", swap)

    plan, _, rows_in, lift = kept["plan"]
    win_state, win_vels, win_coef = kept["window"]
    win_state, win_vels, push, pad_new = call(
        window_kernel, "window", (*buffers(WIN)[:2], real(2, 2, WIN, LANES), real(1, slots, LANES)),
        (rows_in, lift, table, win_state, win_vels, win_coef, pads, edges),
        after=done,
        in_specs=[SMEM] * 2 + [VMEM] * 6,
        scratch=room(WIN)
        + [
            pltpu.VMEM((2, 2, slots, LANES), jnp.float32),
            pltpu.VMEM((2, 2, slots, LANES), jnp.float32),
            pltpu.VMEM((2, slots, LANES), jnp.float32),
        ],
        micros=2.0,
    )

    def coming(stage, value):
        if stage == 0:
            kept["last"] = call(
                window_last_kernel, "window_last", real(6, WIN, LANES), (table, win_state, win_vels, win_coef, push),
                scratch=room(WIN), micros=0.6,
            )
            return (kept["last"],)
        if stage == 4:
            return store_bulk(value)
        return step_bulk(value, 4) if stage < 4 else ()

    pads, handed, done = route(pad_new, kept, 1, coming)
    pad_result = call(last_kernel, "last", real(1, slots, LANES), (plan, pads, handed, pad_state), after=done)
    return *kept["outs"], pad_result


def solution(mesh):
    placed = (
        P(None, "arc", "circ"),
        P(None, "arc", "circ"),
        P("arc", "circ"),
        P("arc", "circ"),
        P("arc", None, "circ"),
        P(),
        P(),
        P(),
    )
    return jax.shard_map(
        local,
        mesh=mesh,
        in_specs=placed,
        out_specs=(P(None, "arc", "circ"), P(None, "arc", "circ"), P("arc", None, "circ")),
        check_vma=False,
    )
```

```python
import functools
import math

import jax
import jax.numpy as jnp
import numpy as np
from jax import lax
from jax.experimental import pallas as pl
from jax.experimental.pallas import tpu as pltpu
from jax.sharding import PartitionSpec as P

STEPS = 4
REACH = 20
TIME_STEP = 0.1
GRAVITY = 0.2
CONTACT_STIFF = 2.0
CRADLE_CURVE = 0.5
PAD_RATE = 0.2
PAD_STIFF = 1.0

LANES = 128
EDGE = 4
HALO = 48
WIN = 64
CHUNKS = 4
GROUP = 11
PARTS = 3
LOAD_GROUP = 4
LIMIT = 16 * 1024 * 1024
MOST = 60 * 1024 * 1024


def arc_digits(index):
    return (index >> 4, (index >> 2) & 3, (index >> 1) & 1, index & 1)


def arc_index(y, z, x, c):
    return (y << 4) + (z << 2) + (x << 1) + c


def flips(y=0, z=0, x=0, c=0):
    out = []
    for i in range(64):
        iy, iz, ix, ic = arc_digits(i)
        out.append((i, arc_index(iy ^ y, iz ^ z, ix ^ x, ic ^ c)))
    return out


def column_table(circ_total):
    step = 2.0 * math.pi / circ_total
    chord = 2.0 * math.sin(step / 2.0)
    length = math.sqrt(step * step + chord * chord)
    rows = []
    for half in range(2):
        cols = (half * LANES + np.arange(2 * LANES)) % circ_total
        phase = step * (cols + 0.5)
        before = step * (cols - 0.5)
        theta = step * cols
        parts = [
            chord / length * np.cos(phase),
            chord / length * np.sin(phase),
            chord / length * np.cos(before),
            chord / length * np.sin(before),
            np.sin(theta),
            np.cos(theta),
            np.zeros_like(theta),
            np.zeros_like(theta),
        ]
        rows.append(np.concatenate([p.reshape(2, LANES) for p in parts], axis=0))
    axial = step / length
    hoop_gain = 1.0 / (chord / length) ** 2
    return np.stack(rows).astype(np.float32), axial, hoop_gain


def edge_kernel(halo, disp, vel, mass, stiff, *rest):
    inner, outer, sems = rest[-3:]
    own = disp.shape[1]
    odd = lax.axis_index("arc") & 1
    copies = []
    for n, (edge, at) in enumerate(((inner, (1 - odd) * (own - halo)), (outer, odd * (own - halo)))):
        span = pl.ds(pl.multiple_of(at, 8), halo)
        copies += [
            pltpu.make_async_copy(disp.at[:, span, :], edge.at[0:3], sems.at[4 * n]),
            pltpu.make_async_copy(vel.at[:, span, :], edge.at[3:6], sems.at[4 * n + 1]),
            pltpu.make_async_copy(mass.at[span, :], edge.at[6], sems.at[4 * n + 2]),
            pltpu.make_async_copy(stiff.at[span, :], edge.at[7], sems.at[4 * n + 3]),
        ]
    for copy in copies:
        copy.start()
    for copy in copies:
        copy.wait()


KEEP, SEND, FROM_Z, FAR_Z, SAME_X, USED, PLAN = 0, 4, 8, 12, 14, 15, 16


def plan_kernel(
    arc_count, own, slot_ref, lift_ref, rows_ref, static_ref, *rest
):
    plan, where_ref, list_ref, lift_out, source = rest[-5:]
    me = lax.axis_index("arc")
    y, z, x, c = arc_digits(me)
    rollers = slot_ref.shape[0]
    roll = static_ref[me]
    begin = static_ref[arc_count + me]
    valid = roll >= 0
    safe = jnp.maximum(roll, 0)
    where_ref[0] = begin
    where_ref[1] = jnp.where(valid, begin, -4 * WIN)
    lift_out[0] = jnp.where(valid, lift_ref[safe], -1e9)
    offset = me * own - HALO + begin
    for step in range(STEPS):
        g = rows_ref[step, pl.ds(safe, 1), :] - offset
        list_ref[step : step + 1, :] = jnp.clip(g, 0, WIN - 1)
    for i in range(source.shape[0]):
        source[i] = -1
    for r in range(rollers):
        source[slot_ref[r]] = static_ref[2 * arc_count + r]

    def line(row, value):
        plan[row : row + 1, :] = jnp.full((1, LANES), value, jnp.int32)

    def index(need):
        ny, _, _, nc = arc_digits(need)
        step = jnp.where((ny >> 1) == (y >> 1), ny ^ y, 2 + (ny ^ y ^ 3))
        return 2 * step + (nc ^ c)

    for way in range(2):
        at = PLAN * way
        for zi in range(4):
            for xr in range(2):
                dest = arc_index(y, z ^ (0, 3, 1, 2)[zi], x ^ xr, c)
                if way == 0:
                    need = slot_ref[jnp.maximum(static_ref[dest], 0)]
                else:
                    need = jnp.maximum(source[dest], 0)
                n = 2 * zi + xr
                line(at + KEEP + n, index(need))
                _, nz, nx, _ = arc_digits(need)
                if n < 4:
                    line(at + FROM_Z + n, (nz == (z ^ 1)).astype(jnp.int32))
                if n < 2:
                    line(at + FAR_Z + n, ((nz != z) & (nz != (z ^ 1))).astype(jnp.int32))
                if n < 1:
                    line(at + SAME_X, (nx == x).astype(jnp.int32))
        line(at + USED, (source[me] >= 0).astype(jnp.int32))


def take(fields, a, span):
    disp, vel, mass, stiff = fields
    if a < 3:
        return disp[a, span, :]
    if a < 6:
        return vel[a - 3, span, :]
    return mass[span, :] if a == 6 else stiff[span, :]


def row_block(fields, inner, outer, odd, a, row):
    halo = inner.shape[1]
    own = fields[0].shape[1]
    if row < halo:
        span = slice(row, row + 8)
        return jnp.where(odd, inner[a, span, :], outer[a, span, :])
    if row < halo + own:
        return take(fields, a, slice(row - halo, row - halo + 8))
    span = slice(row - halo - own, row - halo - own + 8)
    return jnp.where(odd, outer[a, span, :], inner[a, span, :])


def pack_kernel(*refs):
    fields, inner, outer, pack = refs[:4], refs[4], refs[5], refs[-1]
    half = fields[0].shape[1] // 2 + inner.shape[1]
    odd = (lax.axis_index("arc") & 1) > 0
    lane = lax.broadcasted_iota(jnp.int32, (8, LANES), 1) // (2 * EDGE)
    for r in range(0, half, 8):
        packed = jnp.zeros((8, LANES), jnp.float32)
        for part in range(2):
            for a in range(8):
                value = row_block(fields, inner, outer, odd, a, r + part * half)
                moved = pltpu.roll(value, (8 * a + EDGE + 64 * part) % LANES, 1)
                packed = jnp.where(lane == a + 8 * part, moved, packed)
        pack[r : r + 8, :] = packed


def ring_left(tiles, last):
    a, b = (pltpu.roll(t, LANES - 1, 1) for t in tiles)
    return jnp.where(last, b, a), jnp.where(last, a, b)


def ring_right(tiles, first):
    a, b = (pltpu.roll(t, 1, 1) for t in tiles)
    return jnp.where(first, b, a), jnp.where(first, a, b)


def unpack_block(pack, row, half, a, keep):
    upper = row >= half
    at = pl.multiple_of(jnp.where(upper, row - half, row), 8)
    shift = jnp.where(upper, (2 * LANES - 8 * a - EDGE - 64) % LANES, (2 * LANES - 8 * a - EDGE) % LANES)
    return jnp.where(keep, pltpu.roll(pack[pl.ds(at, 8), :], shift, 1), 0.0)


def clear_tail(state, rows):
    for a in range(3):
        for t in range(2):
            state[a, t, rows : rows + 8, :] = jnp.zeros((8, LANES), jnp.float32)


def load_state(group, source, pack, first_row, base, cycle_total, rows, half, state, vels, coef, ends=False):
    lane = lax.broadcasted_iota(jnp.int32, (8, LANES), 1)
    sub = lax.broadcasted_iota(jnp.int32, (8, LANES), 0)
    keep = (lane < EDGE) | (lane >= LANES - EDGE)
    first = lane == 0
    top = sub == 0

    def body(b, carry):
        r = 8 * b if isinstance(b, int) else pl.multiple_of(b * 8, 8)
        e = first_row + r
        span = pl.ds(r, 8)
        for a in range(3):
            state[a, 0, span, :] = source(a, r)
            state[a, 1, span, :] = unpack_block(pack, e, half, a, keep)
            vels[a, 0, span, :] = TIME_STEP * source(3 + a, r)
            vels[a, 1, span, :] = TIME_STEP * unpack_block(pack, e, half, 3 + a, keep)
        for t, m in enumerate((source(6, r), unpack_block(pack, e, half, 6, keep))):
            coef[0, t, span, :] = (TIME_STEP * TIME_STEP) / jnp.where(m > 0.0, m, 1.0)
        ids = base + e + sub
        inside = (ids >= 0) & (ids < cycle_total - 1)
        k = [
            jnp.where(inside, v, 0.0)
            for v in (source(7, r), unpack_block(pack, e, half, 7, keep))
        ]
        kr = ring_right(k, first)
        new = []
        for t in range(2):
            down = pltpu.roll(k[t], 1, 0)
            coef[1, t, span, :] = k[t]
            coef[2, t, span, :] = 0.5 * (k[t] + kr[t])
            coef[3, t, span, :] = (0.5 * HOOP_GAIN) * (k[t] + jnp.where(top, carry[t], down))
            new.append(down)
        return tuple(new)

    zero = jnp.zeros((8, LANES), jnp.float32)

    def several(b, carry):
        for u in range(group):
            carry = body(b * group + u + int(ends), carry)
        return carry

    carry = (zero, zero)
    if ends:
        carry = body(0, carry)
    carry = lax.fori_loop(0, (rows // 8 - 2 * int(ends)) // group, several, carry)
    if ends:
        body(rows // 8 - 1, carry)
    clear_tail(state, rows)


TABLE, AXIAL, HOOP_GAIN = column_table(2 * LANES)


def advance(table, rows, state, vels, coef, later, vels_later, group, push=None, span_of=None):
    lane = lax.broadcasted_iota(jnp.int32, (8, LANES), 1)
    top = lax.broadcasted_iota(jnp.int32, (8, LANES), 0) == 0
    first, last = lane == 0, lane == LANES - 1

    def const(i):
        return [jnp.broadcast_to(table[2 * i + t : 2 * i + t + 1, :], (8, LANES)) for t in range(2)]

    cj, sj, cb, sb = (const(i) for i in range(4))
    two = range(2)

    def block(r, carry, store=True):
        span, below = pl.ds(r, 8), pl.ds(r + 1, 8)
        x, y, z = ([state[a, t, span, :] for t in two] for a in range(3))
        xn, yn, zn = ([state[a, t, below, :] for t in two] for a in range(3))
        p = [cj[t] * y[t] + sj[t] * z[t] for t in two]
        q = [cb[t] * y[t] + sb[t] * z[t] for t in two]
        ax = [AXIAL * x[t] for t in two]
        pn = [cj[t] * yn[t] + sj[t] * zn[t] for t in two]
        qn = [cb[t] * yn[t] + sb[t] * zn[t] for t in two]
        axn = [AXIAL * xn[t] for t in two]
        q_next = ring_left(q, last)
        anti_next = ring_left([q[t] - ax[t] for t in two], last)
        diag_next = ring_left([qn[t] + axn[t] for t in two], last)
        k = [coef[1, t, span, :] for t in two]
        t_d = [k[t] * (diag_next[t] - (p[t] + ax[t])) for t in two]
        t_a = [k[t] * (anti_next[t] - (pn[t] - axn[t])) for t in two]
        t_h = [coef[3, t, span, :] * (q_next[t] - p[t]) for t in two]
        fx = [coef[2, t, span, :] * (xn[t] - x[t]) for t in two]
        d_left = ring_right(t_d, first)
        a_left = ring_right(t_a, first)
        g_left = ring_right([t_a[t] + t_h[t] for t in two], first)
        new = []
        for t in two:
            up = t_d[t] + t_h[t]
            force = [
                fx[t] + AXIAL * (t_d[t] + a_left[t]),
                cj[t] * up - cb[t] * g_left[t],
                sj[t] * up - sb[t] * g_left[t],
            ]
            low = [
                fx[t] + AXIAL * (d_left[t] + t_a[t]),
                cb[t] * d_left[t] - cj[t] * t_a[t],
                sb[t] * d_left[t] - sj[t] * t_a[t],
            ]
            at = (x[t], y[t], z[t])
            inverse = coef[0, t, span, :]
            for a in range(3):
                moved = pltpu.roll(low[a], 1, 0)
                total = force[a] - jnp.where(top, carry[3 * t + a], moved)
                new.append(moved)
                if not store:
                    continue
                if push is not None and a > 0:
                    total = total + push[a - 1, t, span, :]
                w = vels[a, t, span, :] + inverse * total
                if a == 2:
                    w = w - (GRAVITY * TIME_STEP * TIME_STEP)
                vels_later[a, t, span, :] = w
                later[a, t, span, :] = at[a] + w
        return tuple(new)

    def body(b, carry):
        for u in range(group):
            carry = block(pl.multiple_of(b * (8 * group), 8) + 8 * u, carry)
        return carry

    zero = jnp.zeros((8, LANES), jnp.float32)
    carry = (zero,) * 6
    begin, end = span_of or (0, rows)
    if begin > 0:
        carry = block(begin - 8, carry, store=False)
    if group * 8 == rows:
        for u in range(group):
            carry = block(8 * u, carry)
    else:
        lax.fori_loop(begin // (8 * group), end // (8 * group), body, carry)


def window_load_kernel(half, base, cycle_total, where_ref, *refs):
    fields, (inner, outer, columns, state, vels, coef) = refs[:4], refs[4:]
    start = pl.multiple_of(where_ref[0], 8)
    halo = inner.shape[1]
    own = fields[0].shape[1]
    odd = (lax.axis_index("arc") & 1) > 0

    def source(a, r):
        row = start + r
        mid = take(fields, a, pl.ds(pl.multiple_of(jnp.clip(row - halo, 0, own - 8), 8), 8))
        before = row < halo
        at = jnp.where(before, row, jnp.maximum(row - halo - own, 0))
        span = pl.ds(pl.multiple_of(at, 8), 8)
        end = jnp.where(odd == before, inner[a, span, :], outer[a, span, :])
        return jnp.where(before | (row >= halo + own), end, mid)

    first_id = base(lax.axis_index("arc"))
    load_state(4, source, columns, start, first_id, cycle_total, WIN, half, state, vels, coef)


def contact(table, lift, list_ref, step, state, push, taken, given, held):
    slots = held.shape[1]
    push[...] = jnp.zeros_like(push)
    for m in range(slots):
        g = list_ref[step, m]
        for a in range(2):
            for t in range(2):
                taken[a, t, m : m + 1, :] = state[a + 1, t, pl.ds(g, 1), :]
    for t in range(2):
        sin_angle, cos_angle = table[8 + t : 9 + t, :], table[10 + t : 11 + t, :]
        lateral = sin_angle + taken[0, t]
        q = held[t]
        intrusion = lift + CRADLE_CURVE * lateral * lateral - (1.0 - cos_angle) - taken[1, t] - q
        load = CONTACT_STIFF * jnp.maximum(intrusion, 0.0)
        normal = load / jnp.sqrt(1.0 + 4.0 * CRADLE_CURVE * CRADLE_CURVE * lateral * lateral)
        given[0, t] = -2.0 * CRADLE_CURVE * lateral * normal
        given[1, t] = normal
        held[t] = q + PAD_RATE * (load - PAD_STIFF * q)
    for m in range(slots):
        g = list_ref[step, m]
        for a in range(2):
            for t in range(2):
                push[a, t, pl.ds(g, 1), :] += given[a, t, m : m + 1, :]


def window_kernel(
    list_ref, lift_ref, plan, table, state, vels, coef, kept, near, far, cross, *rest
):
    state_out, vels_out, push, pad_out, spare, vels_spare, taken, given, held = rest[-9:]
    same = plan[SAME_X : SAME_X + 1, :] > 0
    held[0] = jnp.where(same, kept[0], near[0])
    held[1] = jnp.where(same, far[0], cross[0])
    lift = lift_ref[0]
    clear_tail(spare, WIN)
    clear_tail(state_out, WIN)
    now = (state, vels)
    for step in range(STEPS):
        contact(table, lift, list_ref, step, now[0], push, taken, given, held)
        if step < STEPS - 1:
            later = (spare, vels_spare) if (STEPS - step) % 2 else (state_out, vels_out)
            advance(table, WIN, *now, coef, *later, WIN // 8, push)
            now = later
    pad_out[0] = held[0]


def window_last_kernel(table, state, vels, coef, push, result, later, vels_later):
    advance(table, WIN, state, vels, coef, later, vels_later, WIN // 8, push)
    for a in range(3):
        result[a] = later[a, 0, :WIN, :]
        result[3 + a] = vels_later[a, 0] * (1.0 / TIME_STEP)


def bulk_load_kernel(half, base, cycle_total, rows, *refs):
    fields, (inner, outer, columns, state, vels, coef) = refs[:4], refs[4:]
    first_row = HALO - 8
    odd = (lax.axis_index("arc") & 1) > 0

    def source(a, r):
        if isinstance(r, int):
            return row_block(fields, inner, outer, odd, a, first_row + r)
        return take(fields, a, pl.ds(pl.multiple_of(r - 8, 8), 8))

    first_id = base(lax.axis_index("arc"))
    load_state(
        LOAD_GROUP, source, columns, first_row, first_id, cycle_total, rows, half, state, vels, coef, ends=True
    )


def bulk_step_kernel(rows, part, table, state, vels, coef, *rest):
    later, vels_later = rest[-2:]
    third = rows // PARTS
    advance(table, rows, state, vels, coef, later, vels_later, GROUP, span_of=(part * third, (part + 1) * third))
    if part == 0:
        clear_tail(later, rows)


def bulk_store_kernel(rows, where_ref, state, vels, window, *rest):
    disp_out, vel_out, token, result, sems = rest[-5:]
    token[...] = jnp.zeros_like(token)
    count = (rows - 16) // CHUNKS
    start = where_ref[1]
    sub = lax.broadcasted_iota(jnp.int32, (8, LANES), 0)

    def body(b, carry):
        r = pl.multiple_of(b * 8, 8)
        inner = pl.ds(pl.multiple_of(r + 8, 8), 8)
        rel = HALO + r - start
        at = pl.ds(pl.multiple_of(jnp.clip(rel, 0, WIN - 8), 8), 8)
        ids = rel + sub
        use = (ids >= STEPS) & (ids < WIN - STEPS)
        for a in range(3):
            result[a, pl.ds(r, 8), :] = jnp.where(use, window[a, at, :], state[a, 0, inner, :])
            result[3 + a, pl.ds(r, 8), :] = jnp.where(
                use, window[3 + a, at, :], vels[a, 0, inner, :] * (1.0 / TIME_STEP)
            )
        return carry

    copies = []
    for chunk in range(CHUNKS):
        lax.fori_loop(chunk * count // 8, (chunk + 1) * count // 8, body, 0)
        span = pl.ds(chunk * count, count)
        for n, out in enumerate((disp_out, vel_out)):
            copy = pltpu.make_async_copy(
                result.at[3 * n : 3 * n + 3, span, :], out.at[:, span, :], sems.at[2 * chunk + n]
            )
            copy.start()
            copies.append(copy)
    for copy in copies:
        copy.wait()


def stack_kernel(first, second, *rest):
    count = first.shape[0]
    rest[-1][:count] = first[...]
    rest[-1][count:] = second[...]


def pick_kernel(way, plan, first, second, *rest):
    keep, send = rest[-2:]
    parts = [ref[n] for ref in (first, second) for n in range(4)]
    for out, row in ((keep, KEEP), (send, SEND)):
        for n in range(4):
            at = PLAN * way + row + n
            index = plan[at : at + 1, :]
            value = parts[0]
            for m in range(1, 8):
                value = jnp.where(index == m, parts[m], value)
            out[n] = value


def choose_kernel(way, row, plan, kept, got, *rest):
    keep, send = rest[-2:]
    count = got.shape[0]
    for n in range(count):
        at = PLAN * way + row + n
        value = jnp.where(plan[at : at + 1, :] > 0, got[n], kept[n])
        if n < count // 2:
            keep[n] = value
        else:
            send[n - count // 2] = value


def last_kernel(plan, mine, handed, before, *rest):
    out = rest[-1]
    used = plan[PLAN + USED : PLAN + USED + 1, :] > 0
    same = plan[PLAN + SAME_X : PLAN + SAME_X + 1, :] > 0
    out[0] = jnp.where(used, jnp.where(same, mine[0], handed[0]), before[0])


VMEM = pl.BlockSpec(memory_space=pltpu.VMEM)
SMEM = pl.BlockSpec(memory_space=pltpu.SMEM)
ANY = pl.BlockSpec(memory_space=pl.ANY)
HBM = pl.BlockSpec(memory_space=pltpu.HBM)


def real(*shape):
    return jax.ShapeDtypeStruct(shape, jnp.float32)


def whole(*shape):
    return jax.ShapeDtypeStruct(shape, jnp.int32)


def call(kernel, name, outs, ins, in_specs=None, out_specs=None, scratch=(), micros=0.1, after=(), limit=LIMIT, aliases=()):
    single = not isinstance(outs, tuple)
    shapes = (outs,) if single else outs
    result = pl.pallas_call(
        kernel,
        out_shape=shapes,
        in_specs=list(in_specs or [VMEM] * len(ins)) + [ANY] * len(after),
        out_specs=tuple(out_specs or [VMEM] * len(shapes)),
        scratch_shapes=list(scratch),
        compiler_params=pltpu.CompilerParams(vmem_limit_bytes=limit),
        cost_estimate=pl.CostEstimate(flops=0, bytes_accessed=int(micros * 3.6e6), transcendentals=0),
        input_output_aliases=dict(aliases),
        name=name,
    )(*ins, *after)
    return result[0] if single else result


def route(value, kept, way, between):
    shape = value.shape[1:]
    got = lax.ppermute(value, "arc", flips(c=1))
    held = call(stack_kernel, "stack", real(2, *shape), (value, got), after=between(0, value))
    got = lax.ppermute(held, "arc", flips(y=1))
    held = call(stack_kernel, "stack", real(4, *shape), (held, got), after=between(1, held))
    got = lax.ppermute(held, "arc", flips(y=3))
    ready = between(2, held)
    plan = kept["plan"][0]
    keep, send = call(
        functools.partial(pick_kernel, way), "pick", (real(4, *shape),) * 2, (plan, held, got), after=ready
    )
    got = lax.ppermute(send, "arc", flips(z=1))
    keep, send = call(
        functools.partial(choose_kernel, way, FROM_Z), "choose", (real(2, *shape),) * 2, (plan, keep, got),
        after=between(3, send),
    )
    got = lax.ppermute(send, "arc", flips(z=3))
    keep, send = call(
        functools.partial(choose_kernel, way, FAR_Z), "choose", (real(1, *shape),) * 2, (plan, keep, got),
        after=between(4, send),
    )
    return keep, lax.ppermute(send, "arc", flips(x=1)), between(5, send), send


def static_tables(arc_count, cycle_dev, roller_total):
    cycle_total = arc_count * cycle_dev
    centres = [r * (cycle_total - 1) // (roller_total - 1) for r in range(roller_total)]
    span = REACH + STEPS - 1
    near = np.full(arc_count, -1, np.int32)
    start = np.zeros(arc_count, np.int32)
    for d in range(arc_count):
        base = d * cycle_dev
        touching = [r for r, c in enumerate(centres) if base - span <= c < base + cycle_dev + span]
        assert len(touching) <= 1
        if touching:
            near[d] = touching[0]
            offset = centres[touching[0]] - base - REACH - STEPS - STEPS + 1 + HALO
            start[d] = offset // 8 * 8
            assert 0 <= start[d] <= cycle_dev + 2 * HALO - WIN
    home = np.array([c // cycle_dev for c in centres], np.int32)
    return near, start, home


def local(displacement, velocity, node_mass, wall_stiff, pad_state, roller_lift, contact_rows, roller_slot):
    cycle_dev = displacement.shape[1]
    slots = pad_state.shape[1]
    roller_total = roller_lift.shape[0]
    arc_count = lax.axis_size("arc")
    cycle_total = cycle_dev * arc_count
    half = cycle_dev // 2 + HALO
    rows = cycle_dev + 16
    fields = (displacement, velocity, node_mass, wall_stiff)
    static = np.concatenate(static_tables(arc_count, cycle_dev, roller_total)).astype(np.int32)
    swap = [(0, 1), (1, 0)]
    table = jnp.asarray(TABLE)[lax.axis_index("circ")]

    def base(me):
        return me * cycle_dev - HALO

    def buffers(count):
        return real(3, 2, count + 8, LANES), real(3, 2, count, LANES), real(4, 2, count, LANES)

    def room(count):
        return [pltpu.VMEM(shape.shape, jnp.float32) for shape in buffers(count)[:2]]

    outward = [pair for i in range(1, arc_count, 2) for pair in ((i, (i + 1) % arc_count), ((i + 1) % arc_count, i))]

    inner, outer = call(
        functools.partial(edge_kernel, HALO), "edge", (real(8, HALO, LANES), real(8, HALO, LANES)), fields,
        in_specs=[HBM] * 4, scratch=[pltpu.SemaphoreType.DMA((8,))], micros=2.0, limit=MOST,
    )
    ends = lax.ppermute(inner, "arc", flips(c=1)), lax.ppermute(outer, "arc", outward)

    def make_plan(value):
        kept["plan"] = call(
            functools.partial(plan_kernel, arc_count, cycle_dev), "plan",
            (whole(2 * PLAN, LANES), whole(2), whole(STEPS, slots), real(1)),
            (roller_slot, roller_lift, contact_rows, jnp.asarray(static)),
            in_specs=[SMEM, SMEM, VMEM, SMEM], out_specs=[VMEM, SMEM, VMEM, SMEM],
            scratch=[pltpu.SMEM((arc_count,), jnp.int32)], micros=1.5, after=(value,),
        )
        return kept["plan"][:1]

    kept = {"done": 0}

    def load_window():
        return call(
            functools.partial(window_load_kernel, half, base, cycle_total), "window_load", buffers(WIN),
            (kept["plan"][1], *fields, *ends, kept["columns"]), in_specs=[SMEM] + [VMEM] * 7, micros=0.8,
        )

    def load_bulk():
        return call(
            functools.partial(bulk_load_kernel, half, base, cycle_total, rows), "bulk_load", buffers(rows),
            (*fields, *ends, kept["columns"]), micros=2.0,
        )

    def step_bulk(value, count):
        for _ in range(count):
            step, part = divmod(kept["done"], PARTS)
            state, vels, coef = kept["bulk"]
            before = kept["next"] if part else ()
            kept["next"] = call(
                functools.partial(bulk_step_kernel, rows, part), "bulk_step", buffers(rows)[:2],
                (table, state, vels, coef, *before), micros=2.4 / PARTS, after=(value,),
                aliases={4: 0, 5: 1} if part else {},
            )
            kept["done"] += 1
            if part == PARTS - 1:
                kept["bulk"] = (*kept["next"], coef)
        return kept["next"][:1]

    def store_bulk(value):
        state, vels, _ = kept["bulk"]
        outs = call(
            functools.partial(bulk_store_kernel, rows), "bulk_store",
            (real(3, cycle_dev, LANES), real(3, cycle_dev, LANES), real(8, LANES)),
            (kept["plan"][1], state, vels, kept["last"], value),
            in_specs=[SMEM] + [VMEM] * 3 + [ANY], out_specs=[HBM] * 2 + [VMEM],
            scratch=[pltpu.VMEM((6, cycle_dev, LANES), jnp.float32), pltpu.SemaphoreType.DMA((2 * CHUNKS,))],
            micros=2.0,
        )
        kept["outs"] = outs[:2]
        return outs[2:]

    def going(stage, value):
        if stage == 1:
            return make_plan(value)
        if stage == 2:
            pack = call(pack_kernel, "pack", real(half, LANES), (*fields, *ends), micros=2.0, after=(value,))
            kept["columns"] = lax.ppermute(pack, "circ", swap)
            return (pack,)
        if stage == 5:
            kept["window"] = load_window()
            kept["bulk"] = load_bulk()
            return (kept["window"][0], kept["bulk"][0])
        return ()

    mine, near, done, sent = route(pad_state, kept, 0, going)
    double = [(2 * s + h, 2 * d + 1 - h) for s, d in flips(x=1) for h in range(2)]
    far = lax.ppermute(mine, "circ", swap)
    cross = lax.ppermute(sent, ("arc", "circ"), double)

    plan, _, rows_in, lift = kept["plan"]
    win_state, win_vels, win_coef = kept["window"]
    win_state, win_vels, push, pad_new = call(
        window_kernel, "window", (*buffers(WIN)[:2], real(2, 2, WIN, LANES), real(1, slots, LANES)),
        (rows_in, lift, plan, table, win_state, win_vels, win_coef, mine, near, far, cross),
        after=done,
        in_specs=[SMEM] * 2 + [VMEM] * 9,
        scratch=room(WIN)
        + [
            pltpu.VMEM((2, 2, slots, LANES), jnp.float32),
            pltpu.VMEM((2, 2, slots, LANES), jnp.float32),
            pltpu.VMEM((2, slots, LANES), jnp.float32),
        ],
        micros=2.0,
    )

    def coming(stage, value):
        if stage == 0:
            kept["last"] = call(
                window_last_kernel, "window_last", real(6, WIN, LANES), (table, win_state, win_vels, win_coef, push),
                scratch=room(WIN), micros=0.6,
            )
            return (kept["last"],)
        if stage == 4:
            return store_bulk(value)
        return step_bulk(value, 4) if stage < 4 else ()

    pads, handed, done, _ = route(pad_new, kept, 1, coming)
    pad_result = call(last_kernel, "last", real(1, slots, LANES), (plan, pads, handed, pad_state), after=done)
    return *kept["outs"], pad_result


def solution(mesh):
    placed = (
        P(None, "arc", "circ"),
        P(None, "arc", "circ"),
        P("arc", "circ"),
        P("arc", "circ"),
        P("arc", None, "circ"),
        P(),
        P(),
        P(),
    )
    return jax.shard_map(
        local,
        mesh=mesh,
        in_specs=placed,
        out_specs=(P(None, "arc", "circ"), P(None, "arc", "circ"), P("arc", None, "circ")),
        check_vma=False,
    )
```

```python
import functools
import math

import jax
import jax.numpy as jnp
import numpy as np
from jax import lax
from jax.experimental import pallas as pl
from jax.experimental.pallas import tpu as pltpu
from jax.sharding import PartitionSpec as P

STEPS = 4
REACH = 20
TIME_STEP = 0.1
GRAVITY = 0.2
CONTACT_STIFF = 2.0
CRADLE_CURVE = 0.5
PAD_RATE = 0.2
PAD_STIFF = 1.0

LANES = 128
EDGE = 4
HALO = 48
WIN = 64
CHUNKS = 4
GROUP = 11
PARTS = 3
LOAD_GROUP = 4
LIMIT = 16 * 1024 * 1024
MOST = 60 * 1024 * 1024


def arc_digits(index):
    return (index >> 4, (index >> 2) & 3, (index >> 1) & 1, index & 1)


def arc_index(y, z, x, c):
    return (y << 4) + (z << 2) + (x << 1) + c


def flips(y=0, z=0, x=0, c=0):
    out = []
    for i in range(64):
        iy, iz, ix, ic = arc_digits(i)
        out.append((i, arc_index(iy ^ y, iz ^ z, ix ^ x, ic ^ c)))
    return out


def column_table(circ_total):
    step = 2.0 * math.pi / circ_total
    chord = 2.0 * math.sin(step / 2.0)
    length = math.sqrt(step * step + chord * chord)
    rows = []
    for half in range(2):
        cols = (half * LANES + np.arange(2 * LANES)) % circ_total
        phase = step * (cols + 0.5)
        before = step * (cols - 0.5)
        theta = step * cols
        parts = [
            chord / length * np.cos(phase),
            chord / length * np.sin(phase),
            chord / length * np.cos(before),
            chord / length * np.sin(before),
            np.sin(theta),
            np.cos(theta),
            np.zeros_like(theta),
            np.zeros_like(theta),
        ]
        rows.append(np.concatenate([p.reshape(2, LANES) for p in parts], axis=0))
    axial = step / length
    hoop_gain = 1.0 / (chord / length) ** 2
    return np.stack(rows).astype(np.float32), axial, hoop_gain


def edge_kernel(halo, disp, vel, mass, stiff, *rest):
    inner, outer, sems = rest[-3:]
    own = disp.shape[1]
    odd = lax.axis_index("arc") & 1
    copies = []
    for n, (edge, at) in enumerate(((inner, (1 - odd) * (own - halo)), (outer, odd * (own - halo)))):
        span = pl.ds(pl.multiple_of(at, 8), halo)
        copies += [
            pltpu.make_async_copy(disp.at[:, span, :], edge.at[0:3], sems.at[4 * n]),
            pltpu.make_async_copy(vel.at[:, span, :], edge.at[3:6], sems.at[4 * n + 1]),
            pltpu.make_async_copy(mass.at[span, :], edge.at[6], sems.at[4 * n + 2]),
            pltpu.make_async_copy(stiff.at[span, :], edge.at[7], sems.at[4 * n + 3]),
        ]
    for copy in copies:
        copy.start()
    for copy in copies:
        copy.wait()


KEEP, SEND, FROM_Z, FAR_Z, SAME_X, USED, PLAN = 0, 4, 8, 12, 14, 15, 16


def plan_kernel(
    arc_count, own, slot_ref, lift_ref, rows_ref, static_ref, *rest
):
    plan, where_ref, list_ref, lift_out, source = rest[-5:]
    me = lax.axis_index("arc")
    y, z, x, c = arc_digits(me)
    rollers = slot_ref.shape[0]
    roll = static_ref[me]
    begin = static_ref[arc_count + me]
    valid = roll >= 0
    safe = jnp.maximum(roll, 0)
    where_ref[0] = begin
    where_ref[1] = jnp.where(valid, begin, -4 * WIN)
    lift_out[0] = jnp.where(valid, lift_ref[safe], -1e9)
    offset = me * own - HALO + begin
    for step in range(STEPS):
        g = rows_ref[step, pl.ds(safe, 1), :] - offset
        list_ref[step : step + 1, :] = jnp.clip(g, 0, WIN - 1)
    for i in range(source.shape[0]):
        source[i] = -1
    for r in range(rollers):
        source[slot_ref[r]] = static_ref[2 * arc_count + r]

    def line(row, value):
        plan[row : row + 1, :] = jnp.full((1, LANES), value, jnp.int32)

    def index(need):
        ny, _, _, nc = arc_digits(need)
        step = jnp.where((ny >> 1) == (y >> 1), ny ^ y, 2 + (ny ^ y ^ 3))
        return 2 * step + (nc ^ c)

    for way in range(2):
        at = PLAN * way
        for zi in range(4):
            for xr in range(2):
                dest = arc_index(y, z ^ (0, 3, 1, 2)[zi], x ^ xr, c)
                if way == 0:
                    need = slot_ref[jnp.maximum(static_ref[dest], 0)]
                else:
                    need = jnp.maximum(source[dest], 0)
                n = 2 * zi + xr
                line(at + KEEP + n, index(need))
                _, nz, nx, _ = arc_digits(need)
                if n < 4:
                    line(at + FROM_Z + n, (nz == (z ^ 1)).astype(jnp.int32))
                if n < 2:
                    line(at + FAR_Z + n, ((nz != z) & (nz != (z ^ 1))).astype(jnp.int32))
                if n < 1:
                    line(at + SAME_X, (nx == x).astype(jnp.int32))
        line(at + USED, (source[me] >= 0).astype(jnp.int32))


def take(fields, a, span):
    disp, vel, mass, stiff = fields
    if a < 3:
        return disp[a, span, :]
    if a < 6:
        return vel[a - 3, span, :]
    return mass[span, :] if a == 6 else stiff[span, :]


def row_block(fields, inner, outer, odd, a, row):
    halo = inner.shape[1]
    own = fields[0].shape[1]
    if row < halo:
        span = slice(row, row + 8)
        return jnp.where(odd, inner[a, span, :], outer[a, span, :])
    if row < halo + own:
        return take(fields, a, slice(row - halo, row - halo + 8))
    span = slice(row - halo - own, row - halo - own + 8)
    return jnp.where(odd, outer[a, span, :], inner[a, span, :])


def pack_kernel(*refs):
    fields, inner, outer, pack = refs[:4], refs[4], refs[5], refs[-1]
    half = fields[0].shape[1] // 2 + inner.shape[1]
    odd = (lax.axis_index("arc") & 1) > 0
    lane = lax.broadcasted_iota(jnp.int32, (8, LANES), 1) // (2 * EDGE)
    for r in range(0, half, 8):
        packed = jnp.zeros((8, LANES), jnp.float32)
        for part in range(2):
            for a in range(8):
                value = row_block(fields, inner, outer, odd, a, r + part * half)
                moved = pltpu.roll(value, (8 * a + EDGE + 64 * part) % LANES, 1)
                packed = jnp.where(lane == a + 8 * part, moved, packed)
        pack[r : r + 8, :] = packed


def ring_left(tiles, last):
    a, b = (pltpu.roll(t, LANES - 1, 1) for t in tiles)
    return jnp.where(last, b, a), jnp.where(last, a, b)


def ring_right(tiles, first):
    a, b = (pltpu.roll(t, 1, 1) for t in tiles)
    return jnp.where(first, b, a), jnp.where(first, a, b)


def unpack_block(pack, row, half, a, keep):
    upper = row >= half
    at = pl.multiple_of(jnp.where(upper, row - half, row), 8)
    shift = jnp.where(upper, (2 * LANES - 8 * a - EDGE - 64) % LANES, (2 * LANES - 8 * a - EDGE) % LANES)
    return jnp.where(keep, pltpu.roll(pack[pl.ds(at, 8), :], shift, 1), 0.0)


def clear_tail(state, rows):
    for a in range(3):
        for t in range(2):
            state[a, t, rows : rows + 8, :] = jnp.zeros((8, LANES), jnp.float32)


def load_state(group, source, pack, first_row, base, cycle_total, rows, half, state, vels, coef, ends=False):
    lane = lax.broadcasted_iota(jnp.int32, (8, LANES), 1)
    sub = lax.broadcasted_iota(jnp.int32, (8, LANES), 0)
    keep = (lane < EDGE) | (lane >= LANES - EDGE)
    first = lane == 0
    top = sub == 0

    def body(b, carry):
        r = 8 * b if isinstance(b, int) else pl.multiple_of(b * 8, 8)
        e = first_row + r
        span = pl.ds(r, 8)
        for a in range(3):
            state[a, 0, span, :] = source(a, r)
            state[a, 1, span, :] = unpack_block(pack, e, half, a, keep)
            vels[a, 0, span, :] = TIME_STEP * source(3 + a, r)
            vels[a, 1, span, :] = TIME_STEP * unpack_block(pack, e, half, 3 + a, keep)
        for t, m in enumerate((source(6, r), unpack_block(pack, e, half, 6, keep))):
            coef[0, t, span, :] = (TIME_STEP * TIME_STEP) / jnp.where(m > 0.0, m, 1.0)
        ids = base + e + sub
        inside = (ids >= 0) & (ids < cycle_total - 1)
        k = [
            jnp.where(inside, v, 0.0)
            for v in (source(7, r), unpack_block(pack, e, half, 7, keep))
        ]
        kr = ring_right(k, first)
        new = []
        for t in range(2):
            down = pltpu.roll(k[t], 1, 0)
            coef[1, t, span, :] = k[t]
            coef[2, t, span, :] = 0.5 * (k[t] + kr[t])
            coef[3, t, span, :] = (0.5 * HOOP_GAIN) * (k[t] + jnp.where(top, carry[t], down))
            new.append(down)
        return tuple(new)

    zero = jnp.zeros((8, LANES), jnp.float32)

    def several(b, carry):
        for u in range(group):
            carry = body(b * group + u + int(ends), carry)
        return carry

    carry = (zero, zero)
    if ends:
        carry = body(0, carry)
    carry = lax.fori_loop(0, (rows // 8 - 2 * int(ends)) // group, several, carry)
    if ends:
        body(rows // 8 - 1, carry)
    clear_tail(state, rows)


TABLE, AXIAL, HOOP_GAIN = column_table(2 * LANES)


def advance(table, rows, state, vels, coef, later, vels_later, group, push=None, span_of=None):
    lane = lax.broadcasted_iota(jnp.int32, (8, LANES), 1)
    top = lax.broadcasted_iota(jnp.int32, (8, LANES), 0) == 0
    first, last = lane == 0, lane == LANES - 1

    def const(i):
        return [jnp.broadcast_to(table[2 * i + t : 2 * i + t + 1, :], (8, LANES)) for t in range(2)]

    cj, sj, cb, sb = (const(i) for i in range(4))
    two = range(2)

    def block(r, carry, store=True):
        span, below = pl.ds(r, 8), pl.ds(r + 1, 8)
        x, y, z = ([state[a, t, span, :] for t in two] for a in range(3))
        xn, yn, zn = ([state[a, t, below, :] for t in two] for a in range(3))
        p = [cj[t] * y[t] + sj[t] * z[t] for t in two]
        q = [cb[t] * y[t] + sb[t] * z[t] for t in two]
        ax = [AXIAL * x[t] for t in two]
        pn = [cj[t] * yn[t] + sj[t] * zn[t] for t in two]
        qn = [cb[t] * yn[t] + sb[t] * zn[t] for t in two]
        axn = [AXIAL * xn[t] for t in two]
        q_next = ring_left(q, last)
        anti_next = ring_left([q[t] - ax[t] for t in two], last)
        diag_next = ring_left([qn[t] + axn[t] for t in two], last)
        k = [coef[1, t, span, :] for t in two]
        t_d = [k[t] * (diag_next[t] - (p[t] + ax[t])) for t in two]
        t_a = [k[t] * (anti_next[t] - (pn[t] - axn[t])) for t in two]
        t_h = [coef[3, t, span, :] * (q_next[t] - p[t]) for t in two]
        fx = [coef[2, t, span, :] * (xn[t] - x[t]) for t in two]
        d_left = ring_right(t_d, first)
        a_left = ring_right(t_a, first)
        g_left = ring_right([t_a[t] + t_h[t] for t in two], first)
        new = []
        for t in two:
            up = t_d[t] + t_h[t]
            force = [
                fx[t] + AXIAL * (t_d[t] + a_left[t]),
                cj[t] * up - cb[t] * g_left[t],
                sj[t] * up - sb[t] * g_left[t],
            ]
            low = [
                fx[t] + AXIAL * (d_left[t] + t_a[t]),
                cb[t] * d_left[t] - cj[t] * t_a[t],
                sb[t] * d_left[t] - sj[t] * t_a[t],
            ]
            at = (x[t], y[t], z[t])
            inverse = coef[0, t, span, :]
            for a in range(3):
                moved = pltpu.roll(low[a], 1, 0)
                total = force[a] - jnp.where(top, carry[3 * t + a], moved)
                new.append(moved)
                if not store:
                    continue
                if push is not None and a > 0:
                    total = total + push[a - 1, t, span, :]
                w = vels[a, t, span, :] + inverse * total
                if a == 2:
                    w = w - (GRAVITY * TIME_STEP * TIME_STEP)
                vels_later[a, t, span, :] = w
                later[a, t, span, :] = at[a] + w
        return tuple(new)

    def body(b, carry):
        for u in range(group):
            carry = block(pl.multiple_of(b * (8 * group), 8) + 8 * u, carry)
        return carry

    zero = jnp.zeros((8, LANES), jnp.float32)
    carry = (zero,) * 6
    begin, end = span_of or (0, rows)
    if begin > 0:
        carry = block(begin - 8, carry, store=False)
    if group * 8 == rows:
        for u in range(group):
            carry = block(8 * u, carry)
    else:
        lax.fori_loop(begin // (8 * group), end // (8 * group), body, carry)


def window_load_kernel(half, base, cycle_total, where_ref, *refs):
    fields, (inner, outer, columns, state, vels, coef) = refs[:4], refs[4:]
    start = pl.multiple_of(where_ref[0], 8)
    halo = inner.shape[1]
    own = fields[0].shape[1]
    odd = (lax.axis_index("arc") & 1) > 0

    def source(a, r):
        row = start + r
        mid = take(fields, a, pl.ds(pl.multiple_of(jnp.clip(row - halo, 0, own - 8), 8), 8))
        before = row < halo
        at = jnp.where(before, row, jnp.maximum(row - halo - own, 0))
        span = pl.ds(pl.multiple_of(at, 8), 8)
        end = jnp.where(odd == before, inner[a, span, :], outer[a, span, :])
        return jnp.where(before | (row >= halo + own), end, mid)

    first_id = base(lax.axis_index("arc"))
    load_state(4, source, columns, start, first_id, cycle_total, WIN, half, state, vels, coef)


def contact(table, lift, list_ref, step, state, push, taken, given, held):
    slots = held.shape[1]
    push[...] = jnp.zeros_like(push)
    for m in range(slots):
        g = list_ref[step, m]
        for a in range(2):
            for t in range(2):
                taken[a, t, m : m + 1, :] = state[a + 1, t, pl.ds(g, 1), :]
    for t in range(2):
        sin_angle, cos_angle = table[8 + t : 9 + t, :], table[10 + t : 11 + t, :]
        lateral = sin_angle + taken[0, t]
        q = held[t]
        intrusion = lift + CRADLE_CURVE * lateral * lateral - (1.0 - cos_angle) - taken[1, t] - q
        load = CONTACT_STIFF * jnp.maximum(intrusion, 0.0)
        normal = load / jnp.sqrt(1.0 + 4.0 * CRADLE_CURVE * CRADLE_CURVE * lateral * lateral)
        given[0, t] = -2.0 * CRADLE_CURVE * lateral * normal
        given[1, t] = normal
        held[t] = q + PAD_RATE * (load - PAD_STIFF * q)
    for m in range(slots):
        g = list_ref[step, m]
        for a in range(2):
            for t in range(2):
                push[a, t, pl.ds(g, 1), :] += given[a, t, m : m + 1, :]


def window_kernel(
    list_ref, lift_ref, plan, table, state, vels, coef, kept, near, far, cross, *rest
):
    state_out, vels_out, push, pad_out, spare, vels_spare, taken, given, held = rest[-9:]
    same = plan[SAME_X : SAME_X + 1, :] > 0
    held[0] = jnp.where(same, kept[0], near[0])
    held[1] = jnp.where(same, far[0], cross[0])
    lift = lift_ref[0]
    clear_tail(spare, WIN)
    clear_tail(state_out, WIN)
    now = (state, vels)
    for step in range(STEPS):
        contact(table, lift, list_ref, step, now[0], push, taken, given, held)
        if step < STEPS - 1:
            later = (spare, vels_spare) if (STEPS - step) % 2 else (state_out, vels_out)
            advance(table, WIN, *now, coef, *later, WIN // 8, push)
            now = later
    pad_out[0] = held[0]


def window_last_kernel(table, state, vels, coef, push, result, later, vels_later):
    advance(table, WIN, state, vels, coef, later, vels_later, WIN // 8, push)
    for a in range(3):
        result[a] = later[a, 0, :WIN, :]
        result[3 + a] = vels_later[a, 0] * (1.0 / TIME_STEP)


def bulk_load_kernel(half, base, cycle_total, rows, *refs):
    fields, (inner, outer, columns), (state, vels, coef) = refs[:4], refs[4:7], refs[-3:]
    first_row = HALO - 8
    odd = (lax.axis_index("arc") & 1) > 0

    def source(a, r):
        if isinstance(r, int):
            return row_block(fields, inner, outer, odd, a, first_row + r)
        return take(fields, a, pl.ds(pl.multiple_of(r - 8, 8), 8))

    first_id = base(lax.axis_index("arc"))
    load_state(
        LOAD_GROUP, source, columns, first_row, first_id, cycle_total, rows, half, state, vels, coef, ends=True
    )


def bulk_step_kernel(rows, part, table, state, vels, coef, *rest):
    later, vels_later = rest[-2:]
    third = rows // PARTS
    advance(table, rows, state, vels, coef, later, vels_later, GROUP, span_of=(part * third, (part + 1) * third))
    if part == 0:
        clear_tail(later, rows)


def bulk_store_kernel(rows, where_ref, state, vels, window, *rest):
    disp_out, vel_out, token, result, sems = rest[-5:]
    token[...] = jnp.zeros_like(token)
    count = (rows - 16) // CHUNKS
    start = where_ref[1]
    sub = lax.broadcasted_iota(jnp.int32, (8, LANES), 0)

    def body(b, carry):
        r = pl.multiple_of(b * 8, 8)
        inner = pl.ds(pl.multiple_of(r + 8, 8), 8)
        rel = HALO + r - start
        at = pl.ds(pl.multiple_of(jnp.clip(rel, 0, WIN - 8), 8), 8)
        ids = rel + sub
        use = (ids >= STEPS) & (ids < WIN - STEPS)
        for a in range(3):
            result[a, pl.ds(r, 8), :] = jnp.where(use, window[a, at, :], state[a, 0, inner, :])
            result[3 + a, pl.ds(r, 8), :] = jnp.where(
                use, window[3 + a, at, :], vels[a, 0, inner, :] * (1.0 / TIME_STEP)
            )
        return carry

    copies = []
    for chunk in range(CHUNKS):
        lax.fori_loop(chunk * count // 8, (chunk + 1) * count // 8, body, 0)
        span = pl.ds(chunk * count, count)
        for n, out in enumerate((disp_out, vel_out)):
            copy = pltpu.make_async_copy(
                result.at[3 * n : 3 * n + 3, span, :], out.at[:, span, :], sems.at[2 * chunk + n]
            )
            copy.start()
            copies.append(copy)
    for copy in copies:
        copy.wait()


def stack_kernel(first, second, *rest):
    count = first.shape[0]
    rest[-1][:count] = first[...]
    rest[-1][count:] = second[...]


def pick_kernel(way, plan, first, second, *rest):
    keep, send = rest[-2:]
    parts = [ref[n] for ref in (first, second) for n in range(4)]
    for out, row in ((keep, KEEP), (send, SEND)):
        for n in range(4):
            at = PLAN * way + row + n
            index = plan[at : at + 1, :]
            value = parts[0]
            for m in range(1, 8):
                value = jnp.where(index == m, parts[m], value)
            out[n] = value


def choose_kernel(way, row, plan, kept, got, *rest):
    keep, send = rest[-2:]
    count = got.shape[0]
    for n in range(count):
        at = PLAN * way + row + n
        value = jnp.where(plan[at : at + 1, :] > 0, got[n], kept[n])
        if n < count // 2:
            keep[n] = value
        else:
            send[n - count // 2] = value


def last_kernel(plan, mine, handed, before, *rest):
    out = rest[-1]
    used = plan[PLAN + USED : PLAN + USED + 1, :] > 0
    same = plan[PLAN + SAME_X : PLAN + SAME_X + 1, :] > 0
    out[0] = jnp.where(used, jnp.where(same, mine[0], handed[0]), before[0])


VMEM = pl.BlockSpec(memory_space=pltpu.VMEM)
SMEM = pl.BlockSpec(memory_space=pltpu.SMEM)
ANY = pl.BlockSpec(memory_space=pl.ANY)
HBM = pl.BlockSpec(memory_space=pltpu.HBM)


def real(*shape):
    return jax.ShapeDtypeStruct(shape, jnp.float32)


def whole(*shape):
    return jax.ShapeDtypeStruct(shape, jnp.int32)


def call(kernel, name, outs, ins, in_specs=None, out_specs=None, scratch=(), micros=0.1, after=(), limit=LIMIT, aliases=()):
    single = not isinstance(outs, tuple)
    shapes = (outs,) if single else outs
    result = pl.pallas_call(
        kernel,
        out_shape=shapes,
        in_specs=list(in_specs or [VMEM] * len(ins)) + [ANY] * len(after),
        out_specs=tuple(out_specs or [VMEM] * len(shapes)),
        scratch_shapes=list(scratch),
        compiler_params=pltpu.CompilerParams(vmem_limit_bytes=limit),
        cost_estimate=pl.CostEstimate(flops=0, bytes_accessed=int(micros * 3.6e6), transcendentals=0),
        input_output_aliases=dict(aliases),
        name=name,
    )(*ins, *after)
    return result[0] if single else result


def route(value, kept, way, between):
    shape = value.shape[1:]
    got = lax.ppermute(value, "arc", flips(c=1))
    held = call(stack_kernel, "stack", real(2, *shape), (value, got), after=between(0, value))
    got = lax.ppermute(held, "arc", flips(y=1))
    held = call(stack_kernel, "stack", real(4, *shape), (held, got), after=between(1, held))
    got = lax.ppermute(held, "arc", flips(y=3))
    ready = between(2, held)
    plan = kept["plan"][0]
    keep, send = call(
        functools.partial(pick_kernel, way), "pick", (real(4, *shape),) * 2, (plan, held, got), after=ready
    )
    got = lax.ppermute(send, "arc", flips(z=1))
    keep, send = call(
        functools.partial(choose_kernel, way, FROM_Z), "choose", (real(2, *shape),) * 2, (plan, keep, got),
        after=between(3, send),
    )
    got = lax.ppermute(send, "arc", flips(z=3))
    keep, send = call(
        functools.partial(choose_kernel, way, FAR_Z), "choose", (real(1, *shape),) * 2, (plan, keep, got),
        after=between(4, send),
    )
    return keep, lax.ppermute(send, "arc", flips(x=1)), between(5, send), send


def static_tables(arc_count, cycle_dev, roller_total):
    cycle_total = arc_count * cycle_dev
    centres = [r * (cycle_total - 1) // (roller_total - 1) for r in range(roller_total)]
    span = REACH + STEPS - 1
    near = np.full(arc_count, -1, np.int32)
    start = np.zeros(arc_count, np.int32)
    for d in range(arc_count):
        base = d * cycle_dev
        touching = [r for r, c in enumerate(centres) if base - span <= c < base + cycle_dev + span]
        assert len(touching) <= 1
        if touching:
            near[d] = touching[0]
            offset = centres[touching[0]] - base - REACH - STEPS - STEPS + 1 + HALO
            start[d] = offset // 8 * 8
            assert 0 <= start[d] <= cycle_dev + 2 * HALO - WIN
    home = np.array([c // cycle_dev for c in centres], np.int32)
    return near, start, home


def local(displacement, velocity, node_mass, wall_stiff, pad_state, roller_lift, contact_rows, roller_slot):
    cycle_dev = displacement.shape[1]
    slots = pad_state.shape[1]
    roller_total = roller_lift.shape[0]
    arc_count = lax.axis_size("arc")
    cycle_total = cycle_dev * arc_count
    half = cycle_dev // 2 + HALO
    rows = cycle_dev + 16
    fields = (displacement, velocity, node_mass, wall_stiff)
    static = np.concatenate(static_tables(arc_count, cycle_dev, roller_total)).astype(np.int32)
    swap = [(0, 1), (1, 0)]
    table = jnp.asarray(TABLE)[lax.axis_index("circ")]

    def base(me):
        return me * cycle_dev - HALO

    def buffers(count):
        return real(3, 2, count + 8, LANES), real(3, 2, count, LANES), real(4, 2, count, LANES)

    def room(count):
        return [pltpu.VMEM(shape.shape, jnp.float32) for shape in buffers(count)[:2]]

    outward = [pair for i in range(1, arc_count, 2) for pair in ((i, (i + 1) % arc_count), ((i + 1) % arc_count, i))]

    inner, outer = call(
        functools.partial(edge_kernel, HALO), "edge", (real(8, HALO, LANES), real(8, HALO, LANES)), fields,
        in_specs=[HBM] * 4, scratch=[pltpu.SemaphoreType.DMA((8,))], micros=2.0, limit=MOST,
    )
    ends = lax.ppermute(inner, "arc", flips(c=1)), lax.ppermute(outer, "arc", outward)

    def make_plan(value):
        kept["plan"] = call(
            functools.partial(plan_kernel, arc_count, cycle_dev), "plan",
            (whole(2 * PLAN, LANES), whole(2), whole(STEPS, slots), real(1)),
            (roller_slot, roller_lift, contact_rows, jnp.asarray(static)),
            in_specs=[SMEM, SMEM, VMEM, SMEM], out_specs=[VMEM, SMEM, VMEM, SMEM],
            scratch=[pltpu.SMEM((arc_count,), jnp.int32)], micros=1.5, after=(value,),
        )
        return kept["plan"][:1]

    kept = {"done": 0}

    def load_window():
        return call(
            functools.partial(window_load_kernel, half, base, cycle_total), "window_load", buffers(WIN),
            (kept["plan"][1], *fields, *ends, kept["columns"]), in_specs=[SMEM] + [VMEM] * 7, micros=0.8,
        )

    def load_bulk(value):
        return call(
            functools.partial(bulk_load_kernel, half, base, cycle_total, rows), "bulk_load", buffers(rows),
            (*fields, *ends, kept["columns"]), micros=2.0, after=(value,),
        )

    def step_bulk(value, count):
        for _ in range(count):
            step, part = divmod(kept["done"], PARTS)
            state, vels, coef = kept["bulk"]
            before = kept["next"] if part else ()
            kept["next"] = call(
                functools.partial(bulk_step_kernel, rows, part), "bulk_step", buffers(rows)[:2],
                (table, state, vels, coef, *before), micros=2.4 / PARTS, after=(value,),
                aliases={4: 0, 5: 1} if part else {},
            )
            kept["done"] += 1
            if part == PARTS - 1:
                kept["bulk"] = (*kept["next"], coef)
        return kept["next"][:1]

    def store_bulk(value):
        state, vels, _ = kept["bulk"]
        outs = call(
            functools.partial(bulk_store_kernel, rows), "bulk_store",
            (real(3, cycle_dev, LANES), real(3, cycle_dev, LANES), real(8, LANES)),
            (kept["plan"][1], state, vels, kept["last"], value),
            in_specs=[SMEM] + [VMEM] * 3 + [ANY], out_specs=[HBM] * 2 + [VMEM],
            scratch=[pltpu.VMEM((6, cycle_dev, LANES), jnp.float32), pltpu.SemaphoreType.DMA((2 * CHUNKS,))],
            micros=2.0,
        )
        kept["outs"] = outs[:2]
        return outs[2:]

    def going(stage, value):
        if stage == 1:
            return make_plan(value)
        if stage == 2:
            pack = call(pack_kernel, "pack", real(half, LANES), (*fields, *ends), micros=2.0, after=(value,))
            kept["columns"] = lax.ppermute(pack, "circ", swap)
            return (pack,)
        if stage == 5:
            kept["window"] = load_window()
            return kept["window"][:1]
        return ()

    mine, near, done, sent = route(pad_state, kept, 0, going)
    double = [(2 * s + h, 2 * d + 1 - h) for s, d in flips(x=1) for h in range(2)]
    far = lax.ppermute(mine, "circ", swap)
    cross = lax.ppermute(sent, ("arc", "circ"), double)

    plan, _, rows_in, lift = kept["plan"]
    win_state, win_vels, win_coef = kept["window"]
    win_state, win_vels, push, pad_new = call(
        window_kernel, "window", (*buffers(WIN)[:2], real(2, 2, WIN, LANES), real(1, slots, LANES)),
        (rows_in, lift, plan, table, win_state, win_vels, win_coef, mine, near, far, cross),
        after=done,
        in_specs=[SMEM] * 2 + [VMEM] * 9,
        scratch=room(WIN)
        + [
            pltpu.VMEM((2, 2, slots, LANES), jnp.float32),
            pltpu.VMEM((2, 2, slots, LANES), jnp.float32),
            pltpu.VMEM((2, slots, LANES), jnp.float32),
        ],
        micros=2.0,
    )

    def coming(stage, value):
        if stage == 0:
            kept["last"] = call(
                window_last_kernel, "window_last", real(6, WIN, LANES), (table, win_state, win_vels, win_coef, push),
                scratch=room(WIN), micros=0.6,
            )
            return (kept["last"],)
        if stage == 1:
            kept["bulk"] = load_bulk(value)
            return kept["bulk"][:1]
        return store_bulk(value) if stage == 5 else step_bulk(value, 4)

    pads, handed, done, _ = route(pad_new, kept, 1, coming)
    pad_result = call(last_kernel, "last", real(1, slots, LANES), (plan, pads, handed, pad_state), after=done)
    return *kept["outs"], pad_result


def solution(mesh):
    placed = (
        P(None, "arc", "circ"),
        P(None, "arc", "circ"),
        P("arc", "circ"),
        P("arc", "circ"),
        P("arc", None, "circ"),
        P(),
        P(),
        P(),
    )
    return jax.shard_map(
        local,
        mesh=mesh,
        in_specs=placed,
        out_specs=(P(None, "arc", "circ"), P(None, "arc", "circ"), P("arc", None, "circ")),
        check_vma=False,
    )
```
